32 devices in a mesh: rep: 2 (over core), fsdp: 16 (over z, y, x).
Axes of the slice: x: 2, y: 2, z: 4, core: 2. Of those that a mesh axis runs over, the one named last changes fastest.
Arguments:
- acts: bfloat16 [2, 2048, 8192], P('rep', 'fsdp'), may hold values from -6 to 6
- value_cots: bfloat16 [2, 2048, 512], P('rep', 'fsdp'), may hold values from -0.059814453 to 0.059814453
- inner_weights: float32 [2, 8192, 512], P('rep', 'fsdp'), may hold values from -0.0625 to 0.0625
- first_moment: float32 [2, 8192, 512], P('rep', 'fsdp'), may hold values from -1.8 to 1.8
- second_moment: float32 [2, 8192, 512], P('rep', 'fsdp'), may hold values from 0.01 to 1
- anchor: float32 [8192, 512], P('fsdp'), may hold values from -0.0625 to 0.0625
- outer_momentum: float32 [8192, 512], P('fsdp'), may hold values from -0.06 to 0.06
Outputs:
- first_next: float32 [2, 8192, 512], P('rep', 'fsdp')
- values_next: bfloat16 [2, 2048, 512], P('rep', 'fsdp')
The draws below stay inside these ranges and needn't reach their ends.
All inputs are finite; a program needn't handle non-finite values.
Results may differ from the reference program's by a relative error of at most 0.0049.
Values may be sent and summed in bfloat16 or wider, within the bound.
No kernel may reach another device: no remote copies, remote signals or barrier semaphores. Data moves between devices by JAX's collectives and lax.ppermute only.
A program may use at most 64 MiB of HBM per device.

```python
import math
from functools import partial
import jax
import jax.numpy as jnp
from jax import lax

D = 8192
C = 512
TOKENS = 2048
N_REP = 2


def strengthened(result, rng, source, target, parts, factor):
    def block_of(dim):
        return (jnp.arange(result.shape[dim]) // (result.shape[dim] // parts)).reshape((-1,) + (1,) * (result.ndim - 1 - dim))

    first = jax.random.permutation(rng, parts)[block_of(target)]
    far = (block_of(target) + parts // 2) % parts
    return jnp.where((block_of(source) == first) | (block_of(source) == far), factor * result, result)


def block_levels(key, dims, pieces, least, top_value):
    def one(axis_at, shards_of):
        steps = jax.random.uniform(jax.random.fold_in(jax.random.fold_in(key, 6), axis_at), (shards_of,), jnp.float32, least / len(pieces), top_value / len(pieces))
        return jnp.repeat(jnp.exp(steps), dims[axis_at] // shards_of).reshape((-1,) + (1,) * (len(dims) - axis_at - 1))

    level = one(*pieces[0])
    for cut in pieces[1:]:
        level = level * one(*cut)
    return level


def normal_values(own_key, dims, scale, limit, split=(), kind=jnp.bfloat16):
    level = block_levels(own_key, dims, split, -0.22, 0.18) if split else 1.0
    drawn = jax.random.normal(own_key, dims, jnp.float32) * scale * level
    return jnp.minimum(jnp.maximum(drawn, -limit), limit).astype(kind)


def gaussian_with(rng, shape, deviation, bound, cuts, heavy, held_as=jnp.bfloat16):
    array = deviation * jax.random.normal(rng, shape, jnp.float32)
    if cuts:
        array = array * block_levels(rng, shape, cuts, -0.22, 0.18)
    return jnp.clip(strengthened(array, jax.random.fold_in(rng, 3), *heavy), -bound, bound).astype(held_as)


def setup_inputs(seed: int = 0) -> dict:
    key_of = jax.random.split(jax.random.key(seed), 8)
    acts = gaussian_with(key_of[0], (N_REP, TOKENS, D), 1.0, 6.0, ((0, 2), (1, 16)), (1, 2, 16, 2.0))
    value_cots = normal_values(key_of[1], (N_REP, TOKENS, C), 0.01, 0.059814453, ((0, 2), (1, 16)))
    inner_weights = normal_values(key_of[2], (N_REP, D, C), D ** -0.5, 0.0625, ((0, 2), (1, 16)), jnp.float32)
    first_moment = normal_values(key_of[3], (N_REP, D, C), 0.3, 1.8, ((0, 2), (1, 16)), jnp.float32)
    second_moment = jnp.clip(jnp.exp(math.log(1.0) - 4.6051702 * jax.random.uniform(key_of[4], (N_REP, D, C), jnp.float32) ** block_levels(key_of[4], (N_REP, D, C), ((0, 2), (1, 16)), -0.2, 0.2)), 0.01, 1.0)
    anchor = normal_values(key_of[5], (D, C), D ** -0.5, 0.0625, ((0, 16),), jnp.float32)
    outer_momentum = normal_values(key_of[6], (D, C), 0.01, 0.06, ((0, 16),), jnp.float32)
    return {"acts": acts, "value_cots": value_cots, "inner_weights": inner_weights, "first_moment": first_moment, "second_moment": second_moment, "anchor": anchor, "outer_momentum": outer_momentum}


decay_first = 0.9
decay_second = 0.95
inner_rate = 0.006
epsilon = 1e-08
outer_rate = 0.7
outer_decay = 0.9

def replica_step(anchor, packed):
    tokens, cots, weights, first, second = packed
    gradient = lax.dot_general(tokens, cots, (((0,), (0,)), ((), ())), preferred_element_type=jnp.float32)
    first_next = decay_first * first + (1.0 - decay_first) * gradient
    second_next = decay_second * second + (1.0 - decay_second) * gradient * gradient
    stepped = weights - inner_rate * first_next / (jnp.sqrt(second_next) + epsilon)
    return (first_next, anchor - stepped)

def forward_rows(weights_next, tokens):
    return jnp.dot(tokens, weights_next, preferred_element_type=jnp.float32).astype(jnp.bfloat16)

def reference(acts, value_cots, inner_weights, first_moment, second_moment, anchor, outer_momentum):
    firsts, drifts = lax.map(partial(replica_step, anchor), (acts, value_cots, inner_weights, first_moment, second_moment))
    drift = lax.optimization_barrier(jnp.sum(drifts, axis=0)) / N_REP
    velocity = outer_decay * outer_momentum + drift
    weights_next = (anchor - outer_rate * (drift + outer_decay * velocity)).astype(jnp.bfloat16)
    values_next = lax.map(partial(forward_rows, weights_next), acts)
    return (firsts, values_next)
```

```python
from functools import partial

import jax
import jax.numpy as jnp
from jax import lax
from jax.experimental import pallas as pl
from jax.experimental.pallas import tpu as pltpu
from jax.sharding import PartitionSpec as P

decay_first = 0.9
decay_second = 0.95
inner_rate = 0.006
epsilon = 1e-08
outer_rate = 0.7
outer_decay = 0.9

PLANES = 4
CONTRACT_ROWS = (((0,), (0,)), ((), ()))
VMEM_BYTES = 40 * 1024 * 1024


def outer_update(average, anchor_rows, momentum_rows):
    velocity = outer_decay * momentum_rows + average
    return (anchor_rows - outer_rate * (average + outer_decay * velocity)).astype(jnp.bfloat16)


def inner_update(gradient, inner_weights, first_moment, second_moment, anchor):
    first_next = decay_first * first_moment + (1.0 - decay_first) * gradient
    second_next = decay_second * second_moment + (1.0 - decay_second) * gradient * gradient
    stepped = inner_weights - inner_rate * first_next / (jnp.sqrt(second_next) + epsilon)
    return first_next, anchor - stepped


def general(acts, value_cots, inner_weights, first_moment, second_moment, anchor, outer_momentum):
    tokens_local = acts[0]
    columns = lax.all_to_all(tokens_local, "fsdp", split_axis=1, concat_axis=0, tiled=True)
    cots = lax.all_gather(value_cots[0], "fsdp", axis=0, tiled=True)
    gradient = lax.dot_general(columns, cots, CONTRACT_ROWS, preferred_element_type=jnp.float32)
    first_next, drift = inner_update(gradient, inner_weights[0], first_moment[0], second_moment[0], anchor)
    average = lax.psum(drift, "rep") / lax.axis_size("rep")
    weights_next = outer_update(average, anchor, outer_momentum)
    gathered = lax.all_gather(weights_next, "fsdp", axis=0, tiled=True)
    values = jnp.dot(tokens_local, gathered, preferred_element_type=jnp.float32)
    return (first_next[None], values.astype(jnp.bfloat16)[None])


def repack_kernel(inner, rows, acts_ref, cots_ref, *refs):
    firsts, rests, sems = refs[:inner], refs[inner : 2 * inner], refs[-1]
    tokens = acts_ref.shape[0]
    f = lax.axis_index("fsdp")
    o, i = f // inner, lax.rem(f, inner)
    copies = []
    for k in range(inner):
        place = (i // 2 + k // 2 - 2 * (i // 2) * (k // 2)) * 2 + (lax.rem(i, 2) + k % 2 - 2 * lax.rem(i, 2) * (k % 2))
        for slot, t in enumerate((3, 2, 1, 0)):
            plane = jnp.where(o < PLANES // 2, t, PLANES - 1 - t)
            start = pl.multiple_of((plane * inner + place) * rows, rows)
            to = firsts[k].at[pl.ds(0, tokens)] if slot == 0 else rests[k].at[pl.ds((slot - 1) * tokens, tokens)]
            copies.append(pltpu.make_async_copy(acts_ref.at[:, pl.ds(start, rows)], to, sems.at[len(copies)]))
        copies.append(pltpu.make_async_copy(cots_ref, firsts[k].at[pl.ds(tokens, tokens)], sems.at[len(copies)]))
    for copy in copies:
        copy.start()
    for copy in copies:
        copy.wait()


def repack(tokens_local, cots_local, inner, rows):
    tokens, _ = tokens_local.shape
    out = [jax.ShapeDtypeStruct((2 * tokens, rows), jnp.bfloat16)] * inner
    out += [jax.ShapeDtypeStruct((3 * tokens, rows), jnp.bfloat16)] * inner
    got = pl.pallas_call(
        partial(repack_kernel, inner, rows),
        out_shape=out,
        in_specs=[pl.BlockSpec(memory_space=pl.ANY)] * 2,
        out_specs=[pl.BlockSpec(memory_space=pl.ANY)] * (2 * inner),
        scratch_shapes=[pltpu.SemaphoreType.DMA((5 * inner,))],
        name="repack",
    )(tokens_local, cots_local)
    return got[:inner], got[inner:]


def first_partial_kernel(inner, tokens, *refs):
    firsts, total_ref, sent_ref = refs[:inner], refs[inner], refs[inner + 1]
    columns = jnp.concatenate([ref[:tokens] for ref in firsts], axis=0)
    cots = jnp.concatenate([ref[tokens:] for ref in firsts], axis=0)
    total = lax.dot_general(columns, cots, CONTRACT_ROWS, preferred_element_type=jnp.float32)
    total_ref[...] = total
    sent_ref[...] = total.astype(jnp.bfloat16)


def rest_partial_kernel(inner, tokens, *refs):
    firsts, rests, outs = refs[:inner], refs[inner : 2 * inner], refs[2 * inner :]
    cots = jnp.concatenate([ref[tokens:] for ref in firsts], axis=0)
    for slot in range(3):
        columns = jnp.concatenate([ref[slot * tokens : (slot + 1) * tokens] for ref in rests], axis=0)
        total = lax.dot_general(columns, cots, CONTRACT_ROWS, preferred_element_type=jnp.float32)
        outs[slot][...] = total
        if slot < 2:
            outs[3 + slot][...] = total.astype(jnp.bfloat16)


def values_kernel(inner, tokens, rows, *refs):
    firsts, rests = refs[:inner], refs[inner : 2 * inner]
    mine_ref, other_ref, mine2_ref, other2_ref, mine3_ref, other3_ref = refs[2 * inner : 2 * inner + 6]
    own_ref, sent_refs, weights = refs[2 * inner + 6], refs[2 * inner + 7 : -1], refs[-1]
    half = rows // 2
    o, r = lax.axis_index("fsdp") // inner, lax.axis_index("rep")
    near = jnp.where(o < PLANES // 2, o, PLANES - 1 - o)

    def put(t, which, value):
        weights[pl.ds(pl.multiple_of(t * rows + which * half, half), half), :] = value

    for slot, t in ((0, near), (1, 1 - near)):
        put(t, r, mine_ref[slot])
        put(t, 1 - r, other_ref[slot])
    put(2, r, mine2_ref[...])
    put(2, 1 - r, other2_ref[...])
    put(3, r, mine3_ref[...])
    put(3, 1 - r, other3_ref[...])
    for k in range(inner):
        total = jnp.dot(firsts[k][:tokens], weights[3 * rows :], preferred_element_type=jnp.float32)
        for slot, t in enumerate((2, 1, 0)):
            total += jnp.dot(
                rests[k][slot * tokens : (slot + 1) * tokens],
                weights[t * rows : (t + 1) * rows],
                preferred_element_type=jnp.float32,
            )
        if k == 0:
            own_ref[...] = total
        else:
            sent_refs[k - 1][...] = total.astype(jnp.bfloat16)


def call(kernel, name, out, inputs, flops, scratch=()):
    moved = sum(x.size * x.dtype.itemsize for x in list(inputs) + list(out))
    return pl.pallas_call(
        kernel,
        out_shape=out,
        in_specs=[pl.BlockSpec(memory_space=pltpu.VMEM)] * len(inputs),
        out_specs=[pl.BlockSpec(memory_space=pltpu.VMEM)] * len(out),
        scratch_shapes=list(scratch),
        compiler_params=pltpu.CompilerParams(vmem_limit_bytes=VMEM_BYTES),
        cost_estimate=pl.CostEstimate(flops=flops, bytes_accessed=moved, transcendentals=0),
        name=name,
    )(*inputs)


def on_device(acts, value_cots, inner_weights, first_moment, second_moment, anchor, outer_momentum):
    inner = lax.axis_size("fsdp") // PLANES
    rows, width = anchor.shape
    if inner != 4 or lax.axis_size("rep") != 2 or rows % 256:
        return general(acts, value_cots, inner_weights, first_moment, second_moment, anchor, outer_momentum)
    tokens = acts.shape[1]
    half = rows // 2
    o = lax.axis_index("fsdp") // inner
    r = lax.axis_index("rep")
    near = jnp.where(o < PLANES // 2, o, PLANES - 1 - o)
    at_end = near == 0

    def line(x, *pairs):
        return lax.ppermute(x, "fsdp", [(a * inner + i, b * inner + i) for a, b in pairs for i in range(inner)])

    def across(x, k):
        return lax.ppermute(x, "fsdp", [(p * inner + i, p * inner + (i ^ k)) for p in range(PLANES) for i in range(inner)])

    def swap(x):
        return lax.ppermute(x, "rep", [(0, 1), (1, 0)])

    def inward(x):
        return line(x, (0, 1), (3, 2))

    def middle(x):
        return line(x, (1, 2), (2, 1))

    def outward(x):
        return line(x, (1, 0), (2, 3))

    firsts, rests = repack(acts[0], value_cots[0], inner, rows)
    firsts = [firsts[0]] + [across(firsts[k], k) for k in range(1, inner)]
    rests = [rests[0]] + [across(rests[k], k) for k in range(1, inner)]

    f32 = jax.ShapeDtypeStruct((rows, width), jnp.float32)
    bf16 = jax.ShapeDtypeStruct((rows, width), jnp.bfloat16)
    flops = 2 * inner * tokens * rows * width
    total3, sent3 = call(partial(first_partial_kernel, inner, tokens), "partial_first", [f32, bf16], firsts, flops)
    a1 = inward(sent3)
    total2, total1, total0, sent2, sent1 = call(
        partial(rest_partial_kernel, inner, tokens), "partial_rest", [f32, f32, f32, bf16, bf16], firsts + rests, 3 * flops
    )
    a2 = inward(sent2)
    a3 = inward(sent1)

    def add(total, got):
        return (total + got.astype(jnp.float32)).astype(jnp.bfloat16)

    b2 = middle(add(total3, a1))
    b3 = middle(add(total2, a2))
    c3 = outward(add(total0, b2))
    own = jnp.where(at_end, total0 + c3.astype(jnp.float32), total1 + a3.astype(jnp.float32) + b3.astype(jnp.float32))
    first_next, drift = inner_update(own, inner_weights[0], first_moment[0], second_moment[0], anchor)

    def half_of(x, which):
        return lax.dynamic_slice_in_dim(x, which * half, half, 0)

    summed = half_of(drift, r) + swap(half_of(drift, 1 - r))
    mine = outer_update(summed / 2, half_of(anchor, r), half_of(outer_momentum, r))
    beside = line(mine, (0, 1), (1, 0), (2, 3), (3, 2))
    far2 = middle(mine)
    far3 = middle(beside)
    mine2 = jnp.where(at_end, outward(far2), far2)
    mine3 = jnp.where(at_end, outward(far3), far3)
    mine = jnp.stack([mine, beside])
    pieces = [mine, swap(mine), mine2, swap(mine2), mine3, swap(mine3)]
    block = jax.ShapeDtypeStruct((tokens, width), jnp.bfloat16)
    values, *sent = call(
        partial(values_kernel, inner, tokens, rows),
        "values",
        [jax.ShapeDtypeStruct((tokens, width), jnp.float32)] + [block] * (inner - 1),
        firsts + rests + pieces,
        4 * flops,
        [pltpu.VMEM((PLANES * rows, width), jnp.bfloat16)],
    )
    for k in range(1, inner):
        values = values + across(sent[k - 1], k).astype(jnp.float32)
    return (first_next[None], values.astype(jnp.bfloat16)[None])


def solution(mesh):
    placed = (
        P("rep", "fsdp", None),
        P("rep", "fsdp", None),
        P("rep", "fsdp", None),
        P("rep", "fsdp", None),
        P("rep", "fsdp", None),
        P("fsdp", None),
        P("fsdp", None),
    )
    return jax.shard_map(
        on_device,
        mesh=mesh,
        in_specs=placed,
        out_specs=(P("rep", "fsdp", None), P("rep", "fsdp", None)),
        check_vma=False,
    )
```

```python
from functools import partial

import jax
import jax.numpy as jnp
from jax import lax
from jax.experimental import pallas as pl
from jax.experimental.pallas import tpu as pltpu
from jax.sharding import PartitionSpec as P

decay_first = 0.9
decay_second = 0.95
inner_rate = 0.006
epsilon = 1e-08
outer_rate = 0.7
outer_decay = 0.9

PLANES = 4
CONTRACT_ROWS = (((0,), (0,)), ((), ()))
VMEM_BYTES = 16 * 1024 * 1024


def outer_update(average, anchor_rows, momentum_rows):
    velocity = outer_decay * momentum_rows + average
    return (anchor_rows - outer_rate * (average + outer_decay * velocity)).astype(jnp.bfloat16)


def inner_update(gradient, inner_weights, first_moment, second_moment, anchor):
    first_next = decay_first * first_moment + (1.0 - decay_first) * gradient
    second_next = decay_second * second_moment + (1.0 - decay_second) * gradient * gradient
    stepped = inner_weights - inner_rate * first_next / (jnp.sqrt(second_next) + epsilon)
    return first_next, anchor - stepped


def general(acts, value_cots, inner_weights, first_moment, second_moment, anchor, outer_momentum):
    tokens_local = acts[0]
    columns = lax.all_to_all(tokens_local, "fsdp", split_axis=1, concat_axis=0, tiled=True)
    cots = lax.all_gather(value_cots[0], "fsdp", axis=0, tiled=True)
    gradient = lax.dot_general(columns, cots, CONTRACT_ROWS, preferred_element_type=jnp.float32)
    first_next, drift = inner_update(gradient, inner_weights[0], first_moment[0], second_moment[0], anchor)
    average = lax.psum(drift, "rep") / lax.axis_size("rep")
    weights_next = outer_update(average, anchor, outer_momentum)
    gathered = lax.all_gather(weights_next, "fsdp", axis=0, tiled=True)
    values = jnp.dot(tokens_local, gathered, preferred_element_type=jnp.float32)
    return (first_next[None], values.astype(jnp.bfloat16)[None])


def mirrored():
    planes_at = lax.axis_size("fsdp") // PLANES
    f = lax.axis_index("fsdp")
    o = f // planes_at
    return o, lax.rem(f, planes_at), jnp.where(o < PLANES // 2, o, PLANES - 1 - o)


def repack_kernel(inner, targets, *refs):
    acts_ref, cots, outs = refs[0], refs[1 : len(refs) - inner], refs[len(refs) - inner :]
    tokens, rows = acts_ref.shape[0], outs[0].shape[1]
    o, i, _ = mirrored()
    for k in range(inner):
        x, y = lax.rem(i, 2), i // 2
        place = (y + k // 2 - 2 * y * (k // 2)) * 2 + x + k % 2 - 2 * x * (k % 2)
        for slot, t in enumerate(targets):
            plane = jnp.where(o < PLANES // 2, t, PLANES - 1 - t)
            start = pl.multiple_of((plane * inner + place) * rows, rows)
            outs[k][slot * tokens : (slot + 1) * tokens] = acts_ref[:, pl.ds(start, rows)]
        for cots_ref in cots:
            outs[k][len(targets) * tokens :] = cots_ref[...]


def repack(inputs, inner, targets, rows):
    tokens = inputs[0].shape[0]
    out = [jax.ShapeDtypeStruct(((len(targets) + len(inputs) - 1) * tokens, rows), jnp.bfloat16)] * inner
    return call(partial(repack_kernel, inner, targets), "repack", out, inputs, 0)


def partial_kernel(inner, tokens, slots, *refs):
    firsts, blocks, outs = refs[:inner], refs[inner : 2 * inner], refs[2 * inner :]
    cots = jnp.concatenate([ref[tokens:] for ref in firsts], axis=0)
    for slot in range(slots):
        columns = jnp.concatenate([ref[slot * tokens : (slot + 1) * tokens] for ref in blocks], axis=0)
        total = lax.dot_general(columns, cots, CONTRACT_ROWS, preferred_element_type=jnp.float32)
        outs[slot][...] = total
        if slot == 0:
            outs[slots][...] = total.astype(jnp.bfloat16)


def first_partial_kernel(inner, tokens, *refs):
    partial_kernel(inner, tokens, 1, *refs[:inner], *refs)


CHUNK = 32


def own_gradient(near, at, refs):
    total0, total1, a3, b3, c3 = refs
    end = total0[at, :] + c3[at, :].astype(jnp.float32)
    inside = total1[at, :] + a3[at, :].astype(jnp.float32) + b3[at, :].astype(jnp.float32)
    return jnp.where(near == 0, end, inside)


def drift_kernel(*refs):
    gradient_refs, (weights, first, second, anchor), drift_ref = refs[:5], refs[5:9], refs[9]
    half = drift_ref.shape[0]
    _, _, near = mirrored()
    base = (1 - lax.axis_index("rep")) * half

    @pl.loop(0, half // CHUNK)
    def _(step):
        at = pl.ds(pl.multiple_of(base + step * CHUNK, CHUNK), CHUNK)
        gradient = own_gradient(near, at, gradient_refs)
        _, drift = inner_update(gradient, weights[at, :], first[at, :], second[at, :], anchor[at, :])
        drift_ref[pl.ds(pl.multiple_of(step * CHUNK, CHUNK), CHUNK), :] = drift


def update_kernel(*refs):
    gradient_refs, (weights, first, second, anchor), (first_ref, drift_ref) = refs[:5], refs[5:9], refs[9:]
    half = drift_ref.shape[0]
    _, _, near = mirrored()
    r = lax.axis_index("rep")

    @pl.loop(0, half // CHUNK)
    def _(step):
        at = pl.ds(pl.multiple_of(r * half + step * CHUNK, CHUNK), CHUNK)
        gradient = own_gradient(near, at, gradient_refs)
        first_next, drift = inner_update(gradient, weights[at, :], first[at, :], second[at, :], anchor[at, :])
        first_ref[at, :] = first_next
        drift_ref[pl.ds(pl.multiple_of(step * CHUNK, CHUNK), CHUNK), :] = drift

    @pl.loop(0, half // CHUNK)
    def _(step):
        at = pl.ds(pl.multiple_of((1 - r) * half + step * CHUNK, CHUNK), CHUNK)
        gradient = own_gradient(near, at, gradient_refs)
        first_ref[at, :] = decay_first * first[at, :] + (1.0 - decay_first) * gradient


def outer_kernel(drift, other, anchor, momentum, out):
    half = out.shape[0]
    at = pl.ds(pl.multiple_of(lax.axis_index("rep") * half, half), half)
    out[...] = outer_update((drift[...] + other[...]) / 2, anchor[at, :], momentum[at, :])


def values_kernel(inner, tokens, rows, *refs):
    firsts, seconds, lasts = refs[:inner], refs[inner : 2 * inner], refs[2 * inner : 3 * inner]
    mine_ref, other_ref, mine2_ref, other2_ref, mine3_ref, other3_ref = refs[3 * inner : 3 * inner + 6]
    own_ref, sent_refs, weights = refs[3 * inner + 6], refs[3 * inner + 7 : -1], refs[-1]
    half = rows // 2
    r = lax.axis_index("rep")
    _, _, near = mirrored()

    def put(t, which, value):
        weights[pl.ds(pl.multiple_of(t * rows + which * half, half), half), :] = value

    for slot, t in ((0, near), (1, 1 - near)):
        put(t, r, mine_ref[slot])
        put(t, 1 - r, other_ref[slot])
    put(2, r, mine2_ref[...])
    put(2, 1 - r, other2_ref[...])
    put(3, r, mine3_ref[...])
    put(3, 1 - r, other3_ref[...])
    for k in range(inner):
        blocks = (lasts[k][tokens:], lasts[k][:tokens], seconds[k][...], firsts[k][:tokens])
        total = jnp.dot(jnp.concatenate(blocks, axis=1), weights[...], preferred_element_type=jnp.float32)
        if k == 0:
            own_ref[...] = total
        else:
            sent_refs[k - 1][...] = total.astype(jnp.bfloat16)


def call(kernel, name, out, inputs, flops, scratch=()):
    moved = sum(x.size * x.dtype.itemsize for x in list(inputs) + list(out))
    return pl.pallas_call(
        kernel,
        out_shape=out,
        in_specs=[pl.BlockSpec(memory_space=pltpu.VMEM)] * len(inputs),
        out_specs=[pl.BlockSpec(memory_space=pltpu.VMEM)] * len(out),
        scratch_shapes=list(scratch),
        compiler_params=pltpu.CompilerParams(vmem_limit_bytes=VMEM_BYTES),
        cost_estimate=pl.CostEstimate(flops=flops, bytes_accessed=moved, transcendentals=0),
        name=name,
    )(*inputs)


def on_device(acts, value_cots, inner_weights, first_moment, second_moment, anchor, outer_momentum):
    inner = lax.axis_size("fsdp") // PLANES
    rows, width = anchor.shape
    if inner != 4 or lax.axis_size("rep") != 2 or rows % 256:
        return general(acts, value_cots, inner_weights, first_moment, second_moment, anchor, outer_momentum)
    tokens = acts.shape[1]
    half = rows // 2
    at_end = mirrored()[2] == 0

    def line(x, *pairs):
        return lax.ppermute(x, "fsdp", [(a * inner + i, b * inner + i) for a, b in pairs for i in range(inner)])

    def across(x, k):
        return lax.ppermute(x, "fsdp", [(p * inner + i, p * inner + (i ^ k)) for p in range(PLANES) for i in range(inner)])

    def swap(x):
        return lax.ppermute(x, "rep", [(0, 1), (1, 0)])

    def inward(x):
        return line(x, (0, 1), (3, 2))

    def middle(x):
        return line(x, (1, 2), (2, 1))

    def outward(x):
        return line(x, (1, 0), (2, 3))

    def around(blocks):
        return [blocks[0]] + [across(blocks[k], k) for k in range(1, inner)]

    firsts = around(repack([acts[0], value_cots[0]], inner, (3,), rows))
    seconds = around(repack([acts[0]], inner, (2,), rows))
    lasts = around(repack([acts[0]], inner, (1, 0), rows))

    f32 = jax.ShapeDtypeStruct((rows, width), jnp.float32)
    bf16 = jax.ShapeDtypeStruct((rows, width), jnp.bfloat16)
    flops = 2 * inner * tokens * rows * width
    total3, sent3 = call(partial(first_partial_kernel, inner, tokens), "partial_first", [f32, bf16], firsts, flops)
    total2, sent2 = call(partial(partial_kernel, inner, tokens, 1), "partial_second", [f32, bf16], firsts + seconds, flops)
    total1, total0, sent1 = call(
        partial(partial_kernel, inner, tokens, 2), "partial_last", [f32, f32, bf16], firsts + lasts, 2 * flops
    )
    a1 = inward(sent3)
    a2 = inward(sent2)
    a3 = inward(sent1)

    def add(total, got):
        return (total + got.astype(jnp.float32)).astype(jnp.bfloat16)

    b2 = middle(add(total3, a1))
    b3 = middle(add(total2, a2))
    c3 = outward(add(total0, b2))
    state = [total0, total1, a3, b3, c3, inner_weights[0], first_moment[0], second_moment[0], anchor]
    half_block = jax.ShapeDtypeStruct((half, width), jnp.float32)
    (drift_out,) = call(drift_kernel, "drift", [half_block], state, 0)
    drift_in = swap(drift_out)
    first_next, drift = call(update_kernel, "update", [f32, half_block], state, 0)
    (mine,) = call(
        outer_kernel,
        "outer",
        [jax.ShapeDtypeStruct((half, width), jnp.bfloat16)],
        [drift, drift_in, anchor, outer_momentum],
        0,
    )
    beside = line(mine, (0, 1), (1, 0), (2, 3), (3, 2))
    far2 = middle(mine)
    far3 = middle(beside)
    mine2 = jnp.where(at_end, outward(far2), far2)
    mine3 = jnp.where(at_end, outward(far3), far3)
    mine = jnp.stack([mine, beside])
    pieces = [mine, swap(mine), mine2, swap(mine2), mine3, swap(mine3)]
    block = jax.ShapeDtypeStruct((tokens, width), jnp.bfloat16)
    values, *sent = call(
        partial(values_kernel, inner, tokens, rows),
        "values",
        [jax.ShapeDtypeStruct((tokens, width), jnp.float32)] + [block] * (inner - 1),
        firsts + seconds + lasts + pieces,
        4 * flops,
        [pltpu.VMEM((PLANES * rows, width), jnp.bfloat16)],
    )
    for k in range(1, inner):
        values = values + across(sent[k - 1], k).astype(jnp.float32)
    return (first_next[None], values.astype(jnp.bfloat16)[None])


def solution(mesh):
    placed = (
        P("rep", "fsdp", None),
        P("rep", "fsdp", None),
        P("rep", "fsdp", None),
        P("rep", "fsdp", None),
        P("rep", "fsdp", None),
        P("fsdp", None),
        P("fsdp", None),
    )
    return jax.shard_map(
        on_device,
        mesh=mesh,
        in_specs=placed,
        out_specs=(P("rep", "fsdp", None), P("rep", "fsdp", None)),
        check_vma=False,
    )
```

```python
from functools import partial

import jax
import jax.numpy as jnp
from jax import lax
from jax.experimental import pallas as pl
from jax.experimental.pallas import tpu as pltpu
from jax.sharding import PartitionSpec as P

decay_first = 0.9
decay_second = 0.95
inner_rate = 0.006
epsilon = 1e-08
outer_rate = 0.7
outer_decay = 0.9

PLANES = 4
CONTRACT_ROWS = (((0,), (0,)), ((), ()))
VMEM_BYTES = 16 * 1024 * 1024


def outer_update(average, anchor_rows, momentum_rows):
    velocity = outer_decay * momentum_rows + average
    return (anchor_rows - outer_rate * (average + outer_decay * velocity)).astype(jnp.bfloat16)


def inner_update(gradient, inner_weights, first_moment, second_moment, anchor):
    first_next = decay_first * first_moment + (1.0 - decay_first) * gradient
    second_next = decay_second * second_moment + (1.0 - decay_second) * gradient * gradient
    stepped = inner_weights - inner_rate * first_next / (jnp.sqrt(second_next) + epsilon)
    return first_next, anchor - stepped


def general(acts, value_cots, inner_weights, first_moment, second_moment, anchor, outer_momentum):
    tokens_local = acts[0]
    columns = lax.all_to_all(tokens_local, "fsdp", split_axis=1, concat_axis=0, tiled=True)
    cots = lax.all_gather(value_cots[0], "fsdp", axis=0, tiled=True)
    gradient = lax.dot_general(columns, cots, CONTRACT_ROWS, preferred_element_type=jnp.float32)
    first_next, drift = inner_update(gradient, inner_weights[0], first_moment[0], second_moment[0], anchor)
    average = lax.psum(drift, "rep") / lax.axis_size("rep")
    weights_next = outer_update(average, anchor, outer_momentum)
    gathered = lax.all_gather(weights_next, "fsdp", axis=0, tiled=True)
    values = jnp.dot(tokens_local, gathered, preferred_element_type=jnp.float32)
    return (first_next[None], values.astype(jnp.bfloat16)[None])


def mirrored():
    planes_at = lax.axis_size("fsdp") // PLANES
    f = lax.axis_index("fsdp")
    o = f // planes_at
    return o, lax.rem(f, planes_at), jnp.where(o < PLANES // 2, o, PLANES - 1 - o)


def repack_kernel(inner, targets, *refs):
    acts_ref, cots, out = refs[0], refs[1:-1], refs[-1]
    tokens, rows = acts_ref.shape[0], out.shape[2]
    o, _, _ = mirrored()
    for place in range(inner):
        for slot, t in enumerate(targets):
            plane = jnp.where(o < PLANES // 2, t, PLANES - 1 - t)
            start = pl.multiple_of((plane * inner + place) * rows, rows)
            out[place, slot * tokens : (slot + 1) * tokens] = acts_ref[:, pl.ds(start, rows)]
        for cots_ref in cots:
            out[place, len(targets) * tokens :] = cots_ref[...]


def repack(inputs, inner, targets, rows):
    tokens = inputs[0].shape[0]
    out = jax.ShapeDtypeStruct((inner, (len(targets) + len(inputs) - 1) * tokens, rows), jnp.bfloat16)
    return call(partial(repack_kernel, inner, targets), "repack", [out], inputs, 0)[0]


def partial_kernel(slots, first, block, *outs):
    inner, tokens, _ = first.shape
    tokens = tokens // 2
    cots = jnp.concatenate([first[k, tokens:] for k in range(inner)], axis=0)
    for slot in range(slots):
        columns = jnp.concatenate([block[k, slot * tokens : (slot + 1) * tokens] for k in range(inner)], axis=0)
        total = lax.dot_general(columns, cots, CONTRACT_ROWS, preferred_element_type=jnp.float32)
        outs[slot][...] = total
        if slot == 0:
            outs[slots][...] = total.astype(jnp.bfloat16)


def first_partial_kernel(first, *outs):
    partial_kernel(1, first, first, *outs)


CHUNK = 32


def own_gradient(near, at, refs):
    total0, total1, a3, b3, c3 = refs
    end = total0[at, :] + c3[at, :].astype(jnp.float32)
    inside = total1[at, :] + a3[at, :].astype(jnp.float32) + b3[at, :].astype(jnp.float32)
    return jnp.where(near == 0, end, inside)


def drift_kernel(*refs):
    gradient_refs, (weights, first, second, anchor), drift_ref = refs[:5], refs[5:9], refs[9]
    half = drift_ref.shape[0]
    _, _, near = mirrored()
    base = (1 - lax.axis_index("rep")) * half

    @pl.loop(0, half // CHUNK)
    def _(step):
        at = pl.ds(pl.multiple_of(base + step * CHUNK, CHUNK), CHUNK)
        gradient = own_gradient(near, at, gradient_refs)
        _, drift = inner_update(gradient, weights[at, :], first[at, :], second[at, :], anchor[at, :])
        drift_ref[pl.ds(pl.multiple_of(step * CHUNK, CHUNK), CHUNK), :] = drift


def update_kernel(*refs):
    gradient_refs, (weights, first, second, anchor), (first_ref, drift_ref) = refs[:5], refs[5:9], refs[9:]
    half = drift_ref.shape[0]
    _, _, near = mirrored()
    r = lax.axis_index("rep")

    @pl.loop(0, half // CHUNK)
    def _(step):
        at = pl.ds(pl.multiple_of(r * half + step * CHUNK, CHUNK), CHUNK)
        gradient = own_gradient(near, at, gradient_refs)
        first_next, drift = inner_update(gradient, weights[at, :], first[at, :], second[at, :], anchor[at, :])
        first_ref[at, :] = first_next
        drift_ref[pl.ds(pl.multiple_of(step * CHUNK, CHUNK), CHUNK), :] = drift

    @pl.loop(0, half // CHUNK)
    def _(step):
        at = pl.ds(pl.multiple_of((1 - r) * half + step * CHUNK, CHUNK), CHUNK)
        gradient = own_gradient(near, at, gradient_refs)
        first_ref[at, :] = decay_first * first[at, :] + (1.0 - decay_first) * gradient


def outer_kernel(drift, other, anchor, momentum, out):
    half = out.shape[0]
    at = pl.ds(pl.multiple_of(lax.axis_index("rep") * half, half), half)
    out[...] = outer_update((drift[...] + other[...]) / 2, anchor[at, :], momentum[at, :])


def values_kernel(first, second, last, mine_ref, other_ref, mine2_ref, other2_ref, mine3_ref, other3_ref, out, weights):
    inner, tokens, rows = second.shape
    half = rows // 2
    r = lax.axis_index("rep")
    _, _, near = mirrored()

    def put(t, which, value):
        weights[pl.ds(pl.multiple_of(t * rows + which * half, half), half), :] = value

    for slot, t in ((0, near), (1, 1 - near)):
        put(t, r, mine_ref[slot])
        put(t, 1 - r, other_ref[slot])
    put(2, r, mine2_ref[...])
    put(2, 1 - r, other2_ref[...])
    put(3, r, mine3_ref[...])
    put(3, 1 - r, other3_ref[...])
    for k in range(inner):
        blocks = (last[k, tokens:], last[k, :tokens], second[k], first[k, :tokens])
        total = jnp.dot(jnp.concatenate(blocks, axis=1), weights[...], preferred_element_type=jnp.float32)
        out[k] = total.astype(jnp.bfloat16)


def call(kernel, name, out, inputs, flops, scratch=()):
    moved = sum(x.size * x.dtype.itemsize for x in list(inputs) + list(out))
    return pl.pallas_call(
        kernel,
        out_shape=out,
        in_specs=[pl.BlockSpec(memory_space=pltpu.VMEM)] * len(inputs),
        out_specs=[pl.BlockSpec(memory_space=pltpu.VMEM)] * len(out),
        scratch_shapes=list(scratch),
        compiler_params=pltpu.CompilerParams(vmem_limit_bytes=VMEM_BYTES),
        cost_estimate=pl.CostEstimate(flops=flops, bytes_accessed=moved, transcendentals=0),
        name=name,
    )(*inputs)


def on_device(acts, value_cots, inner_weights, first_moment, second_moment, anchor, outer_momentum):
    inner = lax.axis_size("fsdp") // PLANES
    rows, width = anchor.shape
    if inner != 4 or lax.axis_size("rep") != 2 or rows % 256:
        return general(acts, value_cots, inner_weights, first_moment, second_moment, anchor, outer_momentum)
    tokens = acts.shape[1]
    half = rows // 2
    at_end = mirrored()[2] == 0

    def line(x, *pairs):
        return lax.ppermute(x, "fsdp", [(a * inner + i, b * inner + i) for a, b in pairs for i in range(inner)])

    def around(x):
        groups = [[p * inner + i for i in range(inner)] for p in range(PLANES)]
        return lax.all_to_all(x, "fsdp", split_axis=0, concat_axis=0, axis_index_groups=groups)

    def swap(x):
        return lax.ppermute(x, "rep", [(0, 1), (1, 0)])

    def inward(x):
        return line(x, (0, 1), (3, 2))

    def middle(x):
        return line(x, (1, 2), (2, 1))

    def outward(x):
        return line(x, (1, 0), (2, 3))

    first = around(repack([acts[0], value_cots[0]], inner, (3,), rows))
    second = around(repack([acts[0]], inner, (2,), rows))
    last = around(repack([acts[0]], inner, (1, 0), rows))

    f32 = jax.ShapeDtypeStruct((rows, width), jnp.float32)
    bf16 = jax.ShapeDtypeStruct((rows, width), jnp.bfloat16)
    flops = 2 * inner * tokens * rows * width
    total3, sent3 = call(first_partial_kernel, "partial_first", [f32, bf16], [first], flops)
    total2, sent2 = call(partial(partial_kernel, 1), "partial_second", [f32, bf16], [first, second], flops)
    total1, total0, sent1 = call(partial(partial_kernel, 2), "partial_last", [f32, f32, bf16], [first, last], 2 * flops)
    a1 = inward(sent3)
    a2 = inward(sent2)
    a3 = inward(sent1)

    def add(total, got):
        return (total + got.astype(jnp.float32)).astype(jnp.bfloat16)

    b2 = middle(add(total3, a1))
    b3 = middle(add(total2, a2))
    c3 = outward(add(total0, b2))
    state = [total0, total1, a3, b3, c3, inner_weights[0], first_moment[0], second_moment[0], anchor]
    half_block = jax.ShapeDtypeStruct((half, width), jnp.float32)
    (drift_out,) = call(drift_kernel, "drift", [half_block], state, 0)
    drift_in = swap(drift_out)
    first_next, drift = call(update_kernel, "update", [f32, half_block], state, 0)
    (mine,) = call(
        outer_kernel,
        "outer",
        [jax.ShapeDtypeStruct((half, width), jnp.bfloat16)],
        [drift, drift_in, anchor, outer_momentum],
        0,
    )
    beside = line(mine, (0, 1), (1, 0), (2, 3), (3, 2))
    far2 = middle(mine)
    far3 = middle(beside)
    mine2 = jnp.where(at_end, outward(far2), far2)
    mine3 = jnp.where(at_end, outward(far3), far3)
    mine = jnp.stack([mine, beside])
    pieces = [mine, swap(mine), mine2, swap(mine2), mine3, swap(mine3)]
    (sent,) = call(
        values_kernel,
        "values",
        [jax.ShapeDtypeStruct((inner, tokens, width), jnp.bfloat16)],
        [first, second, last] + pieces,
        4 * flops,
        [pltpu.VMEM((PLANES * rows, width), jnp.bfloat16)],
    )
    values = jnp.sum(around(sent).astype(jnp.float32), axis=0)
    return (first_next[None], values.astype(jnp.bfloat16)[None])


def solution(mesh):
    placed = (
        P("rep", "fsdp", None),
        P("rep", "fsdp", None),
        P("rep", "fsdp", None),
        P("rep", "fsdp", None),
        P("rep", "fsdp", None),
        P("fsdp", None),
        P("fsdp", None),
    )
    return jax.shard_map(
        on_device,
        mesh=mesh,
        in_specs=placed,
        out_specs=(P("rep", "fsdp", None), P("rep", "fsdp", None)),
        check_vma=False,
    )
```

```python
from functools import partial

import jax
import jax.numpy as jnp
from jax import lax
from jax.experimental import pallas as pl
from jax.experimental.pallas import tpu as pltpu
from jax.sharding import PartitionSpec as P

decay_first = 0.9
decay_second = 0.95
inner_rate = 0.006
epsilon = 1e-08
outer_rate = 0.7
outer_decay = 0.9

PLANES = 4
PARTS = 1
CHUNK = 32
CONTRACT_ROWS = (((0,), (0,)), ((), ()))
VMEM_BYTES = 16 * 1024 * 1024


def outer_update(average, anchor_rows, momentum_rows):
    velocity = outer_decay * momentum_rows + average
    return (anchor_rows - outer_rate * (average + outer_decay * velocity)).astype(jnp.bfloat16)


def inner_update(gradient, inner_weights, first_moment, second_moment, anchor):
    first_next = decay_first * first_moment + (1.0 - decay_first) * gradient
    second_next = decay_second * second_moment + (1.0 - decay_second) * gradient * gradient
    stepped = inner_weights - inner_rate * first_next / (jnp.sqrt(second_next) + epsilon)
    return first_next, anchor - stepped


def general(acts, value_cots, inner_weights, first_moment, second_moment, anchor, outer_momentum):
    tokens_local = acts[0]
    columns = lax.all_to_all(tokens_local, "fsdp", split_axis=1, concat_axis=0, tiled=True)
    cots = lax.all_gather(value_cots[0], "fsdp", axis=0, tiled=True)
    gradient = lax.dot_general(columns, cots, CONTRACT_ROWS, preferred_element_type=jnp.float32)
    first_next, drift = inner_update(gradient, inner_weights[0], first_moment[0], second_moment[0], anchor)
    average = lax.psum(drift, "rep") / lax.axis_size("rep")
    weights_next = outer_update(average, anchor, outer_momentum)
    gathered = lax.all_gather(weights_next, "fsdp", axis=0, tiled=True)
    values = jnp.dot(tokens_local, gathered, preferred_element_type=jnp.float32)
    return (first_next[None], values.astype(jnp.bfloat16)[None])


def flip(at, bits):
    low = lax.rem(at, 2)
    return (at // 2 + bits // 2 - 2 * (at // 2) * (bits // 2)) * 2 + low + bits % 2 - 2 * low * (bits % 2)


def call(kernel, name, out, inputs, flops, scratch=()):
    moved = sum(x.size * x.dtype.itemsize for x in list(inputs) + list(out))
    return pl.pallas_call(
        kernel,
        out_shape=out,
        in_specs=[pl.BlockSpec(memory_space=pltpu.VMEM)] * len(inputs),
        out_specs=[pl.BlockSpec(memory_space=pltpu.VMEM)] * len(out),
        scratch_shapes=list(scratch),
        compiler_params=pltpu.CompilerParams(vmem_limit_bytes=VMEM_BYTES),
        cost_estimate=pl.CostEstimate(flops=flops, bytes_accessed=moved, transcendentals=0),
        name=name,
    )(*inputs)


def repack_kernel(inner, rows, messages, acts_ref, cots_ref, *outs):
    f = lax.axis_index("fsdp")
    o, i = f // inner, lax.rem(f, inner)
    for number, (planes, columns) in enumerate(messages):
        for k in range(inner):
            out = outs[number * inner + k]
            for slot, bits in enumerate(planes):
                start = pl.multiple_of((flip(o, bits) * inner + flip(i, k)) * rows, rows)
                out[:, slot * rows : (slot + 1) * rows] = acts_ref[:, pl.ds(start, rows)]
            if columns:
                out[:, len(planes) * rows :] = cots_ref[:, columns[0] : columns[1]]


def repack(acts, cots, inner, rows, messages):
    tokens = acts.shape[0]
    out = []
    for planes, columns in messages:
        wide = len(planes) * rows + (columns[1] - columns[0] if columns else 0)
        out += [jax.ShapeDtypeStruct((tokens, wide), jnp.bfloat16)] * inner
    got = call(partial(repack_kernel, inner, rows, messages), "repack", out, [acts, cots], 0)
    return [got[n * inner : (n + 1) * inner] for n in range(len(messages))]


def gradient_kernel(inner, rows, acts_at, cots_at, *refs):
    acts_refs, cots_refs, added, out = refs[:inner], refs[inner : 2 * inner], refs[2 * inner : -1], refs[-1]
    columns = jnp.concatenate([ref[:, acts_at : acts_at + rows] for ref in acts_refs], axis=0)
    cots = jnp.concatenate([ref[:, cots_at : cots_at + out.shape[1]] for ref in cots_refs], axis=0)
    total = lax.dot_general(columns, cots, CONTRACT_ROWS, preferred_element_type=jnp.float32)
    for ref in added:
        total += ref[...].astype(jnp.float32)
    out[...] = total.astype(out.dtype)


def gradient_at(at, refs):
    total, beside, far = refs
    return total[at, :] + beside[at, :].astype(jnp.float32) + far[at, :].astype(jnp.float32)


def steps(half, which, body):
    @pl.loop(0, half // CHUNK)
    def _(step):
        start = pl.multiple_of(step * CHUNK, CHUNK)
        body(pl.ds(start, CHUNK), pl.ds(pl.multiple_of(which * half + start, CHUNK), CHUNK))


def drift_kernel(columns, *refs):
    gradient_refs, (weights, first, second, anchor), drift_ref = refs[:3], refs[3:7], refs[7]
    cols = slice(*columns)

    def body(here, at):
        gradient = gradient_at(at, gradient_refs)
        state = (weights[at, cols], first[at, cols], second[at, cols], anchor[at, cols])
        drift_ref[here, :] = inner_update(gradient, *state)[1]

    steps(drift_ref.shape[0], 1 - lax.axis_index("rep"), body)


def update_kernel(columns, *refs):
    gradient_refs, (weights, first, second, anchor), earlier = refs[:3], refs[3:7], refs[7:-2]
    first_ref, drift_ref = refs[-2:]
    cols = slice(*columns)
    half = drift_ref.shape[0]
    r = lax.axis_index("rep")

    def body(here, at):
        gradient = gradient_at(at, gradient_refs)
        state = (weights[at, cols], first[at, cols], second[at, cols], anchor[at, cols])
        first_ref[at, cols], drift_ref[here, :] = inner_update(gradient, *state)

    def others(here, at):
        first_ref[at, cols] = decay_first * first[at, cols] + (1.0 - decay_first) * gradient_at(at, gradient_refs)

    steps(half, r, body)
    steps(half, 1 - r, others)
    for ref in earlier:
        first_ref[:, : columns[0]] = ref[:, : columns[0]]


def outer_kernel(columns, drift, other, anchor, momentum, out):
    half = out.shape[0]
    at = pl.ds(pl.multiple_of(lax.axis_index("rep") * half, half), half)
    cols = slice(*columns)
    out[...] = outer_update((drift[...] + other[...]) / 2, anchor[at, cols], momentum[at, cols])


def values_kernel(inner, rows, places, *refs):
    messages = [refs[n * inner : (n + 1) * inner] for n in range(3)]
    pieces, own_ref, sent_refs, weights = refs[3 * inner : 3 * inner + 8], refs[3 * inner + 8], refs[3 * inner + 9 : -1], refs[-1]
    half = rows // 2
    r = lax.axis_index("rep")
    for bits in range(PLANES):
        for which, piece in ((r, pieces[2 * bits]), (1 - r, pieces[2 * bits + 1])):
            weights[pl.ds(pl.multiple_of(bits * rows + which * half, half), half), :] = piece[...]
    for k in range(inner):
        blocks = [messages[number][k][:, at : at + rows] for number, at in places]
        total = jnp.dot(jnp.concatenate(blocks, axis=1), weights[...], preferred_element_type=jnp.float32)
        if k == 0:
            own_ref[...] = total
        else:
            sent_refs[k - 1][...] = total.astype(jnp.bfloat16)


def on_device(acts, value_cots, inner_weights, first_moment, second_moment, anchor, outer_momentum):
    inner = lax.axis_size("fsdp") // PLANES
    rows, width = anchor.shape
    if inner != 4 or lax.axis_size("rep") != 2 or rows % 256 or width % (128 * PARTS):
        return general(acts, value_cots, inner_weights, first_moment, second_moment, anchor, outer_momentum)
    tokens = acts.shape[1]
    half = rows // 2
    part_width = width // PARTS

    def planes(x, bits):
        return lax.ppermute(x, "fsdp", [(p * inner + i, (p ^ bits) * inner + i) for p in range(PLANES) for i in range(inner)])

    def across(x, k):
        return lax.ppermute(x, "fsdp", [(p * inner + i, p * inner + (i ^ k)) for p in range(PLANES) for i in range(inner)])

    def around(blocks):
        return [blocks[0]] + [across(blocks[k], k) for k in range(1, inner)]

    def swap(x):
        return lax.ppermute(x, "rep", [(0, 1), (1, 0)])

    later = (part_width, width) if PARTS > 1 else None
    (first,) = repack(acts[0], value_cots[0], inner, rows, [((3,), (0, part_width))])
    second, last = repack(acts[0], value_cots[0], inner, rows, [((2, 1), later), ((0,), None)])
    messages = [around(first), around(second), around(last)]
    places = [(2, 0), (1, rows), (1, 0), (0, 0)]

    def gradient(bits, part, dtype, *added):
        number, at = places[bits]
        cots, cots_at = (messages[0], rows) if part == 0 else (messages[1], 2 * rows + (part - 1) * part_width)
        out = jax.ShapeDtypeStruct((rows, part_width), dtype)
        kernel = partial(gradient_kernel, inner, rows, at, cots_at)
        flops = 2 * inner * tokens * rows * part_width
        return call(kernel, "gradient", [out], messages[number] + cots + list(added), flops)[0]

    state = [inner_weights[0], first_moment[0], second_moment[0], anchor]
    half_block = jax.ShapeDtypeStruct((half, part_width), jnp.float32)
    first_next, values = [], []
    for part in range(PARTS):
        columns = (part * part_width, (part + 1) * part_width)
        beside_far = planes(gradient(3, part, jnp.bfloat16), 1)
        beside = planes(gradient(1, part, jnp.bfloat16), 1)
        far = planes(gradient(2, part, jnp.bfloat16, beside_far), 2)
        known = [gradient(0, part, jnp.float32), beside, far] + state
        (drift_out,) = call(partial(drift_kernel, columns), "drift", [half_block], known, 0)
        drift_in = swap(drift_out)
        full = jax.ShapeDtypeStruct((rows, width), jnp.float32)
        *first_next, drift = call(partial(update_kernel, columns), "update", [full, half_block], known + first_next, 0)
        new_half = jax.ShapeDtypeStruct((half, part_width), jnp.bfloat16)
        (mine,) = call(partial(outer_kernel, columns), "outer", [new_half], [drift, drift_in, anchor, outer_momentum], 0)
        mine2 = planes(mine, 2)
        mine1 = planes(mine, 1)
        mine3 = planes(mine2, 1)
        pieces = [y for x in (mine, mine1, mine2, mine3) for y in (x, swap(x))]
        block = jax.ShapeDtypeStruct((tokens, part_width), jnp.bfloat16)
        own, *sent = call(
            partial(values_kernel, inner, rows, places),
            "values",
            [jax.ShapeDtypeStruct((tokens, part_width), jnp.float32)] + [block] * (inner - 1),
            messages[0] + messages[1] + messages[2] + pieces,
            2 * inner * tokens * PLANES * rows * part_width,
            [pltpu.VMEM((PLANES * rows, part_width), jnp.bfloat16)],
        )
        for k in range(1, inner):
            own = own + across(sent[k - 1], k).astype(jnp.float32)
        values.append(own.astype(jnp.bfloat16))
    values = values[0] if PARTS == 1 else jnp.concatenate(values, axis=1)
    return (first_next[0][None], values[None])


def solution(mesh):
    placed = (
        P("rep", "fsdp", None),
        P("rep", "fsdp", None),
        P("rep", "fsdp", None),
        P("rep", "fsdp", None),
        P("rep", "fsdp", None),
        P("fsdp", None),
        P("fsdp", None),
    )
    return jax.shard_map(
        on_device,
        mesh=mesh,
        in_specs=placed,
        out_specs=(P("rep", "fsdp", None), P("rep", "fsdp", None)),
        check_vma=False,
    )
```

```python
from functools import partial

import jax
import jax.numpy as jnp
from jax import lax
from jax.experimental import pallas as pl
from jax.experimental.pallas import tpu as pltpu
from jax.sharding import PartitionSpec as P

decay_first = 0.9
decay_second = 0.95
inner_rate = 0.006
epsilon = 1e-08
outer_rate = 0.7
outer_decay = 0.9

PLANES = 4
PARTS = 2
CHUNK = 32
CONTRACT_ROWS = (((0,), (0,)), ((), ()))
VMEM_BYTES = 16 * 1024 * 1024


def outer_update(average, anchor_rows, momentum_rows):
    velocity = outer_decay * momentum_rows + average
    return (anchor_rows - outer_rate * (average + outer_decay * velocity)).astype(jnp.bfloat16)


def inner_update(gradient, inner_weights, first_moment, second_moment, anchor):
    first_next = decay_first * first_moment + (1.0 - decay_first) * gradient
    second_next = decay_second * second_moment + (1.0 - decay_second) * gradient * gradient
    stepped = inner_weights - inner_rate * first_next / (jnp.sqrt(second_next) + epsilon)
    return first_next, anchor - stepped


def general(acts, value_cots, inner_weights, first_moment, second_moment, anchor, outer_momentum):
    tokens_local = acts[0]
    columns = lax.all_to_all(tokens_local, "fsdp", split_axis=1, concat_axis=0, tiled=True)
    cots = lax.all_gather(value_cots[0], "fsdp", axis=0, tiled=True)
    gradient = lax.dot_general(columns, cots, CONTRACT_ROWS, preferred_element_type=jnp.float32)
    first_next, drift = inner_update(gradient, inner_weights[0], first_moment[0], second_moment[0], anchor)
    average = lax.psum(drift, "rep") / lax.axis_size("rep")
    weights_next = outer_update(average, anchor, outer_momentum)
    gathered = lax.all_gather(weights_next, "fsdp", axis=0, tiled=True)
    values = jnp.dot(tokens_local, gathered, preferred_element_type=jnp.float32)
    return (first_next[None], values.astype(jnp.bfloat16)[None])


def flip(at, bits):
    low = lax.rem(at, 2)
    return (at // 2 + bits // 2 - 2 * (at // 2) * (bits // 2)) * 2 + low + bits % 2 - 2 * low * (bits % 2)


def call(kernel, name, out, inputs, flops, scratch=(), after=()):
    moved = sum(x.size * x.dtype.itemsize for x in list(inputs) + list(out))
    count = len(inputs)

    def without_after(*refs):
        kernel(*refs[:count], *refs[count + len(after) :])

    return pl.pallas_call(
        without_after,
        out_shape=out,
        in_specs=[pl.BlockSpec(memory_space=pltpu.VMEM)] * count + [pl.BlockSpec(memory_space=pl.ANY)] * len(after),
        out_specs=[pl.BlockSpec(memory_space=pltpu.VMEM)] * len(out),
        scratch_shapes=list(scratch),
        compiler_params=pltpu.CompilerParams(vmem_limit_bytes=VMEM_BYTES),
        cost_estimate=pl.CostEstimate(flops=flops, bytes_accessed=moved, transcendentals=0),
        name=name,
    )(*inputs, *after)


def repack_kernel(inner, rows, messages, acts_ref, cots_ref, *outs):
    f = lax.axis_index("fsdp")
    o, i = f // inner, lax.rem(f, inner)
    for number, (planes, columns) in enumerate(messages):
        for k in range(inner):
            out = outs[number * inner + k]
            for slot, bits in enumerate(planes):
                start = pl.multiple_of((flip(o, bits) * inner + flip(i, k)) * rows, rows)
                out[:, slot * rows : (slot + 1) * rows] = acts_ref[:, pl.ds(start, rows)]
            if columns:
                out[:, len(planes) * rows :] = cots_ref[:, columns[0] : columns[1]]


def repack(acts, cots, inner, rows, messages, after=()):
    tokens = acts.shape[0]
    out = []
    for planes, columns in messages:
        wide = len(planes) * rows + (columns[1] - columns[0] if columns else 0)
        out += [jax.ShapeDtypeStruct((tokens, wide), jnp.bfloat16)] * inner
    got = call(partial(repack_kernel, inner, rows, messages), "repack", out, [acts, cots], 0, after=after)
    return [got[n * inner : (n + 1) * inner] for n in range(len(messages))]


def gradient_kernel(inner, rows, acts_at, cots_at, *refs):
    acts_refs, cots_refs, added, out = refs[:inner], refs[inner : 2 * inner], refs[2 * inner : -1], refs[-1]
    columns = jnp.concatenate([ref[:, acts_at : acts_at + rows] for ref in acts_refs], axis=0)
    cots = jnp.concatenate([ref[:, cots_at : cots_at + out.shape[1]] for ref in cots_refs], axis=0)
    total = lax.dot_general(columns, cots, CONTRACT_ROWS, preferred_element_type=jnp.float32)
    for ref in added:
        total += ref[...].astype(jnp.float32)
    out[...] = total.astype(out.dtype)


def gradient_at(at, refs):
    total, beside, far = refs
    return total[at, :] + beside[at, :].astype(jnp.float32) + far[at, :].astype(jnp.float32)


def drift_kernel(columns, *refs):
    gradient_refs, (weights, first, second, anchor), drift_ref = refs[:3], refs[3:7], refs[7]
    cols = slice(*columns)

    @pl.loop(0, drift_ref.shape[0] // CHUNK)
    def _(step):
        at = pl.ds(pl.multiple_of(step * CHUNK, CHUNK), CHUNK)
        state = (weights[at, cols], first[at, cols], second[at, cols], anchor[at, cols])
        drift_ref[at, :] = inner_update(gradient_at(at, gradient_refs), *state)[1]


def moment_kernel(parts, *refs):
    first, out = refs[-2:]
    width = out.shape[1] // parts

    @pl.loop(0, out.shape[0] // CHUNK)
    def _(step):
        at = pl.ds(pl.multiple_of(step * CHUNK, CHUNK), CHUNK)
        for part in range(parts):
            gradient = gradient_at(at, refs[3 * part : 3 * part + 3])
            cols = slice(part * width, (part + 1) * width)
            out[at, cols] = decay_first * first[at, cols] + (1.0 - decay_first) * gradient


def outer_kernel(columns, drift, other, anchor, momentum, out, mine):
    half = mine.shape[0]
    cols = slice(*columns)

    @pl.loop(0, out.shape[0] // CHUNK)
    def _(step):
        at = pl.ds(pl.multiple_of(step * CHUNK, CHUNK), CHUNK)
        out[at, :] = outer_update((drift[at, :] + other[at, :]) / 2, anchor[at, cols], momentum[at, cols])

    mine[...] = out[pl.ds(pl.multiple_of(lax.axis_index("rep") * half, half), half), :]


def values_kernel(inner, rows, places, *refs):
    messages = [refs[n * inner : (n + 1) * inner] for n in range(PLANES)]
    refs = refs[PLANES * inner :]
    pieces, own_ref, sent_refs, weights = refs[:7], refs[7], refs[8:-1], refs[-1]
    half = rows // 2
    r = lax.axis_index("rep")
    weights[:rows] = pieces[0][...]
    for bits in range(1, PLANES):
        for which, piece in ((r, pieces[2 * bits - 1]), (1 - r, pieces[2 * bits])):
            weights[pl.ds(pl.multiple_of(bits * rows + which * half, half), half), :] = piece[...]
    for k in range(inner):
        blocks = [messages[number][k][:, at : at + rows] for number, at in places]
        total = jnp.dot(jnp.concatenate(blocks, axis=1), weights[...], preferred_element_type=jnp.float32)
        if k == 0:
            own_ref[...] = total
        else:
            sent_refs[k - 1][...] = total.astype(jnp.bfloat16)


def sum_kernel(parts, *refs):
    terms, out = refs[:-1], refs[-1]
    each, width = len(terms) // parts, out.shape[1] // parts
    for part in range(parts):
        total = terms[part * each][...]
        for ref in terms[part * each + 1 : (part + 1) * each]:
            total += ref[...].astype(jnp.float32)
        out[:, part * width : (part + 1) * width] = total.astype(out.dtype)


def on_device(acts, value_cots, inner_weights, first_moment, second_moment, anchor, outer_momentum):
    inner = lax.axis_size("fsdp") // PLANES
    rows, width = anchor.shape
    if inner != 4 or lax.axis_size("rep") != 2 or rows % 256 or width % (128 * PARTS):
        return general(acts, value_cots, inner_weights, first_moment, second_moment, anchor, outer_momentum)
    tokens = acts.shape[1]
    half = rows // 2
    part_width = width // PARTS

    def planes(x, bits):
        return lax.ppermute(x, "fsdp", [(p * inner + i, (p ^ bits) * inner + i) for p in range(PLANES) for i in range(inner)])

    def across(x, k):
        return lax.ppermute(x, "fsdp", [(p * inner + i, p * inner + (i ^ k)) for p in range(PLANES) for i in range(inner)])

    def around(blocks):
        return [blocks[0]] + [across(blocks[k], k) for k in range(1, inner)]

    def swap(x):
        return lax.ppermute(x, "rep", [(0, 1), (1, 0)])

    wanted = [((3,), (0, part_width)), ((1,), None), ((2,), None), ((0,), (part_width, width) if PARTS > 1 else None)]
    places = [(3, 0), (1, 0), (2, 0), (0, 0)]
    messages, arrived = [], []
    for message in wanted:
        (packed,) = repack(acts[0], value_cots[0], inner, rows, [message], arrived)
        messages.append(around(packed))
        arrived = messages[-1][1:2]

    def gradient(bits, part, dtype, *added):
        number, at = places[bits]
        cots, cots_at = (messages[0], rows) if part == 0 else (messages[3], rows + (part - 1) * part_width)
        out = jax.ShapeDtypeStruct((rows, part_width), dtype)
        kernel = partial(gradient_kernel, inner, rows, at, cots_at)
        flops = 2 * inner * tokens * rows * part_width
        return call(kernel, "gradient", [out], messages[number] + cots + list(added), flops)[0]

    state = [inner_weights[0], first_moment[0], second_moment[0], anchor]
    block = jax.ShapeDtypeStruct((rows, part_width), jnp.float32)
    new_block = jax.ShapeDtypeStruct((rows, part_width), jnp.bfloat16)
    new_half = jax.ShapeDtypeStruct((half, part_width), jnp.bfloat16)
    full = jax.ShapeDtypeStruct((rows, width), jnp.float32)
    gradients, terms, earlier = [], [], []
    for part in range(PARTS):
        columns = (part * part_width, (part + 1) * part_width)
        beside_far = planes(gradient(3, part, jnp.bfloat16), 1)
        beside = planes(gradient(1, part, jnp.bfloat16), 1)
        far = planes(gradient(2, part, jnp.bfloat16, beside_far), 2)
        known = [gradient(0, part, jnp.float32), beside, far]
        gradients += known
        (drift,) = call(partial(drift_kernel, columns), "drift", [block], known + state, 0, after=earlier)
        first_next = []
        if part == PARTS - 1:
            first_next = call(partial(moment_kernel, PARTS), "moment", [full], gradients + [first_moment[0]], 0)
        new, mine = call(
            partial(outer_kernel, columns),
            "outer",
            [new_block, new_half],
            [drift, swap(drift), anchor, outer_momentum],
            0,
            after=first_next,
        )
        mine2 = planes(mine, 2)
        mine1 = planes(mine, 1)
        mine3 = planes(mine2, 1)
        earlier = [mine1, mine2]
        pieces = [new] + [y for x in (mine1, mine2, mine3) for y in (x, swap(x))]
        sums = jax.ShapeDtypeStruct((tokens, part_width), jnp.bfloat16)
        own, *sent = call(
            partial(values_kernel, inner, rows, places),
            "values",
            [jax.ShapeDtypeStruct((tokens, part_width), jnp.float32)] + [sums] * (inner - 1),
            sum(messages, []) + pieces,
            2 * inner * tokens * PLANES * rows * part_width,
            [pltpu.VMEM((PLANES * rows, part_width), jnp.bfloat16)],
        )
        terms += [own] + [across(sent[k - 1], k) for k in range(1, inner)]
    whole = jax.ShapeDtypeStruct((tokens, width), jnp.bfloat16)
    (values,) = call(partial(sum_kernel, PARTS), "sum", [whole], terms, 0)
    return (first_next[0][None], values[None])


def solution(mesh):
    placed = (
        P("rep", "fsdp", None),
        P("rep", "fsdp", None),
        P("rep", "fsdp", None),
        P("rep", "fsdp", None),
        P("rep", "fsdp", None),
        P("fsdp", None),
        P("fsdp", None),
    )
    return jax.shard_map(
        on_device,
        mesh=mesh,
        in_specs=placed,
        out_specs=(P("rep", "fsdp", None), P("rep", "fsdp", None)),
        check_vma=False,
    )
```

```python
from functools import partial

import jax
import jax.numpy as jnp
from jax import lax
from jax.experimental import pallas as pl
from jax.experimental.pallas import tpu as pltpu
from jax.sharding import PartitionSpec as P

decay_first = 0.9
decay_second = 0.95
inner_rate = 0.006
epsilon = 1e-08
outer_rate = 0.7
outer_decay = 0.9

PLANES = 4
CHUNK = 32
CONTRACT_ROWS = (((0,), (0,)), ((), ()))
AHEAD_FLOPS = 30 * 10**12
VMEM_BYTES = 16 * 1024 * 1024


def outer_update(average, anchor_rows, momentum_rows):
    velocity = outer_decay * momentum_rows + average
    return (anchor_rows - outer_rate * (average + outer_decay * velocity)).astype(jnp.bfloat16)


def inner_update(gradient, inner_weights, first_moment, second_moment, anchor):
    first_next = decay_first * first_moment + (1.0 - decay_first) * gradient
    second_next = decay_second * second_moment + (1.0 - decay_second) * gradient * gradient
    stepped = inner_weights - inner_rate * first_next / (jnp.sqrt(second_next) + epsilon)
    return first_next, anchor - stepped


def general(acts, value_cots, inner_weights, first_moment, second_moment, anchor, outer_momentum):
    tokens_local = acts[0]
    columns = lax.all_to_all(tokens_local, "fsdp", split_axis=1, concat_axis=0, tiled=True)
    cots = lax.all_gather(value_cots[0], "fsdp", axis=0, tiled=True)
    gradient = lax.dot_general(columns, cots, CONTRACT_ROWS, preferred_element_type=jnp.float32)
    first_next, drift = inner_update(gradient, inner_weights[0], first_moment[0], second_moment[0], anchor)
    average = lax.psum(drift, "rep") / lax.axis_size("rep")
    weights_next = outer_update(average, anchor, outer_momentum)
    gathered = lax.all_gather(weights_next, "fsdp", axis=0, tiled=True)
    values = jnp.dot(tokens_local, gathered, preferred_element_type=jnp.float32)
    return (first_next[None], values.astype(jnp.bfloat16)[None])


def flip(at, bits):
    low = lax.rem(at, 2)
    return (at // 2 + bits // 2 - 2 * (at // 2) * (bits // 2)) * 2 + low + bits % 2 - 2 * low * (bits % 2)


def call(kernel, name, out, inputs, flops, scratch=(), after=(), space=pltpu.VMEM):
    moved = sum(x.size * x.dtype.itemsize for x in list(inputs) + list(out))
    count = len(inputs)

    def without_after(*refs):
        kernel(*refs[:count], *refs[count + len(after) :])

    return pl.pallas_call(
        without_after,
        out_shape=out,
        in_specs=[pl.BlockSpec(memory_space=space)] * count + [pl.BlockSpec(memory_space=pl.ANY)] * len(after),
        out_specs=[pl.BlockSpec(memory_space=pltpu.VMEM)] * len(out),
        scratch_shapes=list(scratch),
        compiler_params=pltpu.CompilerParams(vmem_limit_bytes=VMEM_BYTES),
        cost_estimate=pl.CostEstimate(flops=flops, bytes_accessed=moved, transcendentals=0),
        name=name,
    )(*inputs, *after)


def block_start(inner, rows, bits, k):
    f = lax.axis_index("fsdp")
    return pl.multiple_of((flip(f // inner, bits) * inner + flip(lax.rem(f, inner), k)) * rows, rows)


def pack_first_kernel(inner, rows, acts_ref, cots_ref, *refs):
    outs, sems = refs[:inner], refs[inner]
    copies = []
    for k in range(inner):
        block = acts_ref.at[:, pl.ds(block_start(inner, rows, 3, k), rows)]
        copies.append(pltpu.make_async_copy(block, outs[k].at[:, :rows], sems.at[2 * k]))
        copies.append(pltpu.make_async_copy(cots_ref, outs[k].at[:, rows:], sems.at[2 * k + 1]))
    for copy in copies:
        copy.start()
    for copy in copies:
        copy.wait()


def pack_kernel(inner, rows, blocks, acts_ref, *outs):
    for k in range(inner):
        for slot, bits in enumerate(blocks):
            outs[k][:, slot * rows : (slot + 1) * rows] = acts_ref[:, pl.ds(block_start(inner, rows, bits, k), rows)]


def gradient_kernel(inner, rows, acts_at, *refs):
    acts_refs, cots_refs, out = refs[:inner], refs[inner : 2 * inner], refs[-1]
    columns = jnp.concatenate([ref[:, acts_at : acts_at + rows] for ref in acts_refs], axis=0)
    cots = jnp.concatenate([ref[:, rows:] for ref in cots_refs], axis=0)
    out[...] = lax.dot_general(columns, cots, CONTRACT_ROWS, preferred_element_type=jnp.float32).astype(out.dtype)


def add_kernel(total, arrived, out):
    @pl.loop(0, out.shape[0] // CHUNK)
    def _(step):
        at = pl.ds(pl.multiple_of(step * CHUNK, CHUNK), CHUNK)
        out[at, :] = (total[at, :] + arrived[at, :].astype(jnp.float32)).astype(out.dtype)


def gradient_at(at, refs):
    total, beside, far = refs
    return total[at, :] + beside[at, :].astype(jnp.float32) + far[at, :].astype(jnp.float32)


def steps(half, which, body):
    @pl.loop(0, half // CHUNK)
    def _(step):
        start = pl.multiple_of(step * CHUNK, CHUNK)
        body(pl.ds(start, CHUNK), pl.ds(pl.multiple_of(which * half + start, CHUNK), CHUNK))


def drift_kernel(*refs):
    gradient_refs, (weights, first, second, anchor), drift_ref = refs[:3], refs[3:7], refs[7]

    def body(here, at):
        gradient = gradient_at(at, gradient_refs)
        state = (weights[at, :], first[at, :], second[at, :], anchor[at, :])
        drift_ref[here, :] = inner_update(gradient, *state)[1]

    steps(drift_ref.shape[0], 1 - lax.axis_index("rep"), body)


def update_kernel(*refs):
    gradient_refs, (weights, first, second, anchor), (first_ref, drift_ref) = refs[:3], refs[3:7], refs[7:]
    half = drift_ref.shape[0]
    r = lax.axis_index("rep")

    def body(here, at):
        gradient = gradient_at(at, gradient_refs)
        state = (weights[at, :], first[at, :], second[at, :], anchor[at, :])
        first_ref[at, :], drift_ref[here, :] = inner_update(gradient, *state)

    def others(here, at):
        first_ref[at, :] = decay_first * first[at, :] + (1.0 - decay_first) * gradient_at(at, gradient_refs)

    steps(half, r, body)
    steps(half, 1 - r, others)


def outer_kernel(drift, other, anchor, momentum, out):
    half = out.shape[0]
    at = pl.ds(pl.multiple_of(lax.axis_index("rep") * half, half), half)
    out[...] = outer_update((drift[...] + other[...]) / 2, anchor[at, :], momentum[at, :])


def product(messages, rows, pieces):
    r = lax.axis_index("rep")
    half = rows // 2
    total = 0.0
    for (blocks, start), (mine, other) in zip(messages, pieces):
        for which, piece in ((r, mine), (1 - r, other)):
            at = pl.ds(pl.multiple_of(start + which * half, half), half)
            columns = jnp.concatenate([block[:, at] for block in blocks], axis=0)
            total += jnp.dot(columns, piece[...], preferred_element_type=jnp.float32)
    return total


def paired(refs):
    return [(refs[2 * n], refs[2 * n + 1]) for n in range(len(refs) // 2)]


def early_values_kernel(inner, rows, *refs):
    own, both = refs[:inner], refs[inner : 2 * inner]
    refs[-1][...] = product([(own, 0), (both, rows), (both, 0)], rows, paired(refs[2 * inner : -1]))


def late_values_kernel(inner, rows, early, *refs):
    tokens = early.shape[0] // inner
    total = early[...] + product([(refs[:inner], 0)], rows, [refs[inner : inner + 2]])
    for k, out in enumerate(refs[inner + 2 :]):
        out[...] = total[k * tokens : (k + 1) * tokens].astype(out.dtype)


def sum_kernel(*refs):
    total = refs[0][...]
    for ref in refs[1:-1]:
        total += ref[...].astype(jnp.float32)
    refs[-1][...] = total.astype(refs[-1].dtype)


def on_device(acts, value_cots, inner_weights, first_moment, second_moment, anchor, outer_momentum):
    inner = lax.axis_size("fsdp") // PLANES
    rows, width = anchor.shape
    if inner != 4 or lax.axis_size("rep") != 2 or rows % 256 or width % 128:
        return general(acts, value_cots, inner_weights, first_moment, second_moment, anchor, outer_momentum)
    tokens = acts.shape[1]
    half = rows // 2

    def planes(x, bits):
        return lax.ppermute(x, "fsdp", [(p * inner + i, (p ^ bits) * inner + i) for p in range(PLANES) for i in range(inner)])

    def across(x, k):
        return lax.ppermute(x, "fsdp", [(p * inner + i, p * inner + (i ^ k)) for p in range(PLANES) for i in range(inner)])

    def around(blocks):
        return [blocks[0]] + [across(blocks[k], k) for k in range(1, inner)]

    def swap(x):
        return lax.ppermute(x, "rep", [(0, 1), (1, 0)])

    out = [jax.ShapeDtypeStruct((tokens, rows + width), jnp.bfloat16)] * inner
    sems = [pltpu.SemaphoreType.DMA((2 * inner,))]
    kernel = partial(pack_first_kernel, inner, rows)
    first = around(call(kernel, "pack", out, [acts[0], value_cots[0]], 0, sems, space=pltpu.HBM))

    def pack(blocks, after):
        out = [jax.ShapeDtypeStruct((tokens, len(blocks) * rows), jnp.bfloat16)] * inner
        return call(partial(pack_kernel, inner, rows, blocks), "pack", out, [acts[0]], 0, after=after)

    second = around(pack((2, 1), first[1:2]))
    last = around(pack((0,), second[1:]))
    full = jax.ShapeDtypeStruct((rows, width), jnp.float32)
    sent = jax.ShapeDtypeStruct((rows, width), jnp.bfloat16)

    def gradient(message, at, out, flops=2 * inner * tokens * rows * width, after=()):
        return call(partial(gradient_kernel, inner, rows, at), "gradient", [out], message + first, flops, after=after)[0]

    beside_far = planes(gradient(first, 0, sent), 1)
    for_far = gradient(second, 0, full, AHEAD_FLOPS)
    (for_far,) = call(add_kernel, "add", [sent], [for_far, beside_far], 0)
    far = planes(for_far, 2)
    beside = planes(gradient(second, rows, sent, AHEAD_FLOPS // 6, [for_far]), 1)
    known = [gradient(last, 0, full), beside, far, inner_weights[0], first_moment[0], second_moment[0], anchor]
    half_block = jax.ShapeDtypeStruct((half, width), jnp.float32)
    (drift_out,) = call(drift_kernel, "drift", [half_block], known, 0)
    drift_in = swap(drift_out)
    first_next, drift = call(update_kernel, "update", [full, half_block], known, 0)
    new_half = jax.ShapeDtypeStruct((half, width), jnp.bfloat16)
    (mine,) = call(outer_kernel, "outer", [new_half], [drift, drift_in, anchor, outer_momentum], 0)
    mine2 = planes(mine, 2)
    mine1 = planes(mine, 1)
    mine3 = planes(mine2, 1)
    pieces = [y for x in (mine, mine1, mine2) for y in (x, swap(x))]
    flops = 2 * inner * tokens * rows * width
    (early,) = call(
        partial(early_values_kernel, inner, rows),
        "early_values",
        [jax.ShapeDtypeStruct((inner * tokens, width), jnp.float32)],
        last + second + pieces,
        3 * flops,
    )
    block = jax.ShapeDtypeStruct((tokens, width), jnp.bfloat16)
    own, *sums = call(
        partial(late_values_kernel, inner, rows),
        "late_values",
        [jax.ShapeDtypeStruct((tokens, width), jnp.float32)] + [block] * (inner - 1),
        [early] + first + [mine3, swap(mine3)],
        flops,
    )
    terms = [own] + [across(sums[k - 1], k) for k in range(1, inner)]
    (values,) = call(sum_kernel, "sum", [block], terms, 0)
    return (first_next[None], values[None])


def solution(mesh):
    placed = (
        P("rep", "fsdp", None),
        P("rep", "fsdp", None),
        P("rep", "fsdp", None),
        P("rep", "fsdp", None),
        P("rep", "fsdp", None),
        P("fsdp", None),
        P("fsdp", None),
    )
    return jax.shard_map(
        on_device,
        mesh=mesh,
        in_specs=placed,
        out_specs=(P("rep", "fsdp", None), P("rep", "fsdp", None)),
        check_vma=False,
    )
```

```python
from functools import partial

import jax
import jax.numpy as jnp
from jax import lax
from jax.experimental import pallas as pl
from jax.experimental.pallas import tpu as pltpu
from jax.sharding import PartitionSpec as P

decay_first = 0.9
decay_second = 0.95
inner_rate = 0.006
epsilon = 1e-08
outer_rate = 0.7
outer_decay = 0.9

PLANES = 4
CHUNK = 32
CONTRACT_ROWS = (((0,), (0,)), ((), ()))
AHEAD_FLOPS = 12 * 10**12
VMEM_BYTES = 16 * 1024 * 1024


def outer_update(average, anchor_rows, momentum_rows):
    velocity = outer_decay * momentum_rows + average
    return (anchor_rows - outer_rate * (average + outer_decay * velocity)).astype(jnp.bfloat16)


def inner_update(gradient, inner_weights, first_moment, second_moment, anchor):
    first_next = decay_first * first_moment + (1.0 - decay_first) * gradient
    second_next = decay_second * second_moment + (1.0 - decay_second) * gradient * gradient
    stepped = inner_weights - inner_rate * first_next / (jnp.sqrt(second_next) + epsilon)
    return first_next, anchor - stepped


def general(acts, value_cots, inner_weights, first_moment, second_moment, anchor, outer_momentum):
    tokens_local = acts[0]
    columns = lax.all_to_all(tokens_local, "fsdp", split_axis=1, concat_axis=0, tiled=True)
    cots = lax.all_gather(value_cots[0], "fsdp", axis=0, tiled=True)
    gradient = lax.dot_general(columns, cots, CONTRACT_ROWS, preferred_element_type=jnp.float32)
    first_next, drift = inner_update(gradient, inner_weights[0], first_moment[0], second_moment[0], anchor)
    average = lax.psum(drift, "rep") / lax.axis_size("rep")
    weights_next = outer_update(average, anchor, outer_momentum)
    gathered = lax.all_gather(weights_next, "fsdp", axis=0, tiled=True)
    values = jnp.dot(tokens_local, gathered, preferred_element_type=jnp.float32)
    return (first_next[None], values.astype(jnp.bfloat16)[None])


def flip(at, bits):
    low = lax.rem(at, 2)
    return (at // 2 + bits // 2 - 2 * (at // 2) * (bits // 2)) * 2 + low + bits % 2 - 2 * low * (bits % 2)


def call(kernel, name, out, inputs, flops, scratch=(), after=(), space=pltpu.VMEM):
    moved = sum(x.size * x.dtype.itemsize for x in list(inputs) + list(out))
    count = len(inputs)

    def without_after(*refs):
        kernel(*refs[:count], *refs[count + len(after) :])

    return pl.pallas_call(
        without_after,
        out_shape=out,
        in_specs=[pl.BlockSpec(memory_space=space)] * count + [pl.BlockSpec(memory_space=pl.ANY)] * len(after),
        out_specs=[pl.BlockSpec(memory_space=pltpu.VMEM)] * len(out),
        scratch_shapes=list(scratch),
        compiler_params=pltpu.CompilerParams(vmem_limit_bytes=VMEM_BYTES),
        cost_estimate=pl.CostEstimate(flops=flops, bytes_accessed=moved, transcendentals=0),
        name=name,
    )(*inputs, *after)


def block_start(inner, rows, bits, k):
    f = lax.axis_index("fsdp")
    return pl.multiple_of((flip(f // inner, bits) * inner + flip(lax.rem(f, inner), k)) * rows, rows)


def pack_first_kernel(inner, rows, acts_ref, cots_ref, *refs):
    outs, sems = refs[:inner], refs[inner]
    copies = []
    for k in range(inner):
        block = acts_ref.at[:, pl.ds(block_start(inner, rows, 3, k), rows)]
        copies.append(pltpu.make_async_copy(block, outs[k].at[:, :rows], sems.at[2 * k]))
        copies.append(pltpu.make_async_copy(cots_ref, outs[k].at[:, rows:], sems.at[2 * k + 1]))
    for copy in copies:
        copy.start()
    for copy in copies:
        copy.wait()


def pack_kernel(inner, rows, blocks, acts_ref, *outs):
    for k in range(inner):
        for slot, bits in enumerate(blocks):
            outs[k][:, slot * rows : (slot + 1) * rows] = acts_ref[:, pl.ds(block_start(inner, rows, bits, k), rows)]


def partial_gradient(inner, rows, acts_at, acts_refs, cots_refs):
    columns = jnp.concatenate([ref[:, acts_at : acts_at + rows] for ref in acts_refs], axis=0)
    cots = jnp.concatenate([ref[:, rows:] for ref in cots_refs], axis=0)
    return lax.dot_general(columns, cots, CONTRACT_ROWS, preferred_element_type=jnp.float32)


def gradient_kernel(inner, rows, acts_at, *refs):
    total = partial_gradient(inner, rows, acts_at, refs[:inner], refs[inner : 2 * inner])
    at = 0
    for out in refs[2 * inner :]:
        out[...] = total[:, at : at + out.shape[1]].astype(out.dtype)
        at += out.shape[1]


def add_kernel(start, total, arrived, out):
    @pl.loop(0, out.shape[0] // CHUNK)
    def _(step):
        at = pl.ds(pl.multiple_of(step * CHUNK, CHUNK), CHUNK)
        here = total[at, start : start + out.shape[1]]
        out[at, :] = (here + arrived[at, :].astype(jnp.float32)).astype(out.dtype)


def gradient_at(at, refs):
    total, *arrived = refs
    beside, far = (
        jnp.concatenate([ref[at, :].astype(jnp.float32) for ref in pair], axis=1) for pair in (arrived[:2], arrived[2:])
    )
    return total[at, :] + beside + far


def steps(half, which, body):
    @pl.loop(0, half // CHUNK)
    def _(step):
        start = pl.multiple_of(step * CHUNK, CHUNK)
        body(pl.ds(start, CHUNK), pl.ds(pl.multiple_of(which * half + start, CHUNK), CHUNK))


def drift_kernel(*refs):
    gradient_refs, (weights, first, second, anchor), drift_ref = refs[:-5], refs[-5:-1], refs[-1]

    def body(here, at):
        gradient = gradient_at(at, gradient_refs)
        state = (weights[at, :], first[at, :], second[at, :], anchor[at, :])
        drift_ref[here, :] = inner_update(gradient, *state)[1]

    steps(drift_ref.shape[0], 1 - lax.axis_index("rep"), body)


def update_kernel(*refs):
    gradient_refs, (weights, first, second, anchor), (first_ref, drift_ref) = refs[:-6], refs[-6:-2], refs[-2:]
    half = drift_ref.shape[0]
    r = lax.axis_index("rep")

    def body(here, at):
        gradient = gradient_at(at, gradient_refs)
        state = (weights[at, :], first[at, :], second[at, :], anchor[at, :])
        first_ref[at, :], drift_ref[here, :] = inner_update(gradient, *state)

    def others(here, at):
        first_ref[at, :] = decay_first * first[at, :] + (1.0 - decay_first) * gradient_at(at, gradient_refs)

    steps(half, r, body)
    steps(half, 1 - r, others)


def outer_kernel(drift, other, anchor, momentum, out, *cut):
    half = out.shape[0]
    at = pl.ds(pl.multiple_of(lax.axis_index("rep") * half, half), half)
    out[...] = outer_update((drift[...] + other[...]) / 2, anchor[at, :], momentum[at, :])
    start = 0
    for ref in cut:
        ref[...] = out[:, start : start + ref.shape[1]]
        start += ref.shape[1]


def product(messages, rows, pieces):
    r = lax.axis_index("rep")
    half = rows // 2
    total = 0.0
    for (blocks, start), (mine, other) in zip(messages, pieces):
        for which, piece in ((r, mine), (1 - r, other)):
            at = pl.ds(pl.multiple_of(start + which * half, half), half)
            columns = jnp.concatenate([block[:, at] for block in blocks], axis=0)
            total += jnp.dot(columns, piece[...], preferred_element_type=jnp.float32)
    return total


def paired(refs):
    return [(refs[2 * n], refs[2 * n + 1]) for n in range(len(refs) // 2)]


def early_values_kernel(inner, rows, *refs):
    own, both, pieces, out = refs[:inner], refs[inner : 2 * inner], paired(refs[2 * inner : -1]), refs[-1]
    far = [product([(both, 0)], rows, [piece]) for piece in pieces[2:]]
    out[...] = product([(own, 0), (both, rows)], rows, pieces[:2]) + jnp.concatenate(far, axis=1)


def late_values_kernel(inner, rows, early, *refs):
    blocks, pieces, outs = refs[:inner], paired(refs[inner : inner + 4]), refs[inner + 4 :]
    tokens = early.shape[0] // inner
    start = 0
    for piece in pieces:
        cols = slice(start, start + piece[0].shape[1])
        total = early[:, cols] + product([(blocks, 0)], rows, [piece])
        for k, out in enumerate(outs):
            out[:, cols] = total[k * tokens : (k + 1) * tokens].astype(out.dtype)
        start = cols.stop


def sum_kernel(*refs):
    total = refs[0][...]
    for ref in refs[1:-1]:
        total += ref[...].astype(jnp.float32)
    refs[-1][...] = total.astype(refs[-1].dtype)


def on_device(acts, value_cots, inner_weights, first_moment, second_moment, anchor, outer_momentum):
    inner = lax.axis_size("fsdp") // PLANES
    rows, width = anchor.shape
    if inner != 4 or lax.axis_size("rep") != 2 or rows % 256 or width % 512:
        return general(acts, value_cots, inner_weights, first_moment, second_moment, anchor, outer_momentum)
    tokens = acts.shape[1]
    half = rows // 2

    def planes(x, bits):
        return lax.ppermute(x, "fsdp", [(p * inner + i, (p ^ bits) * inner + i) for p in range(PLANES) for i in range(inner)])

    def across(x, k):
        return lax.ppermute(x, "fsdp", [(p * inner + i, p * inner + (i ^ k)) for p in range(PLANES) for i in range(inner)])

    def around(blocks):
        return [blocks[0]] + [across(blocks[k], k) for k in range(1, inner)]

    def swap(x):
        return lax.ppermute(x, "rep", [(0, 1), (1, 0)])

    out = [jax.ShapeDtypeStruct((tokens, rows + width), jnp.bfloat16)] * inner
    sems = [pltpu.SemaphoreType.DMA((2 * inner,))]
    kernel = partial(pack_first_kernel, inner, rows)
    first = around(call(kernel, "pack", out, [acts[0], value_cots[0]], 0, sems, space=pltpu.HBM))

    def pack(blocks, after):
        out = [jax.ShapeDtypeStruct((tokens, len(blocks) * rows), jnp.bfloat16)] * inner
        return call(partial(pack_kernel, inner, rows, blocks), "pack", out, [acts[0]], 0, after=after)

    second = around(pack((2, 1), first[1:2]))
    full = jax.ShapeDtypeStruct((rows, width), jnp.float32)
    sent = jax.ShapeDtypeStruct((rows, width), jnp.bfloat16)
    cut = [jax.ShapeDtypeStruct((rows, columns), jnp.bfloat16) for columns in (3 * width // 4, width // 4)]
    equal = [jax.ShapeDtypeStruct((rows, width // 2), jnp.bfloat16)] * 2

    def gradient(message, at, out, flops=2 * inner * tokens * rows * width, after=()):
        return call(partial(gradient_kernel, inner, rows, at), "gradient", out, message + first, flops, after=after)

    beside_far = [planes(x, 1) for x in gradient(first, 0, cut)]
    (for_far,) = gradient(second, 0, [full], AHEAD_FLOPS)
    far, start = [], 0
    for out, arrived in zip(cut, beside_far):
        (added,) = call(partial(add_kernel, start), "add", [out], [for_far, arrived], 0)
        far.append(planes(added, 2))
        if start == 0:
            for_beside = gradient(second, rows, equal, after=[added])
            beside = [planes(x, 1) for x in for_beside]
        start += out.shape[1]
    last = around(pack((0,), [added, *for_beside]))
    known = [gradient(last, 0, [full])[0], *beside, *far, inner_weights[0], first_moment[0], second_moment[0], anchor]
    half_block = jax.ShapeDtypeStruct((half, width), jnp.float32)
    (drift_out,) = call(drift_kernel, "drift", [half_block], known, 0)
    drift_in = swap(drift_out)
    first_next, drift = call(update_kernel, "update", [full, half_block], known, 0)
    new_half = jax.ShapeDtypeStruct((half, width), jnp.bfloat16)
    new_cut = [jax.ShapeDtypeStruct((half, width // 2), jnp.bfloat16)] * 2
    mine, *mine_cut = call(outer_kernel, "outer", [new_half] + new_cut, [drift, drift_in, anchor, outer_momentum], 0)
    mine2 = [planes(x, 2) for x in mine_cut]
    mine1 = planes(mine, 1)
    mine3 = [planes(x, 1) for x in mine2]
    pieces = [y for x in (mine, mine1, *mine2) for y in (x, swap(x))]
    flops = 2 * inner * tokens * rows * width
    (early,) = call(
        partial(early_values_kernel, inner, rows),
        "early_values",
        [jax.ShapeDtypeStruct((inner * tokens, width), jnp.float32)],
        last + second + pieces,
        3 * flops,
    )
    block = jax.ShapeDtypeStruct((tokens, width), jnp.bfloat16)
    own, *sums = call(
        partial(late_values_kernel, inner, rows),
        "late_values",
        [jax.ShapeDtypeStruct((tokens, width), jnp.float32)] + [block] * (inner - 1),
        [early] + first + [y for x in mine3 for y in (x, swap(x))],
        flops,
    )
    terms = [own] + [across(sums[k - 1], k) for k in range(1, inner)]
    (values,) = call(sum_kernel, "sum", [block], terms, 0)
    return (first_next[None], values[None])


def solution(mesh):
    placed = (
        P("rep", "fsdp", None),
        P("rep", "fsdp", None),
        P("rep", "fsdp", None),
        P("rep", "fsdp", None),
        P("rep", "fsdp", None),
        P("fsdp", None),
        P("fsdp", None),
    )
    return jax.shard_map(
        on_device,
        mesh=mesh,
        in_specs=placed,
        out_specs=(P("rep", "fsdp", None), P("rep", "fsdp", None)),
        check_vma=False,
    )
```

```python
from functools import partial

import jax
import jax.numpy as jnp
from jax import lax
from jax.experimental import pallas as pl
from jax.experimental.pallas import tpu as pltpu
from jax.sharding import PartitionSpec as P

decay_first = 0.9
decay_second = 0.95
inner_rate = 0.006
epsilon = 1e-08
outer_rate = 0.7
outer_decay = 0.9

PLANES = 4
CHUNK = 32
CONTRACT_ROWS = (((0,), (0,)), ((), ()))
AHEAD_FLOPS = 2 * 10**12
LAST_FLOPS = 5 * 10**11
VMEM_BYTES = 16 * 1024 * 1024


def outer_update(average, anchor_rows, momentum_rows):
    velocity = outer_decay * momentum_rows + average
    return (anchor_rows - outer_rate * (average + outer_decay * velocity)).astype(jnp.bfloat16)


def inner_update(gradient, inner_weights, first_moment, second_moment, anchor):
    first_next = decay_first * first_moment + (1.0 - decay_first) * gradient
    second_next = decay_second * second_moment + (1.0 - decay_second) * gradient * gradient
    stepped = inner_weights - inner_rate * first_next / (jnp.sqrt(second_next) + epsilon)
    return first_next, anchor - stepped


def general(acts, value_cots, inner_weights, first_moment, second_moment, anchor, outer_momentum):
    tokens_local = acts[0]
    columns = lax.all_to_all(tokens_local, "fsdp", split_axis=1, concat_axis=0, tiled=True)
    cots = lax.all_gather(value_cots[0], "fsdp", axis=0, tiled=True)
    gradient = lax.dot_general(columns, cots, CONTRACT_ROWS, preferred_element_type=jnp.float32)
    first_next, drift = inner_update(gradient, inner_weights[0], first_moment[0], second_moment[0], anchor)
    average = lax.psum(drift, "rep") / lax.axis_size("rep")
    weights_next = outer_update(average, anchor, outer_momentum)
    gathered = lax.all_gather(weights_next, "fsdp", axis=0, tiled=True)
    values = jnp.dot(tokens_local, gathered, preferred_element_type=jnp.float32)
    return (first_next[None], values.astype(jnp.bfloat16)[None])


def flip(at, bits):
    low = lax.rem(at, 2)
    return (at // 2 + bits // 2 - 2 * (at // 2) * (bits // 2)) * 2 + low + bits % 2 - 2 * low * (bits % 2)


def call(kernel, name, out, inputs, flops, scratch=(), after=(), space=pltpu.VMEM):
    moved = sum(x.size * x.dtype.itemsize for x in list(inputs) + list(out))
    count = len(inputs)

    def without_after(*refs):
        kernel(*refs[:count], *refs[count + len(after) :])

    return pl.pallas_call(
        without_after,
        out_shape=out,
        in_specs=[pl.BlockSpec(memory_space=space)] * count + [pl.BlockSpec(memory_space=pl.ANY)] * len(after),
        out_specs=[pl.BlockSpec(memory_space=pltpu.VMEM)] * len(out),
        scratch_shapes=list(scratch),
        compiler_params=pltpu.CompilerParams(vmem_limit_bytes=VMEM_BYTES),
        cost_estimate=pl.CostEstimate(flops=flops, bytes_accessed=moved, transcendentals=0),
        name=name,
    )(*inputs, *after)


def block_start(inner, rows, bits, k):
    f = lax.axis_index("fsdp")
    return pl.multiple_of((flip(f // inner, bits) * inner + flip(lax.rem(f, inner), k)) * rows, rows)


def pack_first_kernel(inner, rows, acts_ref, cots_ref, *refs):
    outs, sems = refs[:inner], refs[inner]
    copies = []
    for k in range(inner):
        block = acts_ref.at[:, pl.ds(block_start(inner, rows, 3, k), rows)]
        copies.append(pltpu.make_async_copy(block, outs[k].at[:, :rows], sems.at[2 * k]))
        copies.append(pltpu.make_async_copy(cots_ref, outs[k].at[:, rows:], sems.at[2 * k + 1]))
    for copy in copies:
        copy.start()
    for copy in copies:
        copy.wait()


def pack_kernel(inner, rows, blocks, acts_ref, *outs):
    for k in range(inner):
        for slot, bits in enumerate(blocks):
            outs[k][:, slot * rows : (slot + 1) * rows] = acts_ref[:, pl.ds(block_start(inner, rows, bits, k), rows)]


def partial_gradient(inner, rows, acts_at, acts_refs, cots_refs):
    columns = jnp.concatenate([ref[:, acts_at : acts_at + rows] for ref in acts_refs], axis=0)
    cots = jnp.concatenate([ref[:, rows:] for ref in cots_refs], axis=0)
    return lax.dot_general(columns, cots, CONTRACT_ROWS, preferred_element_type=jnp.float32)


def gradient_kernel(inner, rows, acts_at, *refs):
    total = partial_gradient(inner, rows, acts_at, refs[:inner], refs[inner : 2 * inner])
    at = 0
    for out in refs[2 * inner :]:
        out[...] = total[:, at : at + out.shape[1]].astype(out.dtype)
        at += out.shape[1]


def add_kernel(total, arrived, out):
    @pl.loop(0, out.shape[0] // CHUNK)
    def _(step):
        at = pl.ds(pl.multiple_of(step * CHUNK, CHUNK), CHUNK)
        out[at, :] = (total[at, :] + arrived[at, :].astype(jnp.float32)).astype(out.dtype)


def gradient_at(at, refs):
    total = refs[0][at, :]
    beside, far_left, far_right, straight = (ref[at, :].astype(jnp.float32) for ref in refs[1:])
    return total + beside + jnp.concatenate([far_left + straight, far_right], axis=1)


def steps(half, which, body):
    @pl.loop(0, half // CHUNK)
    def _(step):
        start = pl.multiple_of(step * CHUNK, CHUNK)
        body(pl.ds(start, CHUNK), pl.ds(pl.multiple_of(which * half + start, CHUNK), CHUNK))


def drift_kernel(*refs):
    gradient_refs, (weights, first, second, anchor), drift_ref = refs[:-5], refs[-5:-1], refs[-1]

    def body(here, at):
        gradient = gradient_at(at, gradient_refs)
        state = (weights[at, :], first[at, :], second[at, :], anchor[at, :])
        drift_ref[here, :] = inner_update(gradient, *state)[1]

    steps(drift_ref.shape[0], 1 - lax.axis_index("rep"), body)


def update_kernel(*refs):
    gradient_refs, (weights, first, second, anchor), (first_ref, drift_ref) = refs[:-6], refs[-6:-2], refs[-2:]
    half = drift_ref.shape[0]
    r = lax.axis_index("rep")

    def body(here, at):
        gradient = gradient_at(at, gradient_refs)
        state = (weights[at, :], first[at, :], second[at, :], anchor[at, :])
        first_ref[at, :], drift_ref[here, :] = inner_update(gradient, *state)

    def others(here, at):
        first_ref[at, :] = decay_first * first[at, :] + (1.0 - decay_first) * gradient_at(at, gradient_refs)

    steps(half, r, body)
    steps(half, 1 - r, others)


def outer_kernel(drift, other, anchor, momentum, out):
    half = out.shape[0]
    at = pl.ds(pl.multiple_of(lax.axis_index("rep") * half, half), half)
    out[...] = outer_update((drift[...] + other[...]) / 2, anchor[at, :], momentum[at, :])


def product(messages, rows, pieces):
    r = lax.axis_index("rep")
    half = rows // 2
    total = 0.0
    for (blocks, start), (mine, other) in zip(messages, pieces):
        for which, piece in ((r, mine), (1 - r, other)):
            at = pl.ds(pl.multiple_of(start + which * half, half), half)
            columns = jnp.concatenate([block[:, at] for block in blocks], axis=0)
            total += jnp.dot(columns, piece[...], preferred_element_type=jnp.float32)
    return total


def paired(refs):
    return [(refs[2 * n], refs[2 * n + 1]) for n in range(len(refs) // 2)]


def early_values_kernel(inner, rows, *refs):
    own, both = refs[:inner], refs[inner : 2 * inner]
    refs[-1][...] = product([(own, 0), (both, rows), (both, 0)], rows, paired(refs[2 * inner : -1]))


def late_values_kernel(inner, rows, early, *refs):
    tokens = early.shape[0] // inner
    total = early[...] + product([(refs[:inner], 0)], rows, [refs[inner : inner + 2]])
    for k, out in enumerate(refs[inner + 2 :]):
        out[...] = total[k * tokens : (k + 1) * tokens].astype(out.dtype)


def sum_kernel(*refs):
    total = refs[0][...]
    for ref in refs[1:-1]:
        total += ref[...].astype(jnp.float32)
    refs[-1][...] = total.astype(refs[-1].dtype)


def on_device(acts, value_cots, inner_weights, first_moment, second_moment, anchor, outer_momentum):
    inner = lax.axis_size("fsdp") // PLANES
    rows, width = anchor.shape
    if inner != 4 or lax.axis_size("rep") != 2 or rows % 256 or width % 512:
        return general(acts, value_cots, inner_weights, first_moment, second_moment, anchor, outer_momentum)
    tokens = acts.shape[1]
    half = rows // 2

    def planes(x, bits):
        return lax.ppermute(x, "fsdp", [(p * inner + i, (p ^ bits) * inner + i) for p in range(PLANES) for i in range(inner)])

    def across(x, k):
        return lax.ppermute(x, "fsdp", [(p * inner + i, p * inner + (i ^ k)) for p in range(PLANES) for i in range(inner)])

    def around(blocks):
        return [blocks[0]] + [across(blocks[k], k) for k in range(1, inner)]

    def swap(x):
        return lax.ppermute(x, "rep", [(0, 1), (1, 0)])

    out = [jax.ShapeDtypeStruct((tokens, rows + width), jnp.bfloat16)] * inner
    sems = [pltpu.SemaphoreType.DMA((2 * inner,))]
    kernel = partial(pack_first_kernel, inner, rows)
    first = around(call(kernel, "pack", out, [acts[0], value_cots[0]], 0, sems, space=pltpu.HBM))

    def pack(blocks, after, flops=0):
        out = [jax.ShapeDtypeStruct((tokens, len(blocks) * rows), jnp.bfloat16)] * inner
        return call(partial(pack_kernel, inner, rows, blocks), "pack", out, [acts[0]], flops, after=after)

    second = around(pack((2, 1), first[1:2]))
    full = jax.ShapeDtypeStruct((rows, width), jnp.float32)
    sent = jax.ShapeDtypeStruct((rows, width), jnp.bfloat16)
    piece = jax.ShapeDtypeStruct((rows, width // 2), jnp.bfloat16)
    kept = jax.ShapeDtypeStruct((rows, width // 2), jnp.float32)

    def gradient(message, at, out, flops=2 * inner * tokens * rows * width, after=()):
        return call(partial(gradient_kernel, inner, rows, at), "gradient", out, message + first, flops, after=after)

    straight, beside_far = gradient(first, 0, [piece] * 2)
    straight, beside_far = planes(straight, 3), planes(beside_far, 1)
    for_far, to_add = gradient(second, 0, [piece, kept])
    (added,) = call(add_kernel, "add", [piece], [to_add, beside_far], AHEAD_FLOPS, after=[straight])
    far = [planes(for_far, 2), planes(added, 2)]
    (for_beside,) = gradient(second, rows, [sent], after=[added])
    last = around(pack((0,), [far[0], for_beside], LAST_FLOPS))
    known = [gradient(last, 0, [full])[0], planes(for_beside, 1), *far, straight]
    known += [inner_weights[0], first_moment[0], second_moment[0], anchor]
    half_block = jax.ShapeDtypeStruct((half, width), jnp.float32)
    (drift_out,) = call(drift_kernel, "drift", [half_block], known, 0)
    drift_in = swap(drift_out)
    first_next, drift = call(update_kernel, "update", [full, half_block], known, 0)
    new_half = jax.ShapeDtypeStruct((half, width), jnp.bfloat16)
    (mine,) = call(outer_kernel, "outer", [new_half], [drift, drift_in, anchor, outer_momentum], 0)
    mine2 = planes(mine, 2)
    mine1 = planes(mine, 1)
    mine3 = planes(mine2, 1)
    pieces = [y for x in (mine, mine1, mine2) for y in (x, swap(x))]
    flops = 2 * inner * tokens * rows * width
    (early,) = call(
        partial(early_values_kernel, inner, rows),
        "early_values",
        [jax.ShapeDtypeStruct((inner * tokens, width), jnp.float32)],
        last + second + pieces,
        3 * flops,
    )
    block = jax.ShapeDtypeStruct((tokens, width), jnp.bfloat16)
    own, *sums = call(
        partial(late_values_kernel, inner, rows),
        "late_values",
        [jax.ShapeDtypeStruct((tokens, width), jnp.float32)] + [block] * (inner - 1),
        [early] + first + [mine3, swap(mine3)],
        flops,
    )
    terms = [own] + [across(sums[k - 1], k) for k in range(1, inner)]
    (values,) = call(sum_kernel, "sum", [block], terms, 0)
    return (first_next[None], values[None])


def solution(mesh):
    placed = (
        P("rep", "fsdp", None),
        P("rep", "fsdp", None),
        P("rep", "fsdp", None),
        P("rep", "fsdp", None),
        P("rep", "fsdp", None),
        P("fsdp", None),
        P("fsdp", None),
    )
    return jax.shard_map(
        on_device,
        mesh=mesh,
        in_specs=placed,
        out_specs=(P("rep", "fsdp", None), P("rep", "fsdp", None)),
        check_vma=False,
    )
```

```python
from functools import partial

import jax
import jax.numpy as jnp
from jax import lax
from jax.experimental import pallas as pl
from jax.experimental.pallas import tpu as pltpu
from jax.sharding import PartitionSpec as P

decay_first = 0.9
decay_second = 0.95
inner_rate = 0.006
epsilon = 1e-08
outer_rate = 0.7
outer_decay = 0.9

PLANES = 4
CHUNK = 32
CONTRACT_ROWS = (((0,), (0,)), ((), ()))
AHEAD_FLOPS = 10**12
VMEM_BYTES = 16 * 1024 * 1024


def outer_update(average, anchor_rows, momentum_rows):
    velocity = outer_decay * momentum_rows + average
    return (anchor_rows - outer_rate * (average + outer_decay * velocity)).astype(jnp.bfloat16)


def inner_update(gradient, inner_weights, first_moment, second_moment, anchor):
    first_next = decay_first * first_moment + (1.0 - decay_first) * gradient
    second_next = decay_second * second_moment + (1.0 - decay_second) * gradient * gradient
    stepped = inner_weights - inner_rate * first_next / (jnp.sqrt(second_next) + epsilon)
    return first_next, anchor - stepped


def general(acts, value_cots, inner_weights, first_moment, second_moment, anchor, outer_momentum):
    tokens_local = acts[0]
    columns = lax.all_to_all(tokens_local, "fsdp", split_axis=1, concat_axis=0, tiled=True)
    cots = lax.all_gather(value_cots[0], "fsdp", axis=0, tiled=True)
    gradient = lax.dot_general(columns, cots, CONTRACT_ROWS, preferred_element_type=jnp.float32)
    first_next, drift = inner_update(gradient, inner_weights[0], first_moment[0], second_moment[0], anchor)
    average = lax.psum(drift, "rep") / lax.axis_size("rep")
    weights_next = outer_update(average, anchor, outer_momentum)
    gathered = lax.all_gather(weights_next, "fsdp", axis=0, tiled=True)
    values = jnp.dot(tokens_local, gathered, preferred_element_type=jnp.float32)
    return (first_next[None], values.astype(jnp.bfloat16)[None])


def flip(at, bits):
    low = lax.rem(at, 2)
    return (at // 2 + bits // 2 - 2 * (at // 2) * (bits // 2)) * 2 + low + bits % 2 - 2 * low * (bits % 2)


def call(kernel, name, out, inputs, flops, scratch=(), after=(), space=pltpu.VMEM):
    moved = sum(x.size * x.dtype.itemsize for x in list(inputs) + list(out))
    count = len(inputs)

    def without_after(*refs):
        kernel(*refs[:count], *refs[count + len(after) :])

    return pl.pallas_call(
        without_after,
        out_shape=out,
        in_specs=[pl.BlockSpec(memory_space=space)] * count + [pl.BlockSpec(memory_space=pl.ANY)] * len(after),
        out_specs=[pl.BlockSpec(memory_space=pltpu.VMEM)] * len(out),
        scratch_shapes=list(scratch),
        compiler_params=pltpu.CompilerParams(vmem_limit_bytes=VMEM_BYTES),
        cost_estimate=pl.CostEstimate(flops=flops, bytes_accessed=moved, transcendentals=0),
        name=name,
    )(*inputs, *after)


def block_start(inner, rows, bits, k):
    f = lax.axis_index("fsdp")
    return pl.multiple_of((flip(f // inner, bits) * inner + flip(lax.rem(f, inner), k)) * rows, rows)


def pack_first_kernel(inner, rows, acts_ref, cots_ref, *refs):
    outs, sems = refs[:inner], refs[inner]
    copies = []
    for k in range(inner):
        block = acts_ref.at[:, pl.ds(block_start(inner, rows, 3, k), rows)]
        copies.append(pltpu.make_async_copy(block, outs[k].at[:, :rows], sems.at[2 * k]))
        copies.append(pltpu.make_async_copy(cots_ref, outs[k].at[:, rows:], sems.at[2 * k + 1]))
    for copy in copies:
        copy.start()
    for copy in copies:
        copy.wait()


def pack_kernel(inner, rows, blocks, acts_ref, *outs):
    for k in range(inner):
        for slot, bits in enumerate(blocks):
            outs[k][:, slot * rows : (slot + 1) * rows] = acts_ref[:, pl.ds(block_start(inner, rows, bits, k), rows)]


def gradient_kernel(inner, rows, acts_at, *refs):
    acts_refs, cots_refs, arrived, out = refs[:inner], refs[inner : 2 * inner], refs[2 * inner : -1], refs[-1]
    columns = jnp.concatenate([ref[:, acts_at : acts_at + rows] for ref in acts_refs], axis=0)
    cots = jnp.concatenate([ref[:, rows:] for ref in cots_refs], axis=0)
    total = lax.dot_general(columns, cots, CONTRACT_ROWS, preferred_element_type=jnp.float32)
    for ref in arrived:
        total += ref[...].astype(jnp.float32)
    out[...] = total.astype(out.dtype)


def gradient_at(at, refs):
    total, beside, far = refs
    return total[at, :] + beside[at, :].astype(jnp.float32) + far[at, :].astype(jnp.float32)


def steps(half, which, body):
    @pl.loop(0, half // CHUNK)
    def _(step):
        start = pl.multiple_of(step * CHUNK, CHUNK)
        body(pl.ds(start, CHUNK), pl.ds(pl.multiple_of(which * half + start, CHUNK), CHUNK))


def drift_kernel(*refs):
    gradient_refs, (weights, first, second, anchor), drift_ref = refs[:3], refs[3:7], refs[7]

    def body(here, at):
        gradient = gradient_at(at, gradient_refs)
        state = (weights[at, :], first[at, :], second[at, :], anchor[at, :])
        drift_ref[here, :] = inner_update(gradient, *state)[1]

    steps(drift_ref.shape[0], 1 - lax.axis_index("rep"), body)


def update_kernel(*refs):
    gradient_refs, (weights, first, second, anchor), (first_ref, drift_ref) = refs[:3], refs[3:7], refs[7:]
    half = drift_ref.shape[0]
    r = lax.axis_index("rep")

    def body(here, at):
        gradient = gradient_at(at, gradient_refs)
        state = (weights[at, :], first[at, :], second[at, :], anchor[at, :])
        first_ref[at, :], drift_ref[here, :] = inner_update(gradient, *state)

    def others(here, at):
        first_ref[at, :] = decay_first * first[at, :] + (1.0 - decay_first) * gradient_at(at, gradient_refs)

    steps(half, r, body)
    steps(half, 1 - r, others)


def outer_kernel(drift, other, anchor, momentum, out):
    half = out.shape[0]
    at = pl.ds(pl.multiple_of(lax.axis_index("rep") * half, half), half)
    out[...] = outer_update((drift[...] + other[...]) / 2, anchor[at, :], momentum[at, :])


def product(messages, rows, pieces):
    r = lax.axis_index("rep")
    half = rows // 2
    total = 0.0
    for (blocks, start), (mine, other) in zip(messages, pieces):
        for which, piece in ((r, mine), (1 - r, other)):
            at = pl.ds(pl.multiple_of(start + which * half, half), half)
            columns = jnp.concatenate([block[:, at] for block in blocks], axis=0)
            total += jnp.dot(columns, piece[...], preferred_element_type=jnp.float32)
    return total


def paired(refs):
    return [(refs[2 * n], refs[2 * n + 1]) for n in range(len(refs) // 2)]


def early_values_kernel(inner, rows, *refs):
    own, both = refs[:inner], refs[inner : 2 * inner]
    refs[-1][...] = product([(own, 0), (both, rows), (both, 0)], rows, paired(refs[2 * inner : -1]))


def late_values_kernel(inner, rows, early, *refs):
    tokens = early.shape[0] // inner
    total = early[...] + product([(refs[:inner], 0)], rows, [refs[inner : inner + 2]])
    for k, out in enumerate(refs[inner + 2 :]):
        out[...] = total[k * tokens : (k + 1) * tokens].astype(out.dtype)


def sum_kernel(*refs):
    total = refs[0][...]
    for ref in refs[1:-1]:
        total += ref[...].astype(jnp.float32)
    refs[-1][...] = total.astype(refs[-1].dtype)


def on_device(acts, value_cots, inner_weights, first_moment, second_moment, anchor, outer_momentum):
    inner = lax.axis_size("fsdp") // PLANES
    rows, width = anchor.shape
    if inner != 4 or lax.axis_size("rep") != 2 or rows % 256 or width % 128:
        return general(acts, value_cots, inner_weights, first_moment, second_moment, anchor, outer_momentum)
    tokens = acts.shape[1]
    half = rows // 2

    def planes(x, bits):
        return lax.ppermute(x, "fsdp", [(p * inner + i, (p ^ bits) * inner + i) for p in range(PLANES) for i in range(inner)])

    def across(x, k):
        return lax.ppermute(x, "fsdp", [(p * inner + i, p * inner + (i ^ k)) for p in range(PLANES) for i in range(inner)])

    def around(blocks):
        return [blocks[0]] + [across(blocks[k], k) for k in range(1, inner)]

    def swap(x):
        return lax.ppermute(x, "rep", [(0, 1), (1, 0)])

    out = [jax.ShapeDtypeStruct((tokens, rows + width), jnp.bfloat16)] * inner
    sems = [pltpu.SemaphoreType.DMA((2 * inner,))]
    kernel = partial(pack_first_kernel, inner, rows)
    first = around(call(kernel, "pack", out, [acts[0], value_cots[0]], 0, sems, space=pltpu.HBM))

    def pack(blocks, after):
        out = [jax.ShapeDtypeStruct((tokens, len(blocks) * rows), jnp.bfloat16)] * inner
        return call(partial(pack_kernel, inner, rows, blocks), "pack", out, [acts[0]], 0, after=after)

    second = around(pack((2, 1), first[1:2]))
    full = jax.ShapeDtypeStruct((rows, width), jnp.float32)
    sent = jax.ShapeDtypeStruct((rows, width), jnp.bfloat16)

    def gradient(message, at, out, arrived=(), flops=2 * inner * tokens * rows * width):
        kernel = partial(gradient_kernel, inner, rows, at)
        return call(kernel, "gradient", [out], message + first + list(arrived), flops)[0]

    beside_far = planes(gradient(first, 0, sent), 1)
    beside = planes(gradient(second, rows, sent, flops=AHEAD_FLOPS), 1)
    for_far = gradient(second, 0, sent, [beside_far])
    far = planes(for_far, 2)
    last = around(pack((0,), [for_far]))
    known = [gradient(last, 0, full), beside, far, inner_weights[0], first_moment[0], second_moment[0], anchor]
    half_block = jax.ShapeDtypeStruct((half, width), jnp.float32)
    (drift_out,) = call(drift_kernel, "drift", [half_block], known, 0)
    drift_in = swap(drift_out)
    first_next, drift = call(update_kernel, "update", [full, half_block], known, 0)
    new_half = jax.ShapeDtypeStruct((half, width), jnp.bfloat16)
    (mine,) = call(outer_kernel, "outer", [new_half], [drift, drift_in, anchor, outer_momentum], 0)
    mine2 = planes(mine, 2)
    mine1 = planes(mine, 1)
    mine3 = planes(mine2, 1)
    pieces = [y for x in (mine, mine1, mine2) for y in (x, swap(x))]
    flops = 2 * inner * tokens * rows * width
    (early,) = call(
        partial(early_values_kernel, inner, rows),
        "early_values",
        [jax.ShapeDtypeStruct((inner * tokens, width), jnp.float32)],
        last + second + pieces,
        3 * flops,
    )
    block = jax.ShapeDtypeStruct((tokens, width), jnp.bfloat16)
    own, *sums = call(
        partial(late_values_kernel, inner, rows),
        "late_values",
        [jax.ShapeDtypeStruct((tokens, width), jnp.float32)] + [block] * (inner - 1),
        [early] + first + [mine3, swap(mine3)],
        flops,
    )
    terms = [own] + [across(sums[k - 1], k) for k in range(1, inner)]
    (values,) = call(sum_kernel, "sum", [block], terms, 0)
    return (first_next[None], values[None])


def solution(mesh):
    placed = (
        P("rep", "fsdp", None),
        P("rep", "fsdp", None),
        P("rep", "fsdp", None),
        P("rep", "fsdp", None),
        P("rep", "fsdp", None),
        P("fsdp", None),
        P("fsdp", None),
    )
    return jax.shard_map(
        on_device,
        mesh=mesh,
        in_specs=placed,
        out_specs=(P("rep", "fsdp", None), P("rep", "fsdp", None)),
        check_vma=False,
    )
```

```python
from functools import partial

import jax
import jax.numpy as jnp
from jax import lax
from jax.experimental import pallas as pl
from jax.experimental.pallas import tpu as pltpu
from jax.sharding import PartitionSpec as P

decay_first = 0.9
decay_second = 0.95
inner_rate = 0.006
epsilon = 1e-08
outer_rate = 0.7
outer_decay = 0.9

PLANES = 4
CHUNK = 32
CONTRACT_ROWS = (((0,), (0,)), ((), ()))
AHEAD_FLOPS = 10**10
VMEM_BYTES = 16 * 1024 * 1024


def outer_update(average, anchor_rows, momentum_rows):
    velocity = outer_decay * momentum_rows + average
    return (anchor_rows - outer_rate * (average + outer_decay * velocity)).astype(jnp.bfloat16)


def inner_update(gradient, inner_weights, first_moment, second_moment, anchor):
    first_next = decay_first * first_moment + (1.0 - decay_first) * gradient
    second_next = decay_second * second_moment + (1.0 - decay_second) * gradient * gradient
    stepped = inner_weights - inner_rate * first_next / (jnp.sqrt(second_next) + epsilon)
    return first_next, anchor - stepped


def general(acts, value_cots, inner_weights, first_moment, second_moment, anchor, outer_momentum):
    tokens_local = acts[0]
    columns = lax.all_to_all(tokens_local, "fsdp", split_axis=1, concat_axis=0, tiled=True)
    cots = lax.all_gather(value_cots[0], "fsdp", axis=0, tiled=True)
    gradient = lax.dot_general(columns, cots, CONTRACT_ROWS, preferred_element_type=jnp.float32)
    first_next, drift = inner_update(gradient, inner_weights[0], first_moment[0], second_moment[0], anchor)
    average = lax.psum(drift, "rep") / lax.axis_size("rep")
    weights_next = outer_update(average, anchor, outer_momentum)
    gathered = lax.all_gather(weights_next, "fsdp", axis=0, tiled=True)
    values = jnp.dot(tokens_local, gathered, preferred_element_type=jnp.float32)
    return (first_next[None], values.astype(jnp.bfloat16)[None])


def flip(at, bits):
    low = lax.rem(at, 2)
    return (at // 2 + bits // 2 - 2 * (at // 2) * (bits // 2)) * 2 + low + bits % 2 - 2 * low * (bits % 2)


def call(kernel, name, out, inputs, flops, scratch=(), after=(), space=pltpu.VMEM):
    moved = sum(x.size * x.dtype.itemsize for x in list(inputs) + list(out))
    count = len(inputs)

    def without_after(*refs):
        kernel(*refs[:count], *refs[count + len(after) :])

    return pl.pallas_call(
        without_after,
        out_shape=out,
        in_specs=[pl.BlockSpec(memory_space=space)] * count + [pl.BlockSpec(memory_space=pl.ANY)] * len(after),
        out_specs=[pl.BlockSpec(memory_space=pltpu.VMEM)] * len(out),
        scratch_shapes=list(scratch),
        compiler_params=pltpu.CompilerParams(vmem_limit_bytes=VMEM_BYTES),
        cost_estimate=pl.CostEstimate(flops=flops, bytes_accessed=moved, transcendentals=0),
        name=name,
    )(*inputs, *after)


def block_start(inner, rows, bits, k):
    f = lax.axis_index("fsdp")
    return pl.multiple_of((flip(f // inner, bits) * inner + flip(lax.rem(f, inner), k)) * rows, rows)


def pack_first_kernel(inner, rows, acts_ref, cots_ref, *refs):
    outs, sems = refs[:inner], refs[inner]
    copies = []
    for k in range(inner):
        block = acts_ref.at[:, pl.ds(block_start(inner, rows, 3, k), rows)]
        copies.append(pltpu.make_async_copy(block, outs[k].at[:, :rows], sems.at[2 * k]))
        copies.append(pltpu.make_async_copy(cots_ref, outs[k].at[:, rows:], sems.at[2 * k + 1]))
    for copy in copies:
        copy.start()
    for copy in copies:
        copy.wait()


def pack_kernel(inner, rows, blocks, acts_ref, *outs):
    for k in range(inner):
        for slot, bits in enumerate(blocks):
            outs[k][:, slot * rows : (slot + 1) * rows] = acts_ref[:, pl.ds(block_start(inner, rows, bits, k), rows)]


def gradient_kernel(inner, rows, acts_at, *refs):
    acts_refs, cots_refs, arrived, out = refs[:inner], refs[inner : 2 * inner], refs[2 * inner : -1], refs[-1]
    columns = jnp.concatenate([ref[:, acts_at : acts_at + rows] for ref in acts_refs], axis=0)
    cots = jnp.concatenate([ref[:, rows:] for ref in cots_refs], axis=0)
    total = lax.dot_general(columns, cots, CONTRACT_ROWS, preferred_element_type=jnp.float32)
    for ref in arrived:
        total += ref[...].astype(jnp.float32)
    out[...] = total.astype(out.dtype)


def gradient_at(at, refs):
    total, beside, far = refs
    return total[at, :] + beside[at, :].astype(jnp.float32) + far[at, :].astype(jnp.float32)


def steps(half, which, body):
    @pl.loop(0, half // CHUNK)
    def _(step):
        start = pl.multiple_of(step * CHUNK, CHUNK)
        body(pl.ds(start, CHUNK), pl.ds(pl.multiple_of(which * half + start, CHUNK), CHUNK))


def drift_kernel(*refs):
    gradient_refs, (weights, first, second, anchor), drift_ref = refs[:3], refs[3:7], refs[7]

    def body(here, at):
        gradient = gradient_at(at, gradient_refs)
        state = (weights[at, :], first[at, :], second[at, :], anchor[at, :])
        drift_ref[here, :] = inner_update(gradient, *state)[1]

    steps(drift_ref.shape[0], 1 - lax.axis_index("rep"), body)


def update_kernel(*refs):
    gradient_refs, (weights, first, second, anchor), (first_ref, drift_ref) = refs[:3], refs[3:7], refs[7:]
    half = drift_ref.shape[0]
    r = lax.axis_index("rep")

    def body(here, at):
        gradient = gradient_at(at, gradient_refs)
        state = (weights[at, :], first[at, :], second[at, :], anchor[at, :])
        first_ref[at, :], drift_ref[here, :] = inner_update(gradient, *state)

    def others(here, at):
        first_ref[at, :] = decay_first * first[at, :] + (1.0 - decay_first) * gradient_at(at, gradient_refs)

    steps(half, r, body)
    steps(half, 1 - r, others)


def outer_kernel(drift, other, anchor, momentum, out):
    half = out.shape[0]
    at = pl.ds(pl.multiple_of(lax.axis_index("rep") * half, half), half)
    out[...] = outer_update((drift[...] + other[...]) / 2, anchor[at, :], momentum[at, :])


def product(messages, rows, pieces):
    r = lax.axis_index("rep")
    half = rows // 2
    total = 0.0
    for (blocks, start), (mine, other) in zip(messages, pieces):
        for which, piece in ((r, mine), (1 - r, other)):
            at = pl.ds(pl.multiple_of(start + which * half, half), half)
            columns = jnp.concatenate([block[:, at] for block in blocks], axis=0)
            total += jnp.dot(columns, piece[...], preferred_element_type=jnp.float32)
    return total


def paired(refs):
    return [(refs[2 * n], refs[2 * n + 1]) for n in range(len(refs) // 2)]


def early_values_kernel(inner, rows, *refs):
    own, both = refs[:inner], refs[inner : 2 * inner]
    refs[-1][...] = product([(own, 0), (both, rows), (both, 0)], rows, paired(refs[2 * inner : -1]))


def late_values_kernel(inner, rows, early, *refs):
    tokens = early.shape[0] // inner
    total = early[...] + product([(refs[:inner], 0)], rows, [refs[inner : inner + 2]])
    for k, out in enumerate(refs[inner + 2 :]):
        out[...] = total[k * tokens : (k + 1) * tokens].astype(out.dtype)


def sum_kernel(*refs):
    total = refs[0][...]
    for ref in refs[1:-1]:
        total += ref[...].astype(jnp.float32)
    refs[-1][...] = total.astype(refs[-1].dtype)


def on_device(acts, value_cots, inner_weights, first_moment, second_moment, anchor, outer_momentum):
    inner = lax.axis_size("fsdp") // PLANES
    rows, width = anchor.shape
    if inner != 4 or lax.axis_size("rep") != 2 or rows % 256 or width % 128:
        return general(acts, value_cots, inner_weights, first_moment, second_moment, anchor, outer_momentum)
    tokens = acts.shape[1]
    half = rows // 2

    def planes(x, bits):
        return lax.ppermute(x, "fsdp", [(p * inner + i, (p ^ bits) * inner + i) for p in range(PLANES) for i in range(inner)])

    def across(x, k):
        return lax.ppermute(x, "fsdp", [(p * inner + i, p * inner + (i ^ k)) for p in range(PLANES) for i in range(inner)])

    def around(blocks):
        return [blocks[0]] + [across(blocks[k], k) for k in range(1, inner)]

    def swap(x):
        return lax.ppermute(x, "rep", [(0, 1), (1, 0)])

    out = [jax.ShapeDtypeStruct((tokens, rows + width), jnp.bfloat16)] * inner
    sems = [pltpu.SemaphoreType.DMA((2 * inner,))]
    kernel = partial(pack_first_kernel, inner, rows)
    first = around(call(kernel, "pack", out, [acts[0], value_cots[0]], 0, sems, space=pltpu.HBM))

    def pack(blocks, after):
        out = [jax.ShapeDtypeStruct((tokens, len(blocks) * rows), jnp.bfloat16)] * inner
        return call(partial(pack_kernel, inner, rows, blocks), "pack", out, [acts[0]], 0, after=after)

    second = around(pack((2, 1), first[1:2]))
    full = jax.ShapeDtypeStruct((rows, width), jnp.float32)
    sent = jax.ShapeDtypeStruct((rows, width), jnp.bfloat16)

    def gradient(message, at, out, arrived=(), flops=2 * inner * tokens * rows * width):
        kernel = partial(gradient_kernel, inner, rows, at)
        return call(kernel, "gradient", [out], message + first + list(arrived), flops)[0]

    beside_far = planes(gradient(first, 0, sent), 1)
    beside = planes(gradient(second, rows, sent, flops=AHEAD_FLOPS), 1)
    for_far = gradient(second, 0, sent, [beside_far])
    far = planes(for_far, 2)
    last = around(pack((0,), [for_far]))
    known = [gradient(last, 0, full), beside, far, inner_weights[0], first_moment[0], second_moment[0], anchor]
    half_block = jax.ShapeDtypeStruct((half, width), jnp.float32)
    (drift_out,) = call(drift_kernel, "drift", [half_block], known, 0)
    drift_in = swap(drift_out)
    first_next, drift = call(update_kernel, "update", [full, half_block], known, 0)
    new_half = jax.ShapeDtypeStruct((half, width), jnp.bfloat16)
    (mine,) = call(outer_kernel, "outer", [new_half], [drift, drift_in, anchor, outer_momentum], 0)
    mine2 = planes(mine, 2)
    mine1 = planes(mine, 1)
    mine3 = planes(mine2, 1)
    pieces = [y for x in (mine, mine1, mine2) for y in (x, swap(x))]
    flops = 2 * inner * tokens * rows * width
    (early,) = call(
        partial(early_values_kernel, inner, rows),
        "early_values",
        [jax.ShapeDtypeStruct((inner * tokens, width), jnp.float32)],
        last + second + pieces,
        3 * flops,
    )
    block = jax.ShapeDtypeStruct((tokens, width), jnp.bfloat16)
    own, *sums = call(
        partial(late_values_kernel, inner, rows),
        "late_values",
        [jax.ShapeDtypeStruct((tokens, width), jnp.float32)] + [block] * (inner - 1),
        [early] + first + [mine3, swap(mine3)],
        flops,
    )
    terms = [own] + [across(sums[k - 1], k) for k in range(1, inner)]
    (values,) = call(sum_kernel, "sum", [block], terms, 0)
    return (first_next[None], values[None])


def solution(mesh):
    placed = (
        P("rep", "fsdp", None),
        P("rep", "fsdp", None),
        P("rep", "fsdp", None),
        P("rep", "fsdp", None),
        P("rep", "fsdp", None),
        P("fsdp", None),
        P("fsdp", None),
    )
    return jax.shard_map(
        on_device,
        mesh=mesh,
        in_specs=placed,
        out_specs=(P("rep", "fsdp", None), P("rep", "fsdp", None)),
        check_vma=False,
    )
```

```python
from functools import partial

import jax
import jax.numpy as jnp
from jax import lax
from jax.experimental import pallas as pl
from jax.experimental.pallas import tpu as pltpu
from jax.sharding import PartitionSpec as P

decay_first = 0.9
decay_second = 0.95
inner_rate = 0.006
epsilon = 1e-08
outer_rate = 0.7
outer_decay = 0.9

PLANES = 4
CHUNK = 32
CONTRACT_ROWS = (((0,), (0,)), ((), ()))
AHEAD_FLOPS = 10**10
VMEM_BYTES = 16 * 1024 * 1024
FIRST_VMEM_BYTES = 61 * 1024 * 1024


def outer_update(average, anchor_rows, momentum_rows):
    velocity = outer_decay * momentum_rows + average
    return (anchor_rows - outer_rate * (average + outer_decay * velocity)).astype(jnp.bfloat16)


def inner_update(gradient, inner_weights, first_moment, second_moment, anchor):
    first_next = decay_first * first_moment + (1.0 - decay_first) * gradient
    second_next = decay_second * second_moment + (1.0 - decay_second) * gradient * gradient
    stepped = inner_weights - inner_rate * first_next / (jnp.sqrt(second_next) + epsilon)
    return first_next, anchor - stepped


def general(acts, value_cots, inner_weights, first_moment, second_moment, anchor, outer_momentum):
    tokens_local = acts[0]
    columns = lax.all_to_all(tokens_local, "fsdp", split_axis=1, concat_axis=0, tiled=True)
    cots = lax.all_gather(value_cots[0], "fsdp", axis=0, tiled=True)
    gradient = lax.dot_general(columns, cots, CONTRACT_ROWS, preferred_element_type=jnp.float32)
    first_next, drift = inner_update(gradient, inner_weights[0], first_moment[0], second_moment[0], anchor)
    average = lax.psum(drift, "rep") / lax.axis_size("rep")
    weights_next = outer_update(average, anchor, outer_momentum)
    gathered = lax.all_gather(weights_next, "fsdp", axis=0, tiled=True)
    values = jnp.dot(tokens_local, gathered, preferred_element_type=jnp.float32)
    return (first_next[None], values.astype(jnp.bfloat16)[None])


def flip(at, bits):
    low = lax.rem(at, 2)
    return (at // 2 + bits // 2 - 2 * (at // 2) * (bits // 2)) * 2 + low + bits % 2 - 2 * low * (bits % 2)


def call(kernel, name, out, inputs, flops, scratch=(), after=(), space=pltpu.VMEM, moved=None, vmem=VMEM_BYTES):
    if moved is None:
        moved = sum(x.size * x.dtype.itemsize for x in list(inputs) + list(out))
    count = len(inputs)

    def without_after(*refs):
        kernel(*refs[:count], *refs[count + len(after) :])

    return pl.pallas_call(
        without_after,
        out_shape=out,
        in_specs=[pl.BlockSpec(memory_space=space)] * count + [pl.BlockSpec(memory_space=pl.ANY)] * len(after),
        out_specs=[pl.BlockSpec(memory_space=pltpu.VMEM)] * len(out),
        scratch_shapes=list(scratch),
        compiler_params=pltpu.CompilerParams(vmem_limit_bytes=vmem),
        cost_estimate=pl.CostEstimate(flops=flops, bytes_accessed=moved, transcendentals=0),
        name=name,
    )(*inputs, *after)


def block_start(inner, rows, bits, k):
    f = lax.axis_index("fsdp")
    return pl.multiple_of((flip(f // inner, bits) * inner + flip(lax.rem(f, inner), k)) * rows, rows)


def pack_first_kernel(inner, rows, acts_ref, cots_ref, *refs):
    outs, sems = refs[:inner], refs[inner]
    copies = []
    for k in range(inner):
        block = acts_ref.at[:, pl.ds(block_start(inner, rows, 3, k), rows)]
        copies.append(pltpu.make_async_copy(block, outs[k].at[:, :rows], sems.at[2 * k]))
        copies.append(pltpu.make_async_copy(cots_ref, outs[k].at[:, rows:], sems.at[2 * k + 1]))
    for copy in copies:
        copy.start()
    for copy in copies:
        copy.wait()


def pack_kernel(inner, rows, blocks, acts_ref, *outs):
    for k in range(inner):
        for slot, bits in enumerate(blocks):
            outs[k][:, slot * rows : (slot + 1) * rows] = acts_ref[:, pl.ds(block_start(inner, rows, bits, k), rows)]


def gradient_kernel(inner, rows, acts_at, *refs):
    acts_refs, cots_refs, arrived, out = refs[:inner], refs[inner : 2 * inner], refs[2 * inner : -1], refs[-1]
    columns = jnp.concatenate([ref[:, acts_at : acts_at + rows] for ref in acts_refs], axis=0)
    cots = jnp.concatenate([ref[:, rows:] for ref in cots_refs], axis=0)
    total = lax.dot_general(columns, cots, CONTRACT_ROWS, preferred_element_type=jnp.float32)
    for ref in arrived:
        total += ref[...].astype(jnp.float32)
    out[...] = total.astype(out.dtype)


def gradient_at(at, refs):
    total, beside, far = refs
    return total[at, :] + beside[at, :].astype(jnp.float32) + far[at, :].astype(jnp.float32)


def steps(half, which, body):
    @pl.loop(0, half // CHUNK)
    def _(step):
        start = pl.multiple_of(step * CHUNK, CHUNK)
        body(pl.ds(start, CHUNK), pl.ds(pl.multiple_of(which * half + start, CHUNK), CHUNK))


def drift_kernel(*refs):
    gradient_refs, (weights, first, second, anchor), drift_ref = refs[:3], refs[3:7], refs[7]

    def body(here, at):
        gradient = gradient_at(at, gradient_refs)
        state = (weights[at, :], first[at, :], second[at, :], anchor[at, :])
        drift_ref[here, :] = inner_update(gradient, *state)[1]

    steps(drift_ref.shape[0], 1 - lax.axis_index("rep"), body)


def update_kernel(*refs):
    gradient_refs, (weights, first, second, anchor), (first_ref, drift_ref) = refs[:3], refs[3:7], refs[7:]
    half = drift_ref.shape[0]
    r = lax.axis_index("rep")

    def body(here, at):
        gradient = gradient_at(at, gradient_refs)
        state = (weights[at, :], first[at, :], second[at, :], anchor[at, :])
        first_ref[at, :], drift_ref[here, :] = inner_update(gradient, *state)

    def others(here, at):
        first_ref[at, :] = decay_first * first[at, :] + (1.0 - decay_first) * gradient_at(at, gradient_refs)

    steps(half, r, body)
    steps(half, 1 - r, others)


def outer_kernel(drift, other, anchor, momentum, out):
    half = out.shape[0]
    at = pl.ds(pl.multiple_of(lax.axis_index("rep") * half, half), half)
    out[...] = outer_update((drift[...] + other[...]) / 2, anchor[at, :], momentum[at, :])


def product(messages, rows, pieces):
    r = lax.axis_index("rep")
    half = rows // 2
    total = 0.0
    for (blocks, start), (mine, other) in zip(messages, pieces):
        for which, piece in ((r, mine), (1 - r, other)):
            at = pl.ds(pl.multiple_of(start + which * half, half), half)
            columns = jnp.concatenate([block[:, at] for block in blocks], axis=0)
            total += jnp.dot(columns, piece[...], preferred_element_type=jnp.float32)
    return total


def paired(refs):
    return [(refs[2 * n], refs[2 * n + 1]) for n in range(len(refs) // 2)]


def early_values_kernel(inner, rows, *refs):
    own, both = refs[:inner], refs[inner : 2 * inner]
    refs[-1][...] = product([(own, 0), (both, rows), (both, 0)], rows, paired(refs[2 * inner : -1]))


def late_values_kernel(inner, rows, early, *refs):
    tokens = early.shape[0] // inner
    total = early[...] + product([(refs[:inner], 0)], rows, [refs[inner : inner + 2]])
    for k, out in enumerate(refs[inner + 2 :]):
        out[...] = total[k * tokens : (k + 1) * tokens].astype(out.dtype)


def sum_kernel(*refs):
    total = refs[0][...]
    for ref in refs[1:-1]:
        total += ref[...].astype(jnp.float32)
    refs[-1][...] = total.astype(refs[-1].dtype)


def on_device(acts, value_cots, inner_weights, first_moment, second_moment, anchor, outer_momentum):
    inner = lax.axis_size("fsdp") // PLANES
    rows, width = anchor.shape
    if inner != 4 or lax.axis_size("rep") != 2 or rows % 256 or width % 128:
        return general(acts, value_cots, inner_weights, first_moment, second_moment, anchor, outer_momentum)
    tokens = acts.shape[1]
    half = rows // 2

    def planes(x, bits):
        return lax.ppermute(x, "fsdp", [(p * inner + i, (p ^ bits) * inner + i) for p in range(PLANES) for i in range(inner)])

    def across(x, k):
        return lax.ppermute(x, "fsdp", [(p * inner + i, p * inner + (i ^ k)) for p in range(PLANES) for i in range(inner)])

    def around(blocks):
        return [blocks[0]] + [across(blocks[k], k) for k in range(1, inner)]

    def swap(x):
        return lax.ppermute(x, "rep", [(0, 1), (1, 0)])

    out = [jax.ShapeDtypeStruct((tokens, rows + width), jnp.bfloat16)] * inner
    sems = [pltpu.SemaphoreType.DMA((2 * inner,))]
    kernel = partial(pack_first_kernel, inner, rows)
    first = around(call(kernel, "pack", out, [acts[0], value_cots[0]], 0, sems, space=pltpu.HBM, moved=0, vmem=FIRST_VMEM_BYTES))

    def pack(blocks, after):
        out = [jax.ShapeDtypeStruct((tokens, len(blocks) * rows), jnp.bfloat16)] * inner
        return call(partial(pack_kernel, inner, rows, blocks), "pack", out, [acts[0]], 0, after=after)

    second = around(pack((2, 1), first[1:2]))
    full = jax.ShapeDtypeStruct((rows, width), jnp.float32)
    sent = jax.ShapeDtypeStruct((rows, width), jnp.bfloat16)

    def gradient(message, at, out, arrived=(), flops=2 * inner * tokens * rows * width):
        kernel = partial(gradient_kernel, inner, rows, at)
        return call(kernel, "gradient", [out], message + first + list(arrived), flops)[0]

    beside_far = planes(gradient(first, 0, sent), 1)
    beside = planes(gradient(second, rows, sent, flops=AHEAD_FLOPS), 1)
    for_far = gradient(second, 0, sent, [beside_far])
    far = planes(for_far, 2)
    last = around(pack((0,), [for_far]))
    known = [gradient(last, 0, full), beside, far, inner_weights[0], first_moment[0], second_moment[0], anchor]
    half_block = jax.ShapeDtypeStruct((half, width), jnp.float32)
    (drift_out,) = call(drift_kernel, "drift", [half_block], known, 0)
    drift_in = swap(drift_out)
    first_next, drift = call(update_kernel, "update", [full, half_block], known, 0)
    new_half = jax.ShapeDtypeStruct((half, width), jnp.bfloat16)
    (mine,) = call(outer_kernel, "outer", [new_half], [drift, drift_in, anchor, outer_momentum], 0)
    mine2 = planes(mine, 2)
    mine1 = planes(mine, 1)
    mine3 = planes(mine2, 1)
    pieces = [y for x in (mine, mine1, mine2) for y in (x, swap(x))]
    flops = 2 * inner * tokens * rows * width
    (early,) = call(
        partial(early_values_kernel, inner, rows),
        "early_values",
        [jax.ShapeDtypeStruct((inner * tokens, width), jnp.float32)],
        last + second + pieces,
        3 * flops,
    )
    block = jax.ShapeDtypeStruct((tokens, width), jnp.bfloat16)
    own, *sums = call(
        partial(late_values_kernel, inner, rows),
        "late_values",
        [jax.ShapeDtypeStruct((tokens, width), jnp.float32)] + [block] * (inner - 1),
        [early] + first + [mine3, swap(mine3)],
        flops,
    )
    terms = [own] + [across(sums[k - 1], k) for k in range(1, inner)]
    (values,) = call(sum_kernel, "sum", [block], terms, 0)
    return (first_next[None], values[None])


def solution(mesh):
    placed = (
        P("rep", "fsdp", None),
        P("rep", "fsdp", None),
        P("rep", "fsdp", None),
        P("rep", "fsdp", None),
        P("rep", "fsdp", None),
        P("fsdp", None),
        P("fsdp", None),
    )
    return jax.shard_map(
        on_device,
        mesh=mesh,
        in_specs=placed,
        out_specs=(P("rep", "fsdp", None), P("rep", "fsdp", None)),
        check_vma=False,
    )
```

```python
from functools import partial

import jax
import jax.numpy as jnp
from jax import lax
from jax.experimental import pallas as pl
from jax.experimental.pallas import tpu as pltpu
from jax.sharding import PartitionSpec as P

decay_first = 0.9
decay_second = 0.95
inner_rate = 0.006
epsilon = 1e-08
outer_rate = 0.7
outer_decay = 0.9

PLANES = 4
CHUNK = 32
CONTRACT_ROWS = (((0,), (0,)), ((), ()))
AHEAD_FLOPS = 10**10
VMEM_BYTES = 16 * 1024 * 1024
FIRST_VMEM_BYTES = 61 * 1024 * 1024


def outer_update(average, anchor_rows, momentum_rows):
    velocity = outer_decay * momentum_rows + average
    return (anchor_rows - outer_rate * (average + outer_decay * velocity)).astype(jnp.bfloat16)


def inner_update(gradient, inner_weights, first_moment, second_moment, anchor):
    first_next = decay_first * first_moment + (1.0 - decay_first) * gradient
    second_next = decay_second * second_moment + (1.0 - decay_second) * gradient * gradient
    stepped = inner_weights - inner_rate * first_next / (jnp.sqrt(second_next) + epsilon)
    return first_next, anchor - stepped


def general(acts, value_cots, inner_weights, first_moment, second_moment, anchor, outer_momentum):
    tokens_local = acts[0]
    columns = lax.all_to_all(tokens_local, "fsdp", split_axis=1, concat_axis=0, tiled=True)
    cots = lax.all_gather(value_cots[0], "fsdp", axis=0, tiled=True)
    gradient = lax.dot_general(columns, cots, CONTRACT_ROWS, preferred_element_type=jnp.float32)
    first_next, drift = inner_update(gradient, inner_weights[0], first_moment[0], second_moment[0], anchor)
    average = lax.psum(drift, "rep") / lax.axis_size("rep")
    weights_next = outer_update(average, anchor, outer_momentum)
    gathered = lax.all_gather(weights_next, "fsdp", axis=0, tiled=True)
    values = jnp.dot(tokens_local, gathered, preferred_element_type=jnp.float32)
    return (first_next[None], values.astype(jnp.bfloat16)[None])


def flip(at, bits):
    low = lax.rem(at, 2)
    return (at // 2 + bits // 2 - 2 * (at // 2) * (bits // 2)) * 2 + low + bits % 2 - 2 * low * (bits % 2)


def call(kernel, name, out, inputs, flops, scratch=(), after=(), space=pltpu.VMEM, moved=None, vmem=VMEM_BYTES):
    if moved is None:
        moved = sum(x.size * x.dtype.itemsize for x in list(inputs) + list(out))
    count = len(inputs)

    def without_after(*refs):
        kernel(*refs[:count], *refs[count + len(after) :])

    return pl.pallas_call(
        without_after,
        out_shape=out,
        in_specs=[pl.BlockSpec(memory_space=space)] * count + [pl.BlockSpec(memory_space=pl.ANY)] * len(after),
        out_specs=[pl.BlockSpec(memory_space=pltpu.VMEM)] * len(out),
        scratch_shapes=list(scratch),
        compiler_params=pltpu.CompilerParams(vmem_limit_bytes=vmem),
        cost_estimate=pl.CostEstimate(flops=flops, bytes_accessed=moved, transcendentals=0),
        name=name,
    )(*inputs, *after)


def block_start(inner, rows, bits, k):
    f = lax.axis_index("fsdp")
    return pl.multiple_of((flip(f // inner, bits) * inner + flip(lax.rem(f, inner), k)) * rows, rows)


def pack_first_kernel(inner, rows, acts_ref, cots_ref, *refs):
    outs, sems = refs[:inner], refs[inner]
    copies = []
    for k in range(inner):
        block = acts_ref.at[:, pl.ds(block_start(inner, rows, 3, k), rows)]
        copies.append(pltpu.make_async_copy(block, outs[k].at[:, :rows], sems.at[2 * k]))
        copies.append(pltpu.make_async_copy(cots_ref, outs[k].at[:, rows:], sems.at[2 * k + 1]))
    for copy in copies:
        copy.start()
    for copy in copies:
        copy.wait()


def pack_kernel(inner, rows, blocks, acts_ref, *outs):
    for k in range(inner):
        for slot, bits in enumerate(blocks):
            outs[k][:, slot * rows : (slot + 1) * rows] = acts_ref[:, pl.ds(block_start(inner, rows, bits, k), rows)]


def gradient_kernel(inner, rows, acts_at, *refs):
    acts_refs, cots_refs, arrived, out = refs[:inner], refs[inner : 2 * inner], refs[2 * inner : -1], refs[-1]
    columns = jnp.concatenate([ref[:, acts_at : acts_at + rows] for ref in acts_refs], axis=0)
    cots = jnp.concatenate([ref[:, rows:] for ref in cots_refs], axis=0)
    total = lax.dot_general(columns, cots, CONTRACT_ROWS, preferred_element_type=jnp.float32)
    for ref in arrived:
        total += ref[...].astype(jnp.float32)
    out[...] = total.astype(out.dtype)


def gradient_at(at, refs):
    total, beside, far = refs
    return total[at, :] + beside[at, :].astype(jnp.float32) + far[at, :].astype(jnp.float32)


def steps(half, which, body):
    @pl.loop(0, half // CHUNK)
    def _(step):
        start = pl.multiple_of(step * CHUNK, CHUNK)
        body(pl.ds(start, CHUNK), pl.ds(pl.multiple_of(which * half + start, CHUNK), CHUNK))


def drift_kernel(*refs):
    gradient_refs, (weights, first, second, anchor), drift_ref = refs[:3], refs[3:7], refs[7]

    def body(here, at):
        gradient = gradient_at(at, gradient_refs)
        state = (weights[at, :], first[at, :], second[at, :], anchor[at, :])
        drift_ref[here, :] = inner_update(gradient, *state)[1]

    steps(drift_ref.shape[0], 1 - lax.axis_index("rep"), body)


def update_kernel(*refs):
    gradient_refs, (weights, first, second, anchor), (first_ref, drift_ref) = refs[:3], refs[3:7], refs[7:]
    half = drift_ref.shape[0]
    r = lax.axis_index("rep")

    def body(here, at):
        gradient = gradient_at(at, gradient_refs)
        state = (weights[at, :], first[at, :], second[at, :], anchor[at, :])
        first_ref[at, :], drift_ref[here, :] = inner_update(gradient, *state)

    def others(here, at):
        first_ref[at, :] = decay_first * first[at, :] + (1.0 - decay_first) * gradient_at(at, gradient_refs)

    steps(half, r, body)
    steps(half, 1 - r, others)


def outer_kernel(drift, other, anchor, momentum, out):
    half = out.shape[0]
    at = pl.ds(pl.multiple_of(lax.axis_index("rep") * half, half), half)
    out[...] = outer_update((drift[...] + other[...]) / 2, anchor[at, :], momentum[at, :])


def product(messages, rows, pieces):
    r = lax.axis_index("rep")
    half = rows // 2
    total = 0.0
    for (blocks, start), (mine, other) in zip(messages, pieces):
        for which, piece in ((r, mine), (1 - r, other)):
            at = pl.ds(pl.multiple_of(start + which * half, half), half)
            columns = jnp.concatenate([block[:, at] for block in blocks], axis=0)
            total += jnp.dot(columns, piece[...], preferred_element_type=jnp.float32)
    return total


def paired(refs):
    return [(refs[2 * n], refs[2 * n + 1]) for n in range(len(refs) // 2)]


def early_values_kernel(inner, rows, *refs):
    own, both = refs[:inner], refs[inner : 2 * inner]
    refs[-1][...] = product([(own, 0), (both, rows), (both, 0)], rows, paired(refs[2 * inner : -1]))


def late_values_kernel(inner, rows, early, *refs):
    tokens = early.shape[0] // inner
    total = early[...] + product([(refs[:inner], 0)], rows, [refs[inner : inner + 2]])
    for k, out in enumerate(refs[inner + 2 :]):
        out[...] = total[k * tokens : (k + 1) * tokens].astype(out.dtype)


def sum_kernel(*refs):
    total = refs[0][...]
    for ref in refs[1:-1]:
        total += ref[...].astype(jnp.float32)
    refs[-1][...] = total.astype(refs[-1].dtype)


def on_device(acts, value_cots, inner_weights, first_moment, second_moment, anchor, outer_momentum):
    inner = lax.axis_size("fsdp") // PLANES
    rows, width = anchor.shape
    if inner != 4 or lax.axis_size("rep") != 2 or rows % 256 or width % 128:
        return general(acts, value_cots, inner_weights, first_moment, second_moment, anchor, outer_momentum)
    tokens = acts.shape[1]
    half = rows // 2

    def planes(x, bits):
        return lax.ppermute(x, "fsdp", [(p * inner + i, (p ^ bits) * inner + i) for p in range(PLANES) for i in range(inner)])

    def across(x, k):
        return lax.ppermute(x, "fsdp", [(p * inner + i, p * inner + (i ^ k)) for p in range(PLANES) for i in range(inner)])

    def around(blocks):
        return [blocks[0]] + [across(blocks[k], k) for k in range(1, inner)]

    def swap(x):
        return lax.ppermute(x, "rep", [(0, 1), (1, 0)])

    out = [jax.ShapeDtypeStruct((tokens, rows + width), jnp.bfloat16)] * inner
    sems = [pltpu.SemaphoreType.DMA((2 * inner,))]
    kernel = partial(pack_first_kernel, inner, rows)
    first = around(call(kernel, "pack", out, [acts[0], value_cots[0]], 0, sems, space=pltpu.HBM, moved=0, vmem=FIRST_VMEM_BYTES))

    def pack(blocks, after):
        out = [jax.ShapeDtypeStruct((tokens, len(blocks) * rows), jnp.bfloat16)] * inner
        return call(partial(pack_kernel, inner, rows, blocks), "pack", out, [acts[0]], 0, after=after)

    second = around(pack((2, 1), first[1:2]))
    full = jax.ShapeDtypeStruct((rows, width), jnp.float32)
    sent = jax.ShapeDtypeStruct((rows, width), jnp.bfloat16)

    def gradient(message, at, out, arrived=(), flops=2 * inner * tokens * rows * width):
        kernel = partial(gradient_kernel, inner, rows, at)
        return call(kernel, "gradient", [out], message + first + list(arrived), flops)[0]

    beside_far = planes(gradient(first, 0, sent), 1)
    beside = planes(gradient(second, rows, sent, flops=AHEAD_FLOPS), 1)
    for_far = gradient(second, 0, sent, [beside_far])
    far = planes(for_far, 2)
    last = around(pack((0,), [for_far]))
    known = [gradient(last, 0, full), beside, far, inner_weights[0], first_moment[0], second_moment[0], anchor]
    half_block = jax.ShapeDtypeStruct((half, width), jnp.float32)
    (drift_out,) = call(drift_kernel, "drift", [half_block], known, 0)
    drift_in = swap(drift_out)
    first_next, drift = call(update_kernel, "update", [full, half_block], known, 0)
    new_half = jax.ShapeDtypeStruct((half, width), jnp.bfloat16)
    (mine,) = call(outer_kernel, "outer", [new_half], [drift, drift_in, anchor, outer_momentum], 0)
    mine2 = planes(mine, 2)
    mine1 = planes(mine, 1)
    mine3 = planes(mine2, 1)
    pieces = [y for x in (mine, mine1, mine2) for y in (x, swap(x))]
    flops = 2 * inner * tokens * rows * width
    (early,) = call(
        partial(early_values_kernel, inner, rows),
        "early_values",
        [jax.ShapeDtypeStruct((inner * tokens, width), jnp.float32)],
        last + second + pieces,
        3 * flops,
    )
    block = jax.ShapeDtypeStruct((tokens, width), jnp.bfloat16)
    own, *sums = call(
        partial(late_values_kernel, inner, rows),
        "late_values",
        [jax.ShapeDtypeStruct((tokens, width), jnp.float32)] + [block] * (inner - 1),
        [early] + first + [mine3, swap(mine3)],
        flops,
    )
    terms = [own] + [across(sums[k - 1], k) for k in reversed(range(1, inner))]
    (values,) = call(sum_kernel, "sum", [block], terms, 0)
    return (first_next[None], values[None])


def solution(mesh):
    placed = (
        P("rep", "fsdp", None),
        P("rep", "fsdp", None),
        P("rep", "fsdp", None),
        P("rep", "fsdp", None),
        P("rep", "fsdp", None),
        P("fsdp", None),
        P("fsdp", None),
    )
    return jax.shard_map(
        on_device,
        mesh=mesh,
        in_specs=placed,
        out_specs=(P("rep", "fsdp", None), P("rep", "fsdp", None)),
        check_vma=False,
    )
```

```python
from functools import partial

import jax
import jax.numpy as jnp
from jax import lax
from jax.experimental import pallas as pl
from jax.experimental.pallas import tpu as pltpu
from jax.sharding import PartitionSpec as P

decay_first = 0.9
decay_second = 0.95
inner_rate = 0.006
epsilon = 1e-08
outer_rate = 0.7
outer_decay = 0.9

PLANES = 4
CHUNK = 32
CONTRACT_ROWS = (((0,), (0,)), ((), ()))
AHEAD_FLOPS = 10**10
VMEM_BYTES = 16 * 1024 * 1024
FIRST_VMEM_BYTES = 61 * 1024 * 1024


def outer_update(average, anchor_rows, momentum_rows):
    velocity = outer_decay * momentum_rows + average
    return (anchor_rows - outer_rate * (average + outer_decay * velocity)).astype(jnp.bfloat16)


def inner_update(gradient, inner_weights, first_moment, second_moment, anchor):
    first_next = decay_first * first_moment + (1.0 - decay_first) * gradient
    second_next = decay_second * second_moment + (1.0 - decay_second) * gradient * gradient
    stepped = inner_weights - inner_rate * first_next / (jnp.sqrt(second_next) + epsilon)
    return first_next, anchor - stepped


def general(acts, value_cots, inner_weights, first_moment, second_moment, anchor, outer_momentum):
    tokens_local = acts[0]
    columns = lax.all_to_all(tokens_local, "fsdp", split_axis=1, concat_axis=0, tiled=True)
    cots = lax.all_gather(value_cots[0], "fsdp", axis=0, tiled=True)
    gradient = lax.dot_general(columns, cots, CONTRACT_ROWS, preferred_element_type=jnp.float32)
    first_next, drift = inner_update(gradient, inner_weights[0], first_moment[0], second_moment[0], anchor)
    average = lax.psum(drift, "rep") / lax.axis_size("rep")
    weights_next = outer_update(average, anchor, outer_momentum)
    gathered = lax.all_gather(weights_next, "fsdp", axis=0, tiled=True)
    values = jnp.dot(tokens_local, gathered, preferred_element_type=jnp.float32)
    return (first_next[None], values.astype(jnp.bfloat16)[None])


def flip(at, bits):
    low = lax.rem(at, 2)
    return (at // 2 + bits // 2 - 2 * (at // 2) * (bits // 2)) * 2 + low + bits % 2 - 2 * low * (bits % 2)


def call(kernel, name, out, inputs, flops, scratch=(), after=(), space=pltpu.VMEM, moved=None, vmem=VMEM_BYTES):
    if moved is None:
        moved = sum(x.size * x.dtype.itemsize for x in list(inputs) + list(out))
    count = len(inputs)

    def without_after(*refs):
        kernel(*refs[:count], *refs[count + len(after) :])

    return pl.pallas_call(
        without_after,
        out_shape=out,
        in_specs=[pl.BlockSpec(memory_space=space)] * count + [pl.BlockSpec(memory_space=pl.ANY)] * len(after),
        out_specs=[pl.BlockSpec(memory_space=pltpu.VMEM)] * len(out),
        scratch_shapes=list(scratch),
        compiler_params=pltpu.CompilerParams(vmem_limit_bytes=vmem),
        cost_estimate=pl.CostEstimate(flops=flops, bytes_accessed=moved, transcendentals=0),
        name=name,
    )(*inputs, *after)


def block_start(inner, rows, bits, k):
    f = lax.axis_index("fsdp")
    return pl.multiple_of((flip(f // inner, bits) * inner + flip(lax.rem(f, inner), k)) * rows, rows)


def pack_first_kernel(inner, rows, acts_ref, cots_ref, *refs):
    outs, sems = refs[:inner], refs[inner]
    copies = []
    for k in range(inner):
        block = acts_ref.at[:, pl.ds(block_start(inner, rows, 3, k), rows)]
        copies.append(pltpu.make_async_copy(block, outs[k].at[:, :rows], sems.at[2 * k]))
        copies.append(pltpu.make_async_copy(cots_ref, outs[k].at[:, rows:], sems.at[2 * k + 1]))
    for copy in copies:
        copy.start()
    for copy in copies:
        copy.wait()


def pack_kernel(inner, rows, blocks, acts_ref, *outs):
    for k in range(inner):
        for slot, bits in enumerate(blocks):
            outs[k][:, slot * rows : (slot + 1) * rows] = acts_ref[:, pl.ds(block_start(inner, rows, bits, k), rows)]


def gradient_kernel(inner, rows, acts_at, *refs):
    acts_refs, cots_refs, arrived, out = refs[:inner], refs[inner : 2 * inner], refs[2 * inner : -1], refs[-1]
    columns = jnp.concatenate([ref[:, acts_at : acts_at + rows] for ref in acts_refs], axis=0)
    cots = jnp.concatenate([ref[:, rows:] for ref in cots_refs], axis=0)
    total = lax.dot_general(columns, cots, CONTRACT_ROWS, preferred_element_type=jnp.float32)
    for ref in arrived:
        total += ref[...].astype(jnp.float32)
    out[...] = total.astype(out.dtype)


def gradient_at(at, refs):
    total, beside, far = refs
    return total[at, :] + beside[at, :].astype(jnp.float32) + far[at, :].astype(jnp.float32)


def steps(half, which, body):
    @pl.loop(0, half // CHUNK)
    def _(step):
        start = pl.multiple_of(step * CHUNK, CHUNK)
        body(pl.ds(start, CHUNK), pl.ds(pl.multiple_of(which * half + start, CHUNK), CHUNK))


def drift_kernel(*refs):
    gradient_refs, (weights, first, second, anchor), drift_ref = refs[:3], refs[3:7], refs[7]

    def body(here, at):
        gradient = gradient_at(at, gradient_refs)
        state = (weights[at, :], first[at, :], second[at, :], anchor[at, :])
        drift_ref[here, :] = inner_update(gradient, *state)[1]

    steps(drift_ref.shape[0], 1 - lax.axis_index("rep"), body)


def update_kernel(*refs):
    gradient_refs, (weights, first, second, anchor), (first_ref, drift_ref) = refs[:3], refs[3:7], refs[7:]
    half = drift_ref.shape[0]
    r = lax.axis_index("rep")

    def body(here, at):
        gradient = gradient_at(at, gradient_refs)
        state = (weights[at, :], first[at, :], second[at, :], anchor[at, :])
        first_ref[at, :], drift_ref[here, :] = inner_update(gradient, *state)

    def others(here, at):
        first_ref[at, :] = decay_first * first[at, :] + (1.0 - decay_first) * gradient_at(at, gradient_refs)

    steps(half, r, body)
    steps(half, 1 - r, others)


def outer_kernel(drift, other, anchor, momentum, out):
    half = out.shape[0]
    at = pl.ds(pl.multiple_of(lax.axis_index("rep") * half, half), half)
    out[...] = outer_update((drift[...] + other[...]) / 2, anchor[at, :], momentum[at, :])


def copy_kernel(ref, out):
    out[...] = ref[...]


def product(messages, rows, pieces):
    r = lax.axis_index("rep")
    half = rows // 2
    total = 0.0
    for (blocks, start), (mine, other) in zip(messages, pieces):
        for which, piece in ((r, mine), (1 - r, other)):
            at = pl.ds(pl.multiple_of(start + which * half, half), half)
            columns = jnp.concatenate([block[:, at] for block in blocks], axis=0)
            total += jnp.dot(columns, piece[...], preferred_element_type=jnp.float32)
    return total


def paired(refs):
    return [(refs[2 * n], refs[2 * n + 1]) for n in range(len(refs) // 2)]


def early_values_kernel(inner, rows, *refs):
    own, both = refs[:inner], refs[inner : 2 * inner]
    refs[-1][...] = product([(own, 0), (both, rows), (both, 0)], rows, paired(refs[2 * inner : -1]))


def late_values_kernel(inner, rows, early, *refs):
    tokens = early.shape[0] // inner
    total = early[...] + product([(refs[:inner], 0)], rows, [refs[inner : inner + 2]])
    for k, out in enumerate(refs[inner + 2 :]):
        out[...] = total[k * tokens : (k + 1) * tokens].astype(out.dtype)


def sum_kernel(*refs):
    total = refs[0][...]
    for ref in refs[1:-1]:
        total += ref[...].astype(jnp.float32)
    refs[-1][...] = total.astype(refs[-1].dtype)


def on_device(acts, value_cots, inner_weights, first_moment, second_moment, anchor, outer_momentum):
    inner = lax.axis_size("fsdp") // PLANES
    rows, width = anchor.shape
    if inner != 4 or lax.axis_size("rep") != 2 or rows % 256 or width % 128:
        return general(acts, value_cots, inner_weights, first_moment, second_moment, anchor, outer_momentum)
    tokens = acts.shape[1]
    half = rows // 2

    def planes(x, bits):
        return lax.ppermute(x, "fsdp", [(p * inner + i, (p ^ bits) * inner + i) for p in range(PLANES) for i in range(inner)])

    def across(x, k):
        return lax.ppermute(x, "fsdp", [(p * inner + i, p * inner + (i ^ k)) for p in range(PLANES) for i in range(inner)])

    def around(blocks):
        return [blocks[0]] + [across(blocks[k], k) for k in range(1, inner)]

    def swap(x):
        return lax.ppermute(x, "rep", [(0, 1), (1, 0)])

    out = [jax.ShapeDtypeStruct((tokens, rows + width), jnp.bfloat16)] * inner
    sems = [pltpu.SemaphoreType.DMA((2 * inner,))]
    kernel = partial(pack_first_kernel, inner, rows)
    first = around(call(kernel, "pack", out, [acts[0], value_cots[0]], 0, sems, space=pltpu.HBM, moved=0, vmem=FIRST_VMEM_BYTES))

    def pack(blocks, after):
        out = [jax.ShapeDtypeStruct((tokens, len(blocks) * rows), jnp.bfloat16)] * inner
        return call(partial(pack_kernel, inner, rows, blocks), "pack", out, [acts[0]], 0, after=after)

    second = around(pack((2, 1), first[1:2]))
    full = jax.ShapeDtypeStruct((rows, width), jnp.float32)
    sent = jax.ShapeDtypeStruct((rows, width), jnp.bfloat16)

    def gradient(message, at, out, arrived=(), flops=2 * inner * tokens * rows * width):
        kernel = partial(gradient_kernel, inner, rows, at)
        return call(kernel, "gradient", [out], message + first + list(arrived), flops)[0]

    beside_far = planes(gradient(first, 0, sent), 1)
    beside = planes(gradient(second, rows, sent, flops=AHEAD_FLOPS), 1)
    for_far = gradient(second, 0, sent, [beside_far])
    far = planes(for_far, 2)
    last = around(pack((0,), [for_far]))
    known = [gradient(last, 0, full), beside, far, inner_weights[0], first_moment[0], second_moment[0], anchor]
    half_block = jax.ShapeDtypeStruct((half, width), jnp.float32)
    (drift_out,) = call(drift_kernel, "drift", [half_block], known, 0)
    drift_in = swap(drift_out)
    first_next, drift = call(update_kernel, "update", [full, half_block], known, 0)
    new_half = jax.ShapeDtypeStruct((half, width), jnp.bfloat16)
    (mine,) = call(outer_kernel, "outer", [new_half], [drift, drift_in, anchor, outer_momentum], 0)
    mine2 = planes(mine, 2)
    other = swap(mine)
    (again,) = call(copy_kernel, "again", [new_half], [mine], 0, after=[other])
    mine1 = planes(again, 1)
    mine3 = planes(mine2, 1)
    pieces = [mine, other] + [y for x in (mine1, mine2) for y in (x, swap(x))]
    flops = 2 * inner * tokens * rows * width
    (early,) = call(
        partial(early_values_kernel, inner, rows),
        "early_values",
        [jax.ShapeDtypeStruct((inner * tokens, width), jnp.float32)],
        last + second + pieces,
        3 * flops,
    )
    block = jax.ShapeDtypeStruct((tokens, width), jnp.bfloat16)
    own, *sums = call(
        partial(late_values_kernel, inner, rows),
        "late_values",
        [jax.ShapeDtypeStruct((tokens, width), jnp.float32)] + [block] * (inner - 1),
        [early] + first + [mine3, swap(mine3)],
        flops,
    )
    terms = [own] + [across(sums[k - 1], k) for k in range(1, inner)]
    (values,) = call(sum_kernel, "sum", [block], terms, 0)
    return (first_next[None], values[None])


def solution(mesh):
    placed = (
        P("rep", "fsdp", None),
        P("rep", "fsdp", None),
        P("rep", "fsdp", None),
        P("rep", "fsdp", None),
        P("rep", "fsdp", None),
        P("fsdp", None),
        P("fsdp", None),
    )
    return jax.shard_map(
        on_device,
        mesh=mesh,
        in_specs=placed,
        out_specs=(P("rep", "fsdp", None), P("rep", "fsdp", None)),
        check_vma=False,
    )
```

```python
from functools import partial

import jax
import jax.numpy as jnp
from jax import lax
from jax.experimental import pallas as pl
from jax.experimental.pallas import tpu as pltpu
from jax.sharding import PartitionSpec as P

decay_first = 0.9
decay_second = 0.95
inner_rate = 0.006
epsilon = 1e-08
outer_rate = 0.7
outer_decay = 0.9

PLANES = 4
CHUNK = 32
CONTRACT_ROWS = (((0,), (0,)), ((), ()))
VMEM_BYTES = 16 * 1024 * 1024
FIRST_VMEM_BYTES = 61 * 1024 * 1024


def outer_update(average, anchor_rows, momentum_rows):
    velocity = outer_decay * momentum_rows + average
    return (anchor_rows - outer_rate * (average + outer_decay * velocity)).astype(jnp.bfloat16)


def inner_update(gradient, inner_weights, first_moment, second_moment, anchor):
    first_next = decay_first * first_moment + (1.0 - decay_first) * gradient
    second_next = decay_second * second_moment + (1.0 - decay_second) * gradient * gradient
    stepped = inner_weights - inner_rate * first_next / (jnp.sqrt(second_next) + epsilon)
    return first_next, anchor - stepped


def general(acts, value_cots, inner_weights, first_moment, second_moment, anchor, outer_momentum):
    tokens_local = acts[0]
    columns = lax.all_to_all(tokens_local, "fsdp", split_axis=1, concat_axis=0, tiled=True)
    cots = lax.all_gather(value_cots[0], "fsdp", axis=0, tiled=True)
    gradient = lax.dot_general(columns, cots, CONTRACT_ROWS, preferred_element_type=jnp.float32)
    first_next, drift = inner_update(gradient, inner_weights[0], first_moment[0], second_moment[0], anchor)
    average = lax.psum(drift, "rep") / lax.axis_size("rep")
    weights_next = outer_update(average, anchor, outer_momentum)
    gathered = lax.all_gather(weights_next, "fsdp", axis=0, tiled=True)
    values = jnp.dot(tokens_local, gathered, preferred_element_type=jnp.float32)
    return (first_next[None], values.astype(jnp.bfloat16)[None])


def flip(at, bits):
    low = lax.rem(at, 2)
    return (at // 2 + bits // 2 - 2 * (at // 2) * (bits // 2)) * 2 + low + bits % 2 - 2 * low * (bits % 2)


def call(kernel, name, out, inputs, flops, scratch=(), after=(), space=pltpu.VMEM, moved=None, vmem=VMEM_BYTES):
    if moved is None:
        moved = sum(x.size * x.dtype.itemsize for x in list(inputs) + list(out))
    count = len(inputs)

    def without_after(*refs):
        kernel(*refs[:count], *refs[count + len(after) :])

    return pl.pallas_call(
        without_after,
        out_shape=out,
        in_specs=[pl.BlockSpec(memory_space=space)] * count + [pl.BlockSpec(memory_space=pl.ANY)] * len(after),
        out_specs=[pl.BlockSpec(memory_space=pltpu.VMEM)] * len(out),
        scratch_shapes=list(scratch),
        compiler_params=pltpu.CompilerParams(vmem_limit_bytes=vmem),
        cost_estimate=pl.CostEstimate(flops=flops, bytes_accessed=moved, transcendentals=0),
        name=name,
    )(*inputs, *after)


def block_start(inner, rows, bits, k):
    f = lax.axis_index("fsdp")
    return pl.multiple_of((flip(f // inner, bits) * inner + flip(lax.rem(f, inner), k)) * rows, rows)


def pack_first_kernel(inner, rows, acts_ref, cots_ref, *refs):
    outs, sems = refs[:inner], refs[inner]
    copies = []
    for k in range(inner):
        block = acts_ref.at[:, pl.ds(block_start(inner, rows, 3, k), rows)]
        copies.append(pltpu.make_async_copy(block, outs[k].at[:, :rows], sems.at[2 * k]))
        copies.append(pltpu.make_async_copy(cots_ref, outs[k].at[:, rows:], sems.at[2 * k + 1]))
    for copy in copies:
        copy.start()
    for copy in copies:
        copy.wait()


def pack_kernel(inner, rows, blocks, acts_ref, *outs):
    for k in range(inner):
        for slot, bits in enumerate(blocks):
            outs[k][:, slot * rows : (slot + 1) * rows] = acts_ref[:, pl.ds(block_start(inner, rows, bits, k), rows)]


def gradient_kernel(inner, rows, acts_at, *refs):
    acts_refs, cots_refs, arrived, out = refs[:inner], refs[inner : 2 * inner], refs[2 * inner : -1], refs[-1]
    columns = jnp.concatenate([ref[:, acts_at : acts_at + rows] for ref in acts_refs], axis=0)
    cots = jnp.concatenate([ref[:, rows:] for ref in cots_refs], axis=0)
    total = lax.dot_general(columns, cots, CONTRACT_ROWS, preferred_element_type=jnp.float32)
    for ref in arrived:
        total += ref[...].astype(jnp.float32)
    out[...] = total.astype(out.dtype)


def gradient_at(at, refs):
    total, beside, far = refs
    return total[at, :] + beside[at, :].astype(jnp.float32) + far[at, :].astype(jnp.float32)


def steps(half, which, body):
    @pl.loop(0, half // CHUNK)
    def _(step):
        start = pl.multiple_of(step * CHUNK, CHUNK)
        body(pl.ds(start, CHUNK), pl.ds(pl.multiple_of(which * half + start, CHUNK), CHUNK))


def drift_kernel(*refs):
    gradient_refs, (weights, first, second, anchor), drift_ref = refs[:3], refs[3:7], refs[7]

    def body(here, at):
        gradient = gradient_at(at, gradient_refs)
        state = (weights[at, :], first[at, :], second[at, :], anchor[at, :])
        drift_ref[here, :] = inner_update(gradient, *state)[1]

    steps(drift_ref.shape[0], 1 - lax.axis_index("rep"), body)


def update_kernel(*refs):
    gradient_refs, (weights, first, second, anchor), (first_ref, drift_ref) = refs[:3], refs[3:7], refs[7:]
    half = drift_ref.shape[0]
    r = lax.axis_index("rep")

    def body(here, at):
        gradient = gradient_at(at, gradient_refs)
        state = (weights[at, :], first[at, :], second[at, :], anchor[at, :])
        first_ref[at, :], drift_ref[here, :] = inner_update(gradient, *state)

    def others(here, at):
        first_ref[at, :] = decay_first * first[at, :] + (1.0 - decay_first) * gradient_at(at, gradient_refs)

    steps(half, r, body)
    steps(half, 1 - r, others)


def outer_kernel(drift, other, anchor, momentum, out):
    half = out.shape[0]
    at = pl.ds(pl.multiple_of(lax.axis_index("rep") * half, half), half)
    out[...] = outer_update((drift[...] + other[...]) / 2, anchor[at, :], momentum[at, :])


def product(messages, rows, pieces):
    r = lax.axis_index("rep")
    half = rows // 2
    total = 0.0
    for (blocks, start), (mine, other) in zip(messages, pieces):
        for which, piece in ((r, mine), (1 - r, other)):
            at = pl.ds(pl.multiple_of(start + which * half, half), half)
            columns = jnp.concatenate([block[:, at] for block in blocks], axis=0)
            total += jnp.dot(columns, piece[...], preferred_element_type=jnp.float32)
    return total


def paired(refs):
    return [(refs[2 * n], refs[2 * n + 1]) for n in range(len(refs) // 2)]


def early_values_kernel(inner, rows, *refs):
    own, both = refs[:inner], refs[inner : 2 * inner]
    refs[-1][...] = product([(own, 0), (both, rows), (both, 0)], rows, paired(refs[2 * inner : -1]))


def late_values_kernel(inner, rows, early, *refs):
    tokens = early.shape[0] // inner
    total = early[...] + product([(refs[:inner], 0)], rows, [refs[inner : inner + 2]])
    for k, out in enumerate(refs[inner + 2 :]):
        out[...] = total[k * tokens : (k + 1) * tokens].astype(out.dtype)


def sum_kernel(*refs):
    total = refs[0][...]
    for ref in refs[1:-1]:
        total += ref[...].astype(jnp.float32)
    refs[-1][...] = total.astype(refs[-1].dtype)


def on_device(acts, value_cots, inner_weights, first_moment, second_moment, anchor, outer_momentum):
    inner = lax.axis_size("fsdp") // PLANES
    rows, width = anchor.shape
    if inner != 4 or lax.axis_size("rep") != 2 or rows % 256 or width % 128:
        return general(acts, value_cots, inner_weights, first_moment, second_moment, anchor, outer_momentum)
    tokens = acts.shape[1]
    half = rows // 2

    def planes(x, bits):
        return lax.ppermute(x, "fsdp", [(p * inner + i, (p ^ bits) * inner + i) for p in range(PLANES) for i in range(inner)])

    def across(x, k):
        return lax.ppermute(x, "fsdp", [(p * inner + i, p * inner + (i ^ k)) for p in range(PLANES) for i in range(inner)])

    def around(blocks):
        return [blocks[0]] + [across(blocks[k], k) for k in range(1, inner)]

    def swap(x):
        return lax.ppermute(x, "rep", [(0, 1), (1, 0)])

    out = [jax.ShapeDtypeStruct((tokens, rows + width), jnp.bfloat16)] * inner
    sems = [pltpu.SemaphoreType.DMA((2 * inner,))]
    kernel = partial(pack_first_kernel, inner, rows)
    first = around(call(kernel, "pack", out, [acts[0], value_cots[0]], 0, sems, space=pltpu.HBM, moved=0, vmem=FIRST_VMEM_BYTES))

    def pack(blocks, after):
        out = [jax.ShapeDtypeStruct((tokens, len(blocks) * rows), jnp.bfloat16)] * inner
        return call(partial(pack_kernel, inner, rows, blocks), "pack", out, [acts[0]], 0, after=after)

    second = around(pack((2, 1), first[1:2]))
    full = jax.ShapeDtypeStruct((rows, width), jnp.float32)
    sent = jax.ShapeDtypeStruct((rows, width), jnp.bfloat16)

    def gradient(message, at, out, arrived=()):
        kernel = partial(gradient_kernel, inner, rows, at)
        flops = 2 * inner * tokens * rows * width
        return call(kernel, "gradient", [out], message + first + list(arrived), flops)[0]

    beside_far = planes(gradient(first, 0, sent), 1)
    beside = planes(gradient(second, rows, sent), 1)
    for_far = gradient(second, 0, sent, [beside_far])
    far = planes(for_far, 2)
    last = around(pack((0,), [for_far]))
    known = [gradient(last, 0, full), beside, far, inner_weights[0], first_moment[0], second_moment[0], anchor]
    half_block = jax.ShapeDtypeStruct((half, width), jnp.float32)
    (drift_out,) = call(drift_kernel, "drift", [half_block], known, 0)
    drift_in = swap(drift_out)
    first_next, drift = call(update_kernel, "update", [full, half_block], known, 0)
    new_half = jax.ShapeDtypeStruct((half, width), jnp.bfloat16)
    (mine,) = call(outer_kernel, "outer", [new_half], [drift, drift_in, anchor, outer_momentum], 0)
    mine2 = planes(mine, 2)
    mine1 = planes(mine, 1)
    mine3 = planes(mine2, 1)
    pieces = [y for x in (mine, mine1, mine2) for y in (x, swap(x))]
    flops = 2 * inner * tokens * rows * width
    (early,) = call(
        partial(early_values_kernel, inner, rows),
        "early_values",
        [jax.ShapeDtypeStruct((inner * tokens, width), jnp.float32)],
        last + second + pieces,
        3 * flops,
    )
    block = jax.ShapeDtypeStruct((tokens, width), jnp.bfloat16)
    own, *sums = call(
        partial(late_values_kernel, inner, rows),
        "late_values",
        [jax.ShapeDtypeStruct((tokens, width), jnp.float32)] + [block] * (inner - 1),
        [early] + first + [mine3, swap(mine3)],
        flops,
    )
    terms = [own] + [across(sums[k - 1], k) for k in range(1, inner)]
    (values,) = call(sum_kernel, "sum", [block], terms, 0)
    return (first_next[None], values[None])


def solution(mesh):
    placed = (
        P("rep", "fsdp", None),
        P("rep", "fsdp", None),
        P("rep", "fsdp", None),
        P("rep", "fsdp", None),
        P("rep", "fsdp", None),
        P("fsdp", None),
        P("fsdp", None),
    )
    return jax.shard_map(
        on_device,
        mesh=mesh,
        in_specs=placed,
        out_specs=(P("rep", "fsdp", None), P("rep", "fsdp", None)),
        check_vma=False,
    )
```

```python
from functools import partial

import jax
import jax.numpy as jnp
from jax import lax
from jax.experimental import pallas as pl
from jax.experimental.pallas import tpu as pltpu
from jax.sharding import PartitionSpec as P

decay_first = 0.9
decay_second = 0.95
inner_rate = 0.006
epsilon = 1e-08
outer_rate = 0.7
outer_decay = 0.9

PLANES = 4
CHUNK = 32
CONTRACT_ROWS = (((0,), (0,)), ((), ()))
VMEM_BYTES = 16 * 1024 * 1024


def outer_update(average, anchor_rows, momentum_rows):
    velocity = outer_decay * momentum_rows + average
    return (anchor_rows - outer_rate * (average + outer_decay * velocity)).astype(jnp.bfloat16)


def inner_update(gradient, inner_weights, first_moment, second_moment, anchor):
    first_next = decay_first * first_moment + (1.0 - decay_first) * gradient
    second_next = decay_second * second_moment + (1.0 - decay_second) * gradient * gradient
    stepped = inner_weights - inner_rate * first_next / (jnp.sqrt(second_next) + epsilon)
    return first_next, anchor - stepped


def general(acts, value_cots, inner_weights, first_moment, second_moment, anchor, outer_momentum):
    tokens_local = acts[0]
    columns = lax.all_to_all(tokens_local, "fsdp", split_axis=1, concat_axis=0, tiled=True)
    cots = lax.all_gather(value_cots[0], "fsdp", axis=0, tiled=True)
    gradient = lax.dot_general(columns, cots, CONTRACT_ROWS, preferred_element_type=jnp.float32)
    first_next, drift = inner_update(gradient, inner_weights[0], first_moment[0], second_moment[0], anchor)
    average = lax.psum(drift, "rep") / lax.axis_size("rep")
    weights_next = outer_update(average, anchor, outer_momentum)
    gathered = lax.all_gather(weights_next, "fsdp", axis=0, tiled=True)
    values = jnp.dot(tokens_local, gathered, preferred_element_type=jnp.float32)
    return (first_next[None], values.astype(jnp.bfloat16)[None])


def flip(at, bits):
    low = lax.rem(at, 2)
    return (at // 2 + bits // 2 - 2 * (at // 2) * (bits // 2)) * 2 + low + bits % 2 - 2 * low * (bits % 2)


def call(kernel, name, out, inputs, flops, scratch=(), after=()):
    moved = sum(x.size * x.dtype.itemsize for x in list(inputs) + list(out))
    count = len(inputs)

    def without_after(*refs):
        kernel(*refs[:count], *refs[count + len(after) :])

    return pl.pallas_call(
        without_after,
        out_shape=out,
        in_specs=[pl.BlockSpec(memory_space=pltpu.VMEM)] * count + [pl.BlockSpec(memory_space=pl.ANY)] * len(after),
        out_specs=[pl.BlockSpec(memory_space=pltpu.VMEM)] * len(out),
        scratch_shapes=list(scratch),
        compiler_params=pltpu.CompilerParams(vmem_limit_bytes=VMEM_BYTES),
        cost_estimate=pl.CostEstimate(flops=flops, bytes_accessed=moved, transcendentals=0),
        name=name,
    )(*inputs, *after)


def block_start(inner, rows, bits, k):
    f = lax.axis_index("fsdp")
    return pl.multiple_of((flip(f // inner, bits) * inner + flip(lax.rem(f, inner), k)) * rows, rows)


def pack_first_kernel(inner, rows, acts_ref, cots_ref, *outs):
    for k in range(inner):
        outs[k][:, :rows] = acts_ref[:, pl.ds(block_start(inner, rows, 3, k), rows)]
        outs[k][:, rows:] = cots_ref[...]


def pack_kernel(inner, rows, blocks, acts_ref, *outs):
    for k in range(inner):
        for slot, bits in enumerate(blocks):
            outs[k][:, slot * rows : (slot + 1) * rows] = acts_ref[:, pl.ds(block_start(inner, rows, bits, k), rows)]


def gradient_kernel(inner, rows, acts_at, *refs):
    acts_refs, cots_refs, arrived, out = refs[:inner], refs[inner : 2 * inner], refs[2 * inner : -1], refs[-1]
    columns = jnp.concatenate([ref[:, acts_at : acts_at + rows] for ref in acts_refs], axis=0)
    cots = jnp.concatenate([ref[:, rows:] for ref in cots_refs], axis=0)
    total = lax.dot_general(columns, cots, CONTRACT_ROWS, preferred_element_type=jnp.float32)
    for ref in arrived:
        total += ref[...].astype(jnp.float32)
    out[...] = total.astype(out.dtype)


def gradient_at(at, refs):
    total, beside, far = refs
    return total[at, :] + beside[at, :].astype(jnp.float32) + far[at, :].astype(jnp.float32)


def steps(half, which, body):
    @pl.loop(0, half // CHUNK)
    def _(step):
        start = pl.multiple_of(step * CHUNK, CHUNK)
        body(pl.ds(start, CHUNK), pl.ds(pl.multiple_of(which * half + start, CHUNK), CHUNK))


def drift_kernel(*refs):
    gradient_refs, (weights, first, second, anchor), drift_ref = refs[:3], refs[3:7], refs[7]

    def body(here, at):
        gradient = gradient_at(at, gradient_refs)
        state = (weights[at, :], first[at, :], second[at, :], anchor[at, :])
        drift_ref[here, :] = inner_update(gradient, *state)[1]

    steps(drift_ref.shape[0], 1 - lax.axis_index("rep"), body)


def update_kernel(*refs):
    gradient_refs, (weights, first, second, anchor), (first_ref, drift_ref) = refs[:3], refs[3:7], refs[7:]
    half = drift_ref.shape[0]
    r = lax.axis_index("rep")

    def body(here, at):
        gradient = gradient_at(at, gradient_refs)
        state = (weights[at, :], first[at, :], second[at, :], anchor[at, :])
        first_ref[at, :], drift_ref[here, :] = inner_update(gradient, *state)

    def others(here, at):
        first_ref[at, :] = decay_first * first[at, :] + (1.0 - decay_first) * gradient_at(at, gradient_refs)

    steps(half, r, body)
    steps(half, 1 - r, others)


def outer_kernel(drift, other, anchor, momentum, out):
    half = out.shape[0]
    at = pl.ds(pl.multiple_of(lax.axis_index("rep") * half, half), half)
    out[...] = outer_update((drift[...] + other[...]) / 2, anchor[at, :], momentum[at, :])


def product(messages, rows, pieces):
    r = lax.axis_index("rep")
    half = rows // 2
    total = 0.0
    for (blocks, start), (mine, other) in zip(messages, pieces):
        for which, piece in ((r, mine), (1 - r, other)):
            at = pl.ds(pl.multiple_of(start + which * half, half), half)
            columns = jnp.concatenate([block[:, at] for block in blocks], axis=0)
            total += jnp.dot(columns, piece[...], preferred_element_type=jnp.float32)
    return total


def paired(refs):
    return [(refs[2 * n], refs[2 * n + 1]) for n in range(len(refs) // 2)]


def early_values_kernel(inner, rows, *refs):
    own, both = refs[:inner], refs[inner : 2 * inner]
    refs[-1][...] = product([(own, 0), (both, rows), (both, 0)], rows, paired(refs[2 * inner : -1]))


def late_values_kernel(inner, rows, early, *refs):
    tokens = early.shape[0] // inner
    total = early[...] + product([(refs[:inner], 0)], rows, [refs[inner : inner + 2]])
    for k, out in enumerate(refs[inner + 2 :]):
        out[...] = total[k * tokens : (k + 1) * tokens].astype(out.dtype)


def sum_kernel(*refs):
    total = refs[0][...]
    for ref in refs[1:-1]:
        total += ref[...].astype(jnp.float32)
    refs[-1][...] = total.astype(refs[-1].dtype)


def on_device(acts, value_cots, inner_weights, first_moment, second_moment, anchor, outer_momentum):
    inner = lax.axis_size("fsdp") // PLANES
    rows, width = anchor.shape
    if inner != 4 or lax.axis_size("rep") != 2 or rows % 256 or width % 128:
        return general(acts, value_cots, inner_weights, first_moment, second_moment, anchor, outer_momentum)
    tokens = acts.shape[1]
    half = rows // 2

    def planes(x, bits):
        return lax.ppermute(x, "fsdp", [(p * inner + i, (p ^ bits) * inner + i) for p in range(PLANES) for i in range(inner)])

    def across(x, k):
        return lax.ppermute(x, "fsdp", [(p * inner + i, p * inner + (i ^ k)) for p in range(PLANES) for i in range(inner)])

    def around(blocks):
        return [blocks[0]] + [across(blocks[k], k) for k in range(1, inner)]

    def swap(x):
        return lax.ppermute(x, "rep", [(0, 1), (1, 0)])

    out = [jax.ShapeDtypeStruct((tokens, rows + width), jnp.bfloat16)] * inner
    first = around(call(partial(pack_first_kernel, inner, rows), "pack", out, [acts[0], value_cots[0]], 0))

    def pack(blocks, after):
        out = [jax.ShapeDtypeStruct((tokens, len(blocks) * rows), jnp.bfloat16)] * inner
        return call(partial(pack_kernel, inner, rows, blocks), "pack", out, [acts[0]], 0, after=after)

    second = around(pack((2, 1), first[1:2]))
    full = jax.ShapeDtypeStruct((rows, width), jnp.float32)
    sent = jax.ShapeDtypeStruct((rows, width), jnp.bfloat16)

    def gradient(message, at, out, arrived=()):
        kernel = partial(gradient_kernel, inner, rows, at)
        flops = 2 * inner * tokens * rows * width
        return call(kernel, "gradient", [out], message + first + list(arrived), flops)[0]

    beside_far = planes(gradient(first, 0, sent), 1)
    beside = planes(gradient(second, rows, sent), 1)
    for_far = gradient(second, 0, sent, [beside_far])
    far = planes(for_far, 2)
    last = around(pack((0,), [for_far]))
    known = [gradient(last, 0, full), beside, far, inner_weights[0], first_moment[0], second_moment[0], anchor]
    half_block = jax.ShapeDtypeStruct((half, width), jnp.float32)
    (drift_out,) = call(drift_kernel, "drift", [half_block], known, 0)
    drift_in = swap(drift_out)
    first_next, drift = call(update_kernel, "update", [full, half_block], known, 0)
    new_half = jax.ShapeDtypeStruct((half, width), jnp.bfloat16)
    (mine,) = call(outer_kernel, "outer", [new_half], [drift, drift_in, anchor, outer_momentum], 0)
    mine2 = planes(mine, 2)
    mine1 = planes(mine, 1)
    mine3 = planes(mine2, 1)
    pieces = [y for x in (mine, mine1, mine2) for y in (x, swap(x))]
    flops = 2 * inner * tokens * rows * width
    (early,) = call(
        partial(early_values_kernel, inner, rows),
        "early_values",
        [jax.ShapeDtypeStruct((inner * tokens, width), jnp.float32)],
        last + second + pieces,
        3 * flops,
    )
    block = jax.ShapeDtypeStruct((tokens, width), jnp.bfloat16)
    own, *sums = call(
        partial(late_values_kernel, inner, rows),
        "late_values",
        [jax.ShapeDtypeStruct((tokens, width), jnp.float32)] + [block] * (inner - 1),
        [early] + first + [mine3, swap(mine3)],
        flops,
    )
    terms = [own] + [across(sums[k - 1], k) for k in range(1, inner)]
    (values,) = call(sum_kernel, "sum", [block], terms, 0)
    return (first_next[None], values[None])


def solution(mesh):
    placed = (
        P("rep", "fsdp", None),
        P("rep", "fsdp", None),
        P("rep", "fsdp", None),
        P("rep", "fsdp", None),
        P("rep", "fsdp", None),
        P("fsdp", None),
        P("fsdp", None),
    )
    return jax.shard_map(
        on_device,
        mesh=mesh,
        in_specs=placed,
        out_specs=(P("rep", "fsdp", None), P("rep", "fsdp", None)),
        check_vma=False,
    )
```

```python
from functools import partial

import jax
import jax.numpy as jnp
from jax import lax
from jax.experimental import pallas as pl
from jax.experimental.pallas import tpu as pltpu
from jax.sharding import PartitionSpec as P

decay_first = 0.9
decay_second = 0.95
inner_rate = 0.006
epsilon = 1e-08
outer_rate = 0.7
outer_decay = 0.9

PLANES = 4
CHUNK = 32
CONTRACT_ROWS = (((0,), (0,)), ((), ()))
AHEAD_FLOPS = 10**10
VMEM_BYTES = 16 * 1024 * 1024


def outer_update(average, anchor_rows, momentum_rows):
    velocity = outer_decay * momentum_rows + average
    return (anchor_rows - outer_rate * (average + outer_decay * velocity)).astype(jnp.bfloat16)


def inner_update(gradient, inner_weights, first_moment, second_moment, anchor):
    first_next = decay_first * first_moment + (1.0 - decay_first) * gradient
    second_next = decay_second * second_moment + (1.0 - decay_second) * gradient * gradient
    stepped = inner_weights - inner_rate * first_next / (jnp.sqrt(second_next) + epsilon)
    return first_next, anchor - stepped


def general(acts, value_cots, inner_weights, first_moment, second_moment, anchor, outer_momentum):
    tokens_local = acts[0]
    columns = lax.all_to_all(tokens_local, "fsdp", split_axis=1, concat_axis=0, tiled=True)
    cots = lax.all_gather(value_cots[0], "fsdp", axis=0, tiled=True)
    gradient = lax.dot_general(columns, cots, CONTRACT_ROWS, preferred_element_type=jnp.float32)
    first_next, drift = inner_update(gradient, inner_weights[0], first_moment[0], second_moment[0], anchor)
    average = lax.psum(drift, "rep") / lax.axis_size("rep")
    weights_next = outer_update(average, anchor, outer_momentum)
    gathered = lax.all_gather(weights_next, "fsdp", axis=0, tiled=True)
    values = jnp.dot(tokens_local, gathered, preferred_element_type=jnp.float32)
    return (first_next[None], values.astype(jnp.bfloat16)[None])


def flip(at, bits):
    low = lax.rem(at, 2)
    return (at // 2 + bits // 2 - 2 * (at // 2) * (bits // 2)) * 2 + low + bits % 2 - 2 * low * (bits % 2)


def call(kernel, name, out, inputs, flops, scratch=(), after=()):
    moved = sum(x.size * x.dtype.itemsize for x in list(inputs) + list(out))
    count = len(inputs)

    def without_after(*refs):
        kernel(*refs[:count], *refs[count + len(after) :])

    return pl.pallas_call(
        without_after,
        out_shape=out,
        in_specs=[pl.BlockSpec(memory_space=pltpu.VMEM)] * count + [pl.BlockSpec(memory_space=pl.ANY)] * len(after),
        out_specs=[pl.BlockSpec(memory_space=pltpu.VMEM)] * len(out),
        scratch_shapes=list(scratch),
        compiler_params=pltpu.CompilerParams(vmem_limit_bytes=VMEM_BYTES),
        cost_estimate=pl.CostEstimate(flops=flops, bytes_accessed=moved, transcendentals=0),
        name=name,
    )(*inputs, *after)


def block_start(inner, rows, bits, k):
    f = lax.axis_index("fsdp")
    return pl.multiple_of((flip(f // inner, bits) * inner + flip(lax.rem(f, inner), k)) * rows, rows)


def pack_first_kernel(inner, rows, acts_ref, cots_ref, *outs):
    for k in range(inner):
        outs[k][:, :rows] = acts_ref[:, pl.ds(block_start(inner, rows, 3, k), rows)]
        outs[k][:, rows:] = cots_ref[...]


def pack_kernel(inner, rows, blocks, acts_ref, *outs):
    for k in range(inner):
        for slot, bits in enumerate(blocks):
            outs[k][:, slot * rows : (slot + 1) * rows] = acts_ref[:, pl.ds(block_start(inner, rows, bits, k), rows)]


def gradient_kernel(inner, rows, acts_at, *refs):
    acts_refs, cots_refs, arrived, out = refs[:inner], refs[inner : 2 * inner], refs[2 * inner : -1], refs[-1]
    columns = jnp.concatenate([ref[:, acts_at : acts_at + rows] for ref in acts_refs], axis=0)
    cots = jnp.concatenate([ref[:, rows:] for ref in cots_refs], axis=0)
    total = lax.dot_general(columns, cots, CONTRACT_ROWS, preferred_element_type=jnp.float32)
    for ref in arrived:
        total += ref[...].astype(jnp.float32)
    out[...] = total.astype(out.dtype)


def gradient_at(at, refs):
    total, beside, far = refs
    return total[at, :] + beside[at, :].astype(jnp.float32) + far[at, :].astype(jnp.float32)


def steps(half, which, body):
    @pl.loop(0, half // CHUNK)
    def _(step):
        start = pl.multiple_of(step * CHUNK, CHUNK)
        body(pl.ds(start, CHUNK), pl.ds(pl.multiple_of(which * half + start, CHUNK), CHUNK))


def drift_kernel(*refs):
    gradient_refs, (weights, first, second, anchor), drift_ref = refs[:3], refs[3:7], refs[7]

    def body(here, at):
        gradient = gradient_at(at, gradient_refs)
        state = (weights[at, :], first[at, :], second[at, :], anchor[at, :])
        drift_ref[here, :] = inner_update(gradient, *state)[1]

    steps(drift_ref.shape[0], 1 - lax.axis_index("rep"), body)


def update_kernel(*refs):
    gradient_refs, (weights, first, second, anchor), (first_ref, drift_ref) = refs[:3], refs[3:7], refs[7:]
    half = drift_ref.shape[0]
    r = lax.axis_index("rep")

    def body(here, at):
        gradient = gradient_at(at, gradient_refs)
        state = (weights[at, :], first[at, :], second[at, :], anchor[at, :])
        first_ref[at, :], drift_ref[here, :] = inner_update(gradient, *state)

    def others(here, at):
        first_ref[at, :] = decay_first * first[at, :] + (1.0 - decay_first) * gradient_at(at, gradient_refs)

    steps(half, r, body)
    steps(half, 1 - r, others)


def outer_kernel(drift, other, anchor, momentum, out):
    half = out.shape[0]
    at = pl.ds(pl.multiple_of(lax.axis_index("rep") * half, half), half)
    out[...] = outer_update((drift[...] + other[...]) / 2, anchor[at, :], momentum[at, :])


def product(messages, rows, pieces):
    r = lax.axis_index("rep")
    half = rows // 2
    total = 0.0
    for (blocks, start), (mine, other) in zip(messages, pieces):
        for which, piece in ((r, mine), (1 - r, other)):
            at = pl.ds(pl.multiple_of(start + which * half, half), half)
            columns = jnp.concatenate([block[:, at] for block in blocks], axis=0)
            total += jnp.dot(columns, piece[...], preferred_element_type=jnp.float32)
    return total


def paired(refs):
    return [(refs[2 * n], refs[2 * n + 1]) for n in range(len(refs) // 2)]


def early_values_kernel(inner, rows, *refs):
    own, both = refs[:inner], refs[inner : 2 * inner]
    refs[-1][...] = product([(own, 0), (both, rows), (both, 0)], rows, paired(refs[2 * inner : -1]))


def late_values_kernel(inner, rows, early, *refs):
    tokens = early.shape[0] // inner
    total = early[...] + product([(refs[:inner], 0)], rows, [refs[inner : inner + 2]])
    for k, out in enumerate(refs[inner + 2 :]):
        out[...] = total[k * tokens : (k + 1) * tokens].astype(out.dtype)


def sum_kernel(*refs):
    total = refs[0][...]
    for ref in refs[1:-1]:
        total += ref[...].astype(jnp.float32)
    refs[-1][...] = total.astype(refs[-1].dtype)


def on_device(acts, value_cots, inner_weights, first_moment, second_moment, anchor, outer_momentum):
    inner = lax.axis_size("fsdp") // PLANES
    rows, width = anchor.shape
    if inner != 4 or lax.axis_size("rep") != 2 or rows % 256 or width % 128:
        return general(acts, value_cots, inner_weights, first_moment, second_moment, anchor, outer_momentum)
    tokens = acts.shape[1]
    half = rows // 2

    def planes(x, bits):
        return lax.ppermute(x, "fsdp", [(p * inner + i, (p ^ bits) * inner + i) for p in range(PLANES) for i in range(inner)])

    def across(x, k):
        return lax.ppermute(x, "fsdp", [(p * inner + i, p * inner + (i ^ k)) for p in range(PLANES) for i in range(inner)])

    def around(blocks):
        return [blocks[0]] + [across(blocks[k], k) for k in range(1, inner)]

    def swap(x):
        return lax.ppermute(x, "rep", [(0, 1), (1, 0)])

    out = [jax.ShapeDtypeStruct((tokens, rows + width), jnp.bfloat16)] * inner
    first = around(call(partial(pack_first_kernel, inner, rows), "pack", out, [acts[0], value_cots[0]], 0))

    def pack(blocks, after):
        out = [jax.ShapeDtypeStruct((tokens, len(blocks) * rows), jnp.bfloat16)] * inner
        return call(partial(pack_kernel, inner, rows, blocks), "pack", out, [acts[0]], 0, after=after)

    second = around(pack((2, 1), first[1:2]))
    full = jax.ShapeDtypeStruct((rows, width), jnp.float32)
    sent = jax.ShapeDtypeStruct((rows, width), jnp.bfloat16)

    def gradient(message, at, out, arrived=(), flops=2 * inner * tokens * rows * width):
        kernel = partial(gradient_kernel, inner, rows, at)
        return call(kernel, "gradient", [out], message + first + list(arrived), flops)[0]

    beside_far = planes(gradient(first, 0, sent), 1)
    beside = planes(gradient(second, rows, sent, flops=AHEAD_FLOPS), 1)
    for_far = gradient(second, 0, sent, [beside_far])
    far = planes(for_far, 2)
    last = around(pack((0,), [for_far]))
    known = [gradient(last, 0, full), beside, far, inner_weights[0], first_moment[0], second_moment[0], anchor]
    half_block = jax.ShapeDtypeStruct((half, width), jnp.float32)
    (drift_out,) = call(drift_kernel, "drift", [half_block], known, 0)
    drift_in = swap(drift_out)
    first_next, drift = call(update_kernel, "update", [full, half_block], known, 0)
    new_half = jax.ShapeDtypeStruct((half, width), jnp.bfloat16)
    (mine,) = call(outer_kernel, "outer", [new_half], [drift, drift_in, anchor, outer_momentum], 0)
    mine2 = planes(mine, 2)
    mine1 = planes(mine, 1)
    mine3 = planes(mine2, 1)
    pieces = [y for x in (mine, mine1, mine2) for y in (x, swap(x))]
    flops = 2 * inner * tokens * rows * width
    (early,) = call(
        partial(early_values_kernel, inner, rows),
        "early_values",
        [jax.ShapeDtypeStruct((inner * tokens, width), jnp.float32)],
        last + second + pieces,
        3 * flops,
    )
    block = jax.ShapeDtypeStruct((tokens, width), jnp.bfloat16)
    own, *sums = call(
        partial(late_values_kernel, inner, rows),
        "late_values",
        [jax.ShapeDtypeStruct((tokens, width), jnp.float32)] + [block] * (inner - 1),
        [early] + first + [mine3, swap(mine3)],
        flops,
    )
    terms = [own] + [across(sums[k - 1], k) for k in range(1, inner)]
    (values,) = call(sum_kernel, "sum", [block], terms, 0)
    return (first_next[None], values[None])


def solution(mesh):
    placed = (
        P("rep", "fsdp", None),
        P("rep", "fsdp", None),
        P("rep", "fsdp", None),
        P("rep", "fsdp", None),
        P("rep", "fsdp", None),
        P("fsdp", None),
        P("fsdp", None),
    )
    return jax.shard_map(
        on_device,
        mesh=mesh,
        in_specs=placed,
        out_specs=(P("rep", "fsdp", None), P("rep", "fsdp", None)),
        check_vma=False,
    )
```

```python
from functools import partial

import jax
import jax.numpy as jnp
from jax import lax
from jax.experimental import pallas as pl
from jax.experimental.pallas import tpu as pltpu
from jax.sharding import PartitionSpec as P

decay_first = 0.9
decay_second = 0.95
inner_rate = 0.006
epsilon = 1e-08
outer_rate = 0.7
outer_decay = 0.9

PLANES = 4
CHUNK = 32
CONTRACT_ROWS = (((0,), (0,)), ((), ()))
VMEM_BYTES = 16 * 1024 * 1024


def outer_update(average, anchor_rows, momentum_rows):
    velocity = outer_decay * momentum_rows + average
    return (anchor_rows - outer_rate * (average + outer_decay * velocity)).astype(jnp.bfloat16)


def inner_update(gradient, inner_weights, first_moment, second_moment, anchor):
    first_next = decay_first * first_moment + (1.0 - decay_first) * gradient
    second_next = decay_second * second_moment + (1.0 - decay_second) * gradient * gradient
    stepped = inner_weights - inner_rate * first_next / (jnp.sqrt(second_next) + epsilon)
    return first_next, anchor - stepped


def general(acts, value_cots, inner_weights, first_moment, second_moment, anchor, outer_momentum):
    tokens_local = acts[0]
    columns = lax.all_to_all(tokens_local, "fsdp", split_axis=1, concat_axis=0, tiled=True)
    cots = lax.all_gather(value_cots[0], "fsdp", axis=0, tiled=True)
    gradient = lax.dot_general(columns, cots, CONTRACT_ROWS, preferred_element_type=jnp.float32)
    first_next, drift = inner_update(gradient, inner_weights[0], first_moment[0], second_moment[0], anchor)
    average = lax.psum(drift, "rep") / lax.axis_size("rep")
    weights_next = outer_update(average, anchor, outer_momentum)
    gathered = lax.all_gather(weights_next, "fsdp", axis=0, tiled=True)
    values = jnp.dot(tokens_local, gathered, preferred_element_type=jnp.float32)
    return (first_next[None], values.astype(jnp.bfloat16)[None])


def flip(at, bits):
    low = lax.rem(at, 2)
    return (at // 2 + bits // 2 - 2 * (at // 2) * (bits // 2)) * 2 + low + bits % 2 - 2 * low * (bits % 2)


def call(kernel, name, out, inputs, flops, scratch=(), after=()):
    moved = sum(x.size * x.dtype.itemsize for x in list(inputs) + list(out))
    count = len(inputs)

    def without_after(*refs):
        kernel(*refs[:count], *refs[count + len(after) :])

    return pl.pallas_call(
        without_after,
        out_shape=out,
        in_specs=[pl.BlockSpec(memory_space=pltpu.VMEM)] * count + [pl.BlockSpec(memory_space=pl.ANY)] * len(after),
        out_specs=[pl.BlockSpec(memory_space=pltpu.VMEM)] * len(out),
        scratch_shapes=list(scratch),
        compiler_params=pltpu.CompilerParams(vmem_limit_bytes=VMEM_BYTES),
        cost_estimate=pl.CostEstimate(flops=flops, bytes_accessed=moved, transcendentals=0),
        name=name,
    )(*inputs, *after)


def block_start(inner, rows, bits, k):
    f = lax.axis_index("fsdp")
    return pl.multiple_of((flip(f // inner, bits) * inner + flip(lax.rem(f, inner), k)) * rows, rows)


def pack_first_kernel(inner, rows, acts_ref, cots_ref, *outs):
    for k in range(inner):
        outs[k][:, :rows] = acts_ref[:, pl.ds(block_start(inner, rows, 3, k), rows)]
        outs[k][:, rows:] = cots_ref[...]


def pack_kernel(inner, rows, blocks, acts_ref, *outs):
    for k in range(inner):
        for slot, bits in enumerate(blocks):
            outs[k][:, slot * rows : (slot + 1) * rows] = acts_ref[:, pl.ds(block_start(inner, rows, bits, k), rows)]


def gradient_kernel(inner, rows, acts_at, arrived, *refs):
    acts_refs, cots_refs, refs = refs[:inner], refs[inner : 2 * inner], refs[2 * inner :]
    columns = jnp.concatenate([ref[:, acts_at : acts_at + rows] for ref in acts_refs], axis=0)
    cots = jnp.concatenate([ref[:, rows:] for ref in cots_refs], axis=0)
    total = lax.dot_general(columns, cots, CONTRACT_ROWS, preferred_element_type=jnp.float32)
    for ref in refs[:arrived]:
        total += ref[...].astype(jnp.float32)
    at = 0
    for out in refs[arrived:]:
        out[...] = total[:, at : at + out.shape[1]].astype(out.dtype)
        at += out.shape[1]


def gradient_at(at, refs):
    total, far, *beside = refs
    beside = jnp.concatenate([ref[at, :].astype(jnp.float32) for ref in beside], axis=1)
    return total[at, :] + beside + far[at, :].astype(jnp.float32)


def steps(half, which, body):
    @pl.loop(0, half // CHUNK)
    def _(step):
        start = pl.multiple_of(step * CHUNK, CHUNK)
        body(pl.ds(start, CHUNK), pl.ds(pl.multiple_of(which * half + start, CHUNK), CHUNK))


def drift_kernel(*refs):
    gradient_refs, (weights, first, second, anchor), drift_ref = refs[:-5], refs[-5:-1], refs[-1]

    def body(here, at):
        gradient = gradient_at(at, gradient_refs)
        state = (weights[at, :], first[at, :], second[at, :], anchor[at, :])
        drift_ref[here, :] = inner_update(gradient, *state)[1]

    steps(drift_ref.shape[0], 1 - lax.axis_index("rep"), body)


def update_kernel(*refs):
    gradient_refs, (weights, first, second, anchor), (first_ref, drift_ref) = refs[:-6], refs[-6:-2], refs[-2:]
    half = drift_ref.shape[0]
    r = lax.axis_index("rep")

    def body(here, at):
        gradient = gradient_at(at, gradient_refs)
        state = (weights[at, :], first[at, :], second[at, :], anchor[at, :])
        first_ref[at, :], drift_ref[here, :] = inner_update(gradient, *state)

    def others(here, at):
        first_ref[at, :] = decay_first * first[at, :] + (1.0 - decay_first) * gradient_at(at, gradient_refs)

    steps(half, r, body)
    steps(half, 1 - r, others)


def outer_kernel(drift, other, anchor, momentum, out):
    half = out.shape[0]
    at = pl.ds(pl.multiple_of(lax.axis_index("rep") * half, half), half)
    out[...] = outer_update((drift[...] + other[...]) / 2, anchor[at, :], momentum[at, :])


def product(messages, rows, pieces):
    r = lax.axis_index("rep")
    half = rows // 2
    total = 0.0
    for (blocks, start), (mine, other) in zip(messages, pieces):
        for which, piece in ((r, mine), (1 - r, other)):
            at = pl.ds(pl.multiple_of(start + which * half, half), half)
            columns = jnp.concatenate([block[:, at] for block in blocks], axis=0)
            total += jnp.dot(columns, piece[...], preferred_element_type=jnp.float32)
    return total


def paired(refs):
    return [(refs[2 * n], refs[2 * n + 1]) for n in range(len(refs) // 2)]


def early_values_kernel(inner, rows, *refs):
    own, both = refs[:inner], refs[inner : 2 * inner]
    refs[-1][...] = product([(own, 0), (both, rows), (both, 0)], rows, paired(refs[2 * inner : -1]))


def late_values_kernel(inner, rows, early, *refs):
    tokens = early.shape[0] // inner
    total = early[...] + product([(refs[:inner], 0)], rows, [refs[inner : inner + 2]])
    for k, out in enumerate(refs[inner + 2 :]):
        out[...] = total[k * tokens : (k + 1) * tokens].astype(out.dtype)


def sum_kernel(*refs):
    total = refs[0][...]
    for ref in refs[1:-1]:
        total += ref[...].astype(jnp.float32)
    refs[-1][...] = total.astype(refs[-1].dtype)


def on_device(acts, value_cots, inner_weights, first_moment, second_moment, anchor, outer_momentum):
    inner = lax.axis_size("fsdp") // PLANES
    rows, width = anchor.shape
    if inner != 4 or lax.axis_size("rep") != 2 or rows % 256 or width % 256:
        return general(acts, value_cots, inner_weights, first_moment, second_moment, anchor, outer_momentum)
    tokens = acts.shape[1]
    half = rows // 2

    def planes(x, bits):
        return lax.ppermute(x, "fsdp", [(p * inner + i, (p ^ bits) * inner + i) for p in range(PLANES) for i in range(inner)])

    def across(x, k):
        return lax.ppermute(x, "fsdp", [(p * inner + i, p * inner + (i ^ k)) for p in range(PLANES) for i in range(inner)])

    def around(blocks):
        return [blocks[0]] + [across(blocks[k], k) for k in range(1, inner)]

    def swap(x):
        return lax.ppermute(x, "rep", [(0, 1), (1, 0)])

    out = [jax.ShapeDtypeStruct((tokens, rows + width), jnp.bfloat16)] * inner
    first = around(call(partial(pack_first_kernel, inner, rows), "pack", out, [acts[0], value_cots[0]], 0))

    def pack(blocks, after):
        out = [jax.ShapeDtypeStruct((tokens, len(blocks) * rows), jnp.bfloat16)] * inner
        return call(partial(pack_kernel, inner, rows, blocks), "pack", out, [acts[0]], 0, after=after)

    second = around(pack((2, 1), first[1:2]))
    full = jax.ShapeDtypeStruct((rows, width), jnp.float32)
    sent = jax.ShapeDtypeStruct((rows, width), jnp.bfloat16)

    def gradient(message, at, out, arrived=(), after=()):
        kernel = partial(gradient_kernel, inner, rows, at, len(arrived))
        flops = 2 * inner * tokens * rows * width
        return call(kernel, "gradient", out, message + first + list(arrived), flops, after=after)

    piece = jax.ShapeDtypeStruct((rows, width // 2), jnp.bfloat16)
    beside_far = planes(gradient(first, 0, [sent])[0], 1)
    (for_far,) = gradient(second, 0, [sent], [beside_far])
    far = planes(for_far, 2)
    for_beside = gradient(second, rows, [piece] * 2, after=[for_far])
    beside = [planes(x, 1) for x in for_beside]
    last = around(pack((0,), for_beside[:1]))
    known = [gradient(last, 0, [full])[0], far, *beside, inner_weights[0], first_moment[0], second_moment[0], anchor]
    half_block = jax.ShapeDtypeStruct((half, width), jnp.float32)
    (drift_out,) = call(drift_kernel, "drift", [half_block], known, 0)
    drift_in = swap(drift_out)
    first_next, drift = call(update_kernel, "update", [full, half_block], known, 0)
    new_half = jax.ShapeDtypeStruct((half, width), jnp.bfloat16)
    (mine,) = call(outer_kernel, "outer", [new_half], [drift, drift_in, anchor, outer_momentum], 0)
    mine2 = planes(mine, 2)
    mine1 = planes(mine, 1)
    mine3 = planes(mine2, 1)
    pieces = [y for x in (mine, mine1, mine2) for y in (x, swap(x))]
    flops = 2 * inner * tokens * rows * width
    (early,) = call(
        partial(early_values_kernel, inner, rows),
        "early_values",
        [jax.ShapeDtypeStruct((inner * tokens, width), jnp.float32)],
        last + second + pieces,
        3 * flops,
    )
    block = jax.ShapeDtypeStruct((tokens, width), jnp.bfloat16)
    own, *sums = call(
        partial(late_values_kernel, inner, rows),
        "late_values",
        [jax.ShapeDtypeStruct((tokens, width), jnp.float32)] + [block] * (inner - 1),
        [early] + first + [mine3, swap(mine3)],
        flops,
    )
    terms = [own] + [across(sums[k - 1], k) for k in range(1, inner)]
    (values,) = call(sum_kernel, "sum", [block], terms, 0)
    return (first_next[None], values[None])


def solution(mesh):
    placed = (
        P("rep", "fsdp", None),
        P("rep", "fsdp", None),
        P("rep", "fsdp", None),
        P("rep", "fsdp", None),
        P("rep", "fsdp", None),
        P("fsdp", None),
        P("fsdp", None),
    )
    return jax.shard_map(
        on_device,
        mesh=mesh,
        in_specs=placed,
        out_specs=(P("rep", "fsdp", None), P("rep", "fsdp", None)),
        check_vma=False,
    )
```

```python
from functools import partial

import jax
import jax.numpy as jnp
from jax import lax
from jax.experimental import pallas as pl
from jax.experimental.pallas import tpu as pltpu
from jax.sharding import PartitionSpec as P

decay_first = 0.9
decay_second = 0.95
inner_rate = 0.006
epsilon = 1e-08
outer_rate = 0.7
outer_decay = 0.9

PLANES = 4
CHUNK = 32
CONTRACT_ROWS = (((0,), (0,)), ((), ()))
VMEM_BYTES = 16 * 1024 * 1024


def outer_update(average, anchor_rows, momentum_rows):
    velocity = outer_decay * momentum_rows + average
    return (anchor_rows - outer_rate * (average + outer_decay * velocity)).astype(jnp.bfloat16)


def inner_update(gradient, inner_weights, first_moment, second_moment, anchor):
    first_next = decay_first * first_moment + (1.0 - decay_first) * gradient
    second_next = decay_second * second_moment + (1.0 - decay_second) * gradient * gradient
    stepped = inner_weights - inner_rate * first_next / (jnp.sqrt(second_next) + epsilon)
    return first_next, anchor - stepped


def general(acts, value_cots, inner_weights, first_moment, second_moment, anchor, outer_momentum):
    tokens_local = acts[0]
    columns = lax.all_to_all(tokens_local, "fsdp", split_axis=1, concat_axis=0, tiled=True)
    cots = lax.all_gather(value_cots[0], "fsdp", axis=0, tiled=True)
    gradient = lax.dot_general(columns, cots, CONTRACT_ROWS, preferred_element_type=jnp.float32)
    first_next, drift = inner_update(gradient, inner_weights[0], first_moment[0], second_moment[0], anchor)
    average = lax.psum(drift, "rep") / lax.axis_size("rep")
    weights_next = outer_update(average, anchor, outer_momentum)
    gathered = lax.all_gather(weights_next, "fsdp", axis=0, tiled=True)
    values = jnp.dot(tokens_local, gathered, preferred_element_type=jnp.float32)
    return (first_next[None], values.astype(jnp.bfloat16)[None])


def flip(at, bits):
    low = lax.rem(at, 2)
    return (at // 2 + bits // 2 - 2 * (at // 2) * (bits // 2)) * 2 + low + bits % 2 - 2 * low * (bits % 2)


def call(kernel, name, out, inputs, flops, scratch=(), after=()):
    moved = sum(x.size * x.dtype.itemsize for x in list(inputs) + list(out))
    count = len(inputs)

    def without_after(*refs):
        kernel(*refs[:count], *refs[count + len(after) :])

    return pl.pallas_call(
        without_after,
        out_shape=out,
        in_specs=[pl.BlockSpec(memory_space=pltpu.VMEM)] * count + [pl.BlockSpec(memory_space=pl.ANY)] * len(after),
        out_specs=[pl.BlockSpec(memory_space=pltpu.VMEM)] * len(out),
        scratch_shapes=list(scratch),
        compiler_params=pltpu.CompilerParams(vmem_limit_bytes=VMEM_BYTES),
        cost_estimate=pl.CostEstimate(flops=flops, bytes_accessed=moved, transcendentals=0),
        name=name,
    )(*inputs, *after)


def block_start(inner, rows, bits, k):
    f = lax.axis_index("fsdp")
    return pl.multiple_of((flip(f // inner, bits) * inner + flip(lax.rem(f, inner), k)) * rows, rows)


def pack_first_kernel(inner, rows, acts_ref, cots_ref, *outs):
    for k in range(inner):
        outs[k][:, :rows] = acts_ref[:, pl.ds(block_start(inner, rows, 3, k), rows)]
        outs[k][:, rows:] = cots_ref[...]


def pack_kernel(inner, rows, blocks, acts_ref, *outs):
    for k in range(inner):
        for slot, bits in enumerate(blocks):
            outs[k][:, slot * rows : (slot + 1) * rows] = acts_ref[:, pl.ds(block_start(inner, rows, bits, k), rows)]


def gradient_kernel(inner, rows, acts_at, *refs):
    acts_refs, cots_refs, arrived, out = refs[:inner], refs[inner : 2 * inner], refs[2 * inner : -1], refs[-1]
    columns = jnp.concatenate([ref[:, acts_at : acts_at + rows] for ref in acts_refs], axis=0)
    cots = jnp.concatenate([ref[:, rows:] for ref in cots_refs], axis=0)
    total = lax.dot_general(columns, cots, CONTRACT_ROWS, preferred_element_type=jnp.float32)
    for ref in arrived:
        total += ref[...].astype(jnp.float32)
    out[...] = total.astype(out.dtype)


def gradient_at(at, refs):
    total, beside, far = refs
    return total[at, :] + beside[at, :].astype(jnp.float32) + far[at, :].astype(jnp.float32)


def steps(half, which, body):
    @pl.loop(0, half // CHUNK)
    def _(step):
        start = pl.multiple_of(step * CHUNK, CHUNK)
        body(pl.ds(start, CHUNK), pl.ds(pl.multiple_of(which * half + start, CHUNK), CHUNK))


def drift_kernel(*refs):
    gradient_refs, (weights, first, second, anchor), drift_ref = refs[:3], refs[3:7], refs[7]

    def body(here, at):
        gradient = gradient_at(at, gradient_refs)
        state = (weights[at, :], first[at, :], second[at, :], anchor[at, :])
        drift_ref[here, :] = inner_update(gradient, *state)[1]

    steps(drift_ref.shape[0], 1 - lax.axis_index("rep"), body)


def update_kernel(*refs):
    gradient_refs, (weights, first, second, anchor), (first_ref, drift_ref) = refs[:3], refs[3:7], refs[7:]
    half = drift_ref.shape[0]
    r = lax.axis_index("rep")

    def body(here, at):
        gradient = gradient_at(at, gradient_refs)
        state = (weights[at, :], first[at, :], second[at, :], anchor[at, :])
        first_ref[at, :], drift_ref[here, :] = inner_update(gradient, *state)

    def others(here, at):
        first_ref[at, :] = decay_first * first[at, :] + (1.0 - decay_first) * gradient_at(at, gradient_refs)

    steps(half, r, body)
    steps(half, 1 - r, others)


def outer_kernel(drift, other, anchor, momentum, out):
    half = out.shape[0]
    at = pl.ds(pl.multiple_of(lax.axis_index("rep") * half, half), half)
    out[...] = outer_update((drift[...] + other[...]) / 2, anchor[at, :], momentum[at, :])


def product(messages, rows, pieces):
    r = lax.axis_index("rep")
    half = rows // 2
    total = 0.0
    for (blocks, start), (mine, other) in zip(messages, pieces):
        for which, piece in ((r, mine), (1 - r, other)):
            at = pl.ds(pl.multiple_of(start + which * half, half), half)
            columns = jnp.concatenate([block[:, at] for block in blocks], axis=0)
            total += jnp.dot(columns, piece[...], preferred_element_type=jnp.float32)
    return total


def paired(refs):
    return [(refs[2 * n], refs[2 * n + 1]) for n in range(len(refs) // 2)]


def early_values_kernel(inner, rows, *refs):
    own, both = refs[:inner], refs[inner : 2 * inner]
    refs[-1][...] = product([(own, 0), (both, rows), (both, 0)], rows, paired(refs[2 * inner : -1]))


def late_values_kernel(inner, rows, early, *refs):
    tokens = early.shape[0] // inner
    total = early[...] + product([(refs[:inner], 0)], rows, [refs[inner : inner + 2]])
    for k, out in enumerate(refs[inner + 2 :]):
        out[...] = total[k * tokens : (k + 1) * tokens].astype(out.dtype)


def sum_kernel(*refs):
    total = refs[0][...]
    for ref in refs[1:-1]:
        total += ref[...].astype(jnp.float32)
    refs[-1][...] = total.astype(refs[-1].dtype)


def on_device(acts, value_cots, inner_weights, first_moment, second_moment, anchor, outer_momentum):
    inner = lax.axis_size("fsdp") // PLANES
    rows, width = anchor.shape
    if inner != 4 or lax.axis_size("rep") != 2 or rows % 256 or width % 128:
        return general(acts, value_cots, inner_weights, first_moment, second_moment, anchor, outer_momentum)
    tokens = acts.shape[1]
    half = rows // 2

    def planes(x, bits):
        return lax.ppermute(x, "fsdp", [(p * inner + i, (p ^ bits) * inner + i) for p in range(PLANES) for i in range(inner)])

    def across(x, k):
        return lax.ppermute(x, "fsdp", [(p * inner + i, p * inner + (i ^ k)) for p in range(PLANES) for i in range(inner)])

    order = list(reversed(range(1, inner)))

    def around(blocks):
        return [blocks[0]] + [across(blocks[k], k) for k in order]

    def swap(x):
        return lax.ppermute(x, "rep", [(0, 1), (1, 0)])

    out = [jax.ShapeDtypeStruct((tokens, rows + width), jnp.bfloat16)] * inner
    first = around(call(partial(pack_first_kernel, inner, rows), "pack", out, [acts[0], value_cots[0]], 0))

    def pack(blocks, after):
        out = [jax.ShapeDtypeStruct((tokens, len(blocks) * rows), jnp.bfloat16)] * inner
        return call(partial(pack_kernel, inner, rows, blocks), "pack", out, [acts[0]], 0, after=after)

    second = around(pack((2, 1), first[1:2]))
    full = jax.ShapeDtypeStruct((rows, width), jnp.float32)
    sent = jax.ShapeDtypeStruct((rows, width), jnp.bfloat16)

    def gradient(message, at, out, arrived=()):
        kernel = partial(gradient_kernel, inner, rows, at)
        flops = 2 * inner * tokens * rows * width
        return call(kernel, "gradient", [out], message + first + list(arrived), flops)[0]

    beside_far = planes(gradient(first, 0, sent), 1)
    beside = planes(gradient(second, rows, sent), 1)
    for_far = gradient(second, 0, sent, [beside_far])
    far = planes(for_far, 2)
    last = around(pack((0,), [for_far]))
    known = [gradient(last, 0, full), beside, far, inner_weights[0], first_moment[0], second_moment[0], anchor]
    half_block = jax.ShapeDtypeStruct((half, width), jnp.float32)
    (drift_out,) = call(drift_kernel, "drift", [half_block], known, 0)
    drift_in = swap(drift_out)
    first_next, drift = call(update_kernel, "update", [full, half_block], known, 0)
    new_half = jax.ShapeDtypeStruct((half, width), jnp.bfloat16)
    (mine,) = call(outer_kernel, "outer", [new_half], [drift, drift_in, anchor, outer_momentum], 0)
    mine2 = planes(mine, 2)
    mine1 = planes(mine, 1)
    mine3 = planes(mine2, 1)
    pieces = [y for x in (mine, mine1, mine2) for y in (x, swap(x))]
    flops = 2 * inner * tokens * rows * width
    (early,) = call(
        partial(early_values_kernel, inner, rows),
        "early_values",
        [jax.ShapeDtypeStruct((inner * tokens, width), jnp.float32)],
        last + second + pieces,
        3 * flops,
    )
    block = jax.ShapeDtypeStruct((tokens, width), jnp.bfloat16)
    own, *sums = call(
        partial(late_values_kernel, inner, rows),
        "late_values",
        [jax.ShapeDtypeStruct((tokens, width), jnp.float32)] + [block] * (inner - 1),
        [early] + first + [mine3, swap(mine3)],
        flops,
    )
    terms = [own] + [across(x, k) for x, k in zip(sums, order)]
    (values,) = call(sum_kernel, "sum", [block], terms, 0)
    return (first_next[None], values[None])


def solution(mesh):
    placed = (
        P("rep", "fsdp", None),
        P("rep", "fsdp", None),
        P("rep", "fsdp", None),
        P("rep", "fsdp", None),
        P("rep", "fsdp", None),
        P("fsdp", None),
        P("fsdp", None),
    )
    return jax.shard_map(
        on_device,
        mesh=mesh,
        in_specs=placed,
        out_specs=(P("rep", "fsdp", None), P("rep", "fsdp", None)),
        check_vma=False,
    )
```

```python
from functools import partial

import jax
import jax.numpy as jnp
from jax import lax
from jax.experimental import pallas as pl
from jax.experimental.pallas import tpu as pltpu
from jax.sharding import PartitionSpec as P

decay_first = 0.9
decay_second = 0.95
inner_rate = 0.006
epsilon = 1e-08
outer_rate = 0.7
outer_decay = 0.9

PLANES = 4
CHUNK = 32
CONTRACT_ROWS = (((0,), (0,)), ((), ()))
VMEM_BYTES = 16 * 1024 * 1024


def outer_update(average, anchor_rows, momentum_rows):
    velocity = outer_decay * momentum_rows + average
    return (anchor_rows - outer_rate * (average + outer_decay * velocity)).astype(jnp.bfloat16)


def inner_update(gradient, inner_weights, first_moment, second_moment, anchor):
    first_next = decay_first * first_moment + (1.0 - decay_first) * gradient
    second_next = decay_second * second_moment + (1.0 - decay_second) * gradient * gradient
    stepped = inner_weights - inner_rate * first_next / (jnp.sqrt(second_next) + epsilon)
    return first_next, anchor - stepped


def general(acts, value_cots, inner_weights, first_moment, second_moment, anchor, outer_momentum):
    tokens_local = acts[0]
    columns = lax.all_to_all(tokens_local, "fsdp", split_axis=1, concat_axis=0, tiled=True)
    cots = lax.all_gather(value_cots[0], "fsdp", axis=0, tiled=True)
    gradient = lax.dot_general(columns, cots, CONTRACT_ROWS, preferred_element_type=jnp.float32)
    first_next, drift = inner_update(gradient, inner_weights[0], first_moment[0], second_moment[0], anchor)
    average = lax.psum(drift, "rep") / lax.axis_size("rep")
    weights_next = outer_update(average, anchor, outer_momentum)
    gathered = lax.all_gather(weights_next, "fsdp", axis=0, tiled=True)
    values = jnp.dot(tokens_local, gathered, preferred_element_type=jnp.float32)
    return (first_next[None], values.astype(jnp.bfloat16)[None])


def flip(at, bits):
    low = lax.rem(at, 2)
    return (at // 2 + bits // 2 - 2 * (at // 2) * (bits // 2)) * 2 + low + bits % 2 - 2 * low * (bits % 2)


def call(kernel, name, out, inputs, flops, scratch=(), after=()):
    moved = sum(x.size * x.dtype.itemsize for x in list(inputs) + list(out))
    count = len(inputs)

    def without_after(*refs):
        kernel(*refs[:count], *refs[count + len(after) :])

    return pl.pallas_call(
        without_after,
        out_shape=out,
        in_specs=[pl.BlockSpec(memory_space=pltpu.VMEM)] * count + [pl.BlockSpec(memory_space=pl.ANY)] * len(after),
        out_specs=[pl.BlockSpec(memory_space=pltpu.VMEM)] * len(out),
        scratch_shapes=list(scratch),
        compiler_params=pltpu.CompilerParams(vmem_limit_bytes=VMEM_BYTES),
        cost_estimate=pl.CostEstimate(flops=flops, bytes_accessed=moved, transcendentals=0),
        name=name,
    )(*inputs, *after)


def block_start(inner, rows, bits, k):
    f = lax.axis_index("fsdp")
    return pl.multiple_of((flip(f // inner, bits) * inner + flip(lax.rem(f, inner), k)) * rows, rows)


def pack_first_kernel(inner, rows, acts_ref, cots_ref, *outs):
    for k in range(inner):
        outs[k][:, :rows] = acts_ref[:, pl.ds(block_start(inner, rows, 3, k), rows)]
        outs[k][:, rows:] = cots_ref[...]


def pack_kernel(inner, rows, blocks, acts_ref, *outs):
    for k in range(inner):
        for slot, bits in enumerate(blocks):
            outs[k][:, slot * rows : (slot + 1) * rows] = acts_ref[:, pl.ds(block_start(inner, rows, bits, k), rows)]


def gradient_kernel(inner, rows, acts_at, *refs):
    acts_refs, cots_refs, arrived, out = refs[:inner], refs[inner : 2 * inner], refs[2 * inner : -1], refs[-1]
    columns = jnp.concatenate([ref[:, acts_at : acts_at + rows] for ref in acts_refs], axis=0)
    cots = jnp.concatenate([ref[:, rows:] for ref in cots_refs], axis=0)
    total = lax.dot_general(columns, cots, CONTRACT_ROWS, preferred_element_type=jnp.float32)
    for ref in arrived:
        total += ref[...].astype(jnp.float32)
    out[...] = total.astype(out.dtype)


def gradient_at(at, refs):
    total, beside, far = refs
    return total[at, :] + beside[at, :].astype(jnp.float32) + far[at, :].astype(jnp.float32)


def steps(half, which, body):
    @pl.loop(0, half // CHUNK)
    def _(step):
        start = pl.multiple_of(step * CHUNK, CHUNK)
        body(pl.ds(start, CHUNK), pl.ds(pl.multiple_of(which * half + start, CHUNK), CHUNK))


def drift_kernel(*refs):
    gradient_refs, (weights, first, second, anchor), drift_ref = refs[:3], refs[3:7], refs[7]

    def body(here, at):
        gradient = gradient_at(at, gradient_refs)
        state = (weights[at, :], first[at, :], second[at, :], anchor[at, :])
        drift_ref[here, :] = inner_update(gradient, *state)[1]

    steps(drift_ref.shape[0], 1 - lax.axis_index("rep"), body)


def update_kernel(*refs):
    gradient_refs, (weights, first, second, anchor), (first_ref, drift_ref) = refs[:3], refs[3:7], refs[7:]
    half = drift_ref.shape[0]
    r = lax.axis_index("rep")

    def body(here, at):
        gradient = gradient_at(at, gradient_refs)
        state = (weights[at, :], first[at, :], second[at, :], anchor[at, :])
        first_ref[at, :], drift_ref[here, :] = inner_update(gradient, *state)

    def others(here, at):
        first_ref[at, :] = decay_first * first[at, :] + (1.0 - decay_first) * gradient_at(at, gradient_refs)

    steps(half, r, body)
    steps(half, 1 - r, others)


def outer_kernel(drift, other, anchor, momentum, out):
    half = out.shape[0]
    at = pl.ds(pl.multiple_of(lax.axis_index("rep") * half, half), half)
    out[...] = outer_update((drift[...] + other[...]) / 2, anchor[at, :], momentum[at, :])


def product(messages, rows, pieces):
    r = lax.axis_index("rep")
    half = rows // 2
    total = 0.0
    for (blocks, start), (mine, other) in zip(messages, pieces):
        for which, piece in ((r, mine), (1 - r, other)):
            at = pl.ds(pl.multiple_of(start + which * half, half), half)
            columns = jnp.concatenate([block[:, at] for block in blocks], axis=0)
            total += jnp.dot(columns, piece[...], preferred_element_type=jnp.float32)
    return total


def paired(refs):
    return [(refs[2 * n], refs[2 * n + 1]) for n in range(len(refs) // 2)]


def early_values_kernel(inner, rows, *refs):
    own, both = refs[:inner], refs[inner : 2 * inner]
    refs[-1][...] = product([(own, 0), (both, rows), (both, 0)], rows, paired(refs[2 * inner : -1]))


def late_values_kernel(inner, rows, early, *refs):
    tokens = early.shape[0] // inner
    total = early[...] + product([(refs[:inner], 0)], rows, [refs[inner : inner + 2]])
    for k, out in enumerate(refs[inner + 2 :]):
        out[...] = total[k * tokens : (k + 1) * tokens].astype(out.dtype)


def sum_kernel(*refs):
    total = refs[0][...]
    for ref in refs[1:-1]:
        total += ref[...].astype(jnp.float32)
    refs[-1][...] = total.astype(refs[-1].dtype)


def on_device(acts, value_cots, inner_weights, first_moment, second_moment, anchor, outer_momentum):
    inner = lax.axis_size("fsdp") // PLANES
    rows, width = anchor.shape
    if inner != 4 or lax.axis_size("rep") != 2 or rows % 256 or width % 128:
        return general(acts, value_cots, inner_weights, first_moment, second_moment, anchor, outer_momentum)
    tokens = acts.shape[1]
    half = rows // 2

    def planes(x, bits):
        return lax.ppermute(x, "fsdp", [(p * inner + i, (p ^ bits) * inner + i) for p in range(PLANES) for i in range(inner)])

    def across(x, k):
        return lax.ppermute(x, "fsdp", [(p * inner + i, p * inner + (i ^ k)) for p in range(PLANES) for i in range(inner)])

    def around(blocks):
        return [blocks[0]] + [across(blocks[k], k) for k in range(1, inner)]

    def swap(x):
        return lax.ppermute(x, "rep", [(0, 1), (1, 0)])

    out = [jax.ShapeDtypeStruct((tokens, rows + width), jnp.bfloat16)] * inner
    first = around(call(partial(pack_first_kernel, inner, rows), "pack", out, [acts[0], value_cots[0]], 0))

    def pack(blocks, after):
        out = [jax.ShapeDtypeStruct((tokens, len(blocks) * rows), jnp.bfloat16)] * inner
        return call(partial(pack_kernel, inner, rows, blocks), "pack", out, [acts[0]], 0, after=after)

    second = around(pack((2, 1), first[1:2]))
    full = jax.ShapeDtypeStruct((rows, width), jnp.float32)
    sent = jax.ShapeDtypeStruct((rows, width), jnp.bfloat16)

    def gradient(message, at, out, arrived=()):
        kernel = partial(gradient_kernel, inner, rows, at)
        flops = 2 * inner * tokens * rows * width
        return call(kernel, "gradient", [out], message + first + list(arrived), flops)[0]

    beside_far = planes(gradient(first, 0, sent), 1)
    beside = planes(gradient(second, rows, sent), 1)
    for_far = gradient(second, 0, sent, [beside_far])
    far = planes(for_far, 2)
    last = around(pack((0,), [for_far]))
    known = [gradient(last, 0, full), beside, far, inner_weights[0], first_moment[0], second_moment[0], anchor]
    half_block = jax.ShapeDtypeStruct((half, width), jnp.float32)
    (drift_out,) = call(drift_kernel, "drift", [half_block], known, 0)
    drift_in = swap(drift_out)
    first_next, drift = call(update_kernel, "update", [full, half_block], known, 0)
    new_half = jax.ShapeDtypeStruct((half, width), jnp.bfloat16)
    (mine,) = call(outer_kernel, "outer", [new_half], [drift, drift_in, anchor, outer_momentum], 0)
    mine2 = planes(mine, 2)
    mine1 = planes(mine, 1)
    mine3 = planes(mine2, 1)
    pieces = [y for x in (mine, mine1, mine2) for y in (x, swap(x))]
    flops = 2 * inner * tokens * rows * width
    (early,) = call(
        partial(early_values_kernel, inner, rows),
        "early_values",
        [jax.ShapeDtypeStruct((inner * tokens, width), jnp.float32)],
        last + second + pieces,
        3 * flops,
    )
    block = jax.ShapeDtypeStruct((tokens, width), jnp.bfloat16)
    own, *sums = call(
        partial(late_values_kernel, inner, rows),
        "late_values",
        [jax.ShapeDtypeStruct((tokens, width), jnp.float32)] + [block] * (inner - 1),
        [early] + first + [mine3, swap(mine3)],
        flops,
    )
    terms = [own] + [across(sums[k - 1], k) for k in reversed(range(1, inner))]
    (values,) = call(sum_kernel, "sum", [block], terms, 0)
    return (first_next[None], values[None])


def solution(mesh):
    placed = (
        P("rep", "fsdp", None),
        P("rep", "fsdp", None),
        P("rep", "fsdp", None),
        P("rep", "fsdp", None),
        P("rep", "fsdp", None),
        P("fsdp", None),
        P("fsdp", None),
    )
    return jax.shard_map(
        on_device,
        mesh=mesh,
        in_specs=placed,
        out_specs=(P("rep", "fsdp", None), P("rep", "fsdp", None)),
        check_vma=False,
    )
```
